256 devices in a mesh: lat: 32 (over z_lo, y, x), lev: 8 (over z_hi, core).
Axes of the slice: x: 4, y: 4, z: 8 (z_hi: 4, z_lo: 2; z = z_hi * 2 + z_lo), core: 2. Of those that a mesh axis runs over, the one named last changes fastest.
Arguments:
- zonal_wind_speed: float32 [768, 64, 1152], P('lat', 'lev'), may hold values from -1 to 1
- meridional_wind_speed: float32 [768, 64, 1152], P('lat', 'lev'), may hold values from -1 to 1
- thermal_state: float32 [768, 64, 1152], P('lat', 'lev'), may hold values from 0.5 to 2
- pressure_depth: float32 [768, 64, 1152], P('lat', 'lev'), may hold values from 1 to 2
- primary_scalar_mixing: float32 [768, 64, 1152], P('lat', 'lev'), may hold values from -6 to 6
- secondary_scalar_mixing: float32 [768, 64, 1152], P('lat', 'lev'), may hold values from 0.1 to 10
- terrain_potential_height: float32 [768, 1152], P('lat'), may hold values from -6 to 6
Outputs:
- east_out: float32 [768, 64, 1152], P('lat', 'lev')
- north_out: float32 [768, 64, 1152], P('lat', 'lev')
- temperature_out: float32 [768, 64, 1152], P('lat', 'lev')
- thickness_out: float32 [768, 64, 1152], P('lat', 'lev')
- tracer_one_out: float32 [768, 64, 1152], P('lat', 'lev')
- tracer_two_out: float32 [768, 64, 1152], P('lat', 'lev')
- geopotential: float32 [768, 64, 1152], P('lat', 'lev')
The draws below stay inside these ranges and needn't reach their ends.
All inputs are finite; a program needn't handle non-finite values.
Results may differ from the reference program's by a relative error of at most 0.00007.
Values sent between devices are 32-bit elements; how exact they have to be, the bound alone decides.
A program may use at most 128 MiB of HBM per device.

```python
import math
import jax
import jax.numpy as jnp

MERIDIAN_TOTAL = 1152
PARALLEL_TOTAL = 768
SHEET_TOTAL = 64


def steps_of(rng, shape, split, low, top_value):
    loudness = 1.0
    for dim, shards_of in split:
        draws = jax.random.uniform(jax.random.fold_in(jax.random.fold_in(rng, 6), dim), (shards_of,), jnp.float32, low / len(split), top_value / len(split))
        loudness = loudness * jnp.repeat(jnp.exp(draws), shape[dim] // shards_of).reshape((-1,) + (1,) * (len(shape) - 1 - dim))
    return loudness


def scatter_about(own_key, shape, spread, limit, split=(), kind=jnp.bfloat16):
    values = jax.random.normal(own_key, shape, jnp.float32) * spread
    if len(split) > 0:
        values = steps_of(own_key, shape, split, -0.22, 0.18) * values
    return jnp.clip(values, min=-limit, max=limit).astype(kind)


def setup_inputs(seed: int = 0) -> dict:
    seeds = jax.random.split(jax.random.key(seed), 8)
    zonal_wind_speed = jnp.clip(jax.random.uniform(seeds[0], (PARALLEL_TOTAL, SHEET_TOTAL, MERIDIAN_TOTAL), jnp.float32, -1.0, 1.0) * steps_of(seeds[0], (PARALLEL_TOTAL, SHEET_TOTAL, MERIDIAN_TOTAL), ((0, 32), (1, 8)), -0.4, 0.0), -1.0, 1.0)
    meridional_wind_speed = jnp.clip(jax.random.uniform(seeds[1], (PARALLEL_TOTAL, SHEET_TOTAL, MERIDIAN_TOTAL), jnp.float32, -1.0, 1.0) * steps_of(seeds[1], (PARALLEL_TOTAL, SHEET_TOTAL, MERIDIAN_TOTAL), ((0, 32), (1, 8)), -0.4, 0.0), -1.0, 1.0)
    thermal_state = jnp.clip(jnp.exp(math.log(2.0) - 1.3862944 * jax.random.uniform(seeds[2], (PARALLEL_TOTAL, SHEET_TOTAL, MERIDIAN_TOTAL), jnp.float32) ** steps_of(seeds[2], (PARALLEL_TOTAL, SHEET_TOTAL, MERIDIAN_TOTAL), ((0, 32), (1, 8)), -0.2, 0.2)), 0.5, 2.0)
    pressure_depth = jnp.clip(1.0 + 1.0 * jax.random.uniform(seeds[3], (PARALLEL_TOTAL, SHEET_TOTAL, MERIDIAN_TOTAL), jnp.float32) ** steps_of(seeds[3], (PARALLEL_TOTAL, SHEET_TOTAL, MERIDIAN_TOTAL), ((0, 32), (1, 8)), -0.2, 0.2), 1.0, 2.0)
    primary_scalar_mixing = scatter_about(seeds[4], (PARALLEL_TOTAL, SHEET_TOTAL, MERIDIAN_TOTAL), 1.0, 6.0, ((0, 32), (1, 8)), jnp.float32)
    secondary_scalar_mixing = jnp.clip(jnp.exp(math.log(10.0) - 4.6051702 * jax.random.uniform(seeds[5], (PARALLEL_TOTAL, SHEET_TOTAL, MERIDIAN_TOTAL), jnp.float32) ** steps_of(seeds[5], (PARALLEL_TOTAL, SHEET_TOTAL, MERIDIAN_TOTAL), ((0, 32), (1, 8)), -0.2, 0.2)), 0.1, 10.0)
    terrain_potential_height = scatter_about(seeds[6], (PARALLEL_TOTAL, MERIDIAN_TOTAL), 1.0, 6.0, ((0, 32),), jnp.float32)
    return dict(zonal_wind_speed=zonal_wind_speed, meridional_wind_speed=meridional_wind_speed, thermal_state=thermal_state, pressure_depth=pressure_depth, primary_scalar_mixing=primary_scalar_mixing, secondary_scalar_mixing=secondary_scalar_mixing, terrain_potential_height=terrain_potential_height)


courant = 0.1
gradient_scale = 0.1
dry_air_rconst = 0.3
top_pressure = 1.0
cut_square = 0.5


def extend(values):
    return jnp.concatenate([values[:1], values, values[-1:]], axis=0)


def zonal_diff(values):
    return jnp.roll(values, -1, 2) - jnp.roll(values, 1, 2)


def merid_diff(values):
    padded = extend(values)
    return padded[2:] - padded[:-2]


def advect_update(values, wind_u, wind_v):
    return values - courant * (wind_u * zonal_diff(values) + wind_v * merid_diff(values))


def damping_table():
    latitudes = (jnp.arange(PARALLEL_TOTAL, dtype=jnp.float32) + 0.5) * (math.pi / PARALLEL_TOTAL) - 0.5 * math.pi
    waves = jnp.sin(jnp.arange(MERIDIAN_TOTAL, dtype=jnp.float32) * (math.pi / MERIDIAN_TOTAL))
    cosine_sq = jnp.cos(latitudes)[:, None] ** 2
    return cosine_sq / jnp.maximum(cosine_sq, cut_square * waves[None, :] ** 2)


def polar_filter(values, damping):
    spectrum = jnp.fft.fft(values, axis=-1)
    return jnp.real(jnp.fft.ifft(spectrum * damping[:, None, :], axis=-1)).astype(values.dtype)


def integrate_pressure_heights(pressure_depth, thermal_state, bottom_sheet_index):
    running = jnp.cumsum(pressure_depth, axis=1)
    interface = top_pressure + jnp.concatenate([jnp.zeros_like(pressure_depth[:, :1]), running], axis=1)
    edge_pressure_natural_log = jnp.log(interface)
    sheet_thickness_range = dry_air_rconst * thermal_state * (edge_pressure_natural_log[:, 1:] - edge_pressure_natural_log[:, :-1])
    underneath = jnp.flip(jnp.cumsum(jnp.flip(sheet_thickness_range, 1), 1), 1) - sheet_thickness_range
    geopotential = bottom_sheet_index[:, None, :] + underneath + 0.5 * sheet_thickness_range
    log_mid = 0.5 * (edge_pressure_natural_log[:, 1:] + edge_pressure_natural_log[:, :-1])
    return geopotential, log_mid


def reference(zonal_wind_speed, meridional_wind_speed, thermal_state, pressure_depth, primary_scalar_mixing, secondary_scalar_mixing, terrain_potential_height):
    carried_quantities = [advect_update(lone_vertical_profile, zonal_wind_speed, meridional_wind_speed) for lone_vertical_profile in (zonal_wind_speed, meridional_wind_speed, thermal_state, pressure_depth, primary_scalar_mixing, secondary_scalar_mixing)]
    damping = damping_table()
    east_filt = polar_filter(carried_quantities[0], damping)
    north_filt = polar_filter(carried_quantities[1], damping)
    geopotential, log_mid = integrate_pressure_heights(carried_quantities[3], carried_quantities[2], terrain_potential_height)
    gas_pull = dry_air_rconst * carried_quantities[2]
    east_out = east_filt - gradient_scale * (zonal_diff(geopotential) + gas_pull * zonal_diff(log_mid))
    north_out = north_filt - gradient_scale * (merid_diff(geopotential) + gas_pull * merid_diff(log_mid))
    return east_out, north_out, carried_quantities[2], carried_quantities[3], carried_quantities[4], carried_quantities[5], geopotential
```

```python
import functools
import math

import jax
import jax.numpy as jnp
import numpy as np
from jax import lax
from jax.experimental import pallas as pl
from jax.experimental.pallas import tpu as pltpu
from jax.sharding import PartitionSpec as P

MESH = pl.DeviceIdType.MESH
F32 = jnp.float32
BF16 = jnp.bfloat16

ROWS, LEVS, LON = 24, 8, 1152
NLAT = 32
CHIPS = 4
LANE = 128
COURANT = 0.1
GRAD = 0.1
GAS = 0.3
TOP = 1.0
CUT = 0.5

INTERIOR = ((1, 6), (13, 5))
EDGE = len(INTERIOR)
NCHUNK = EDGE + 1


@functools.cache
def tables():
    b = np.arange(LANE)
    fwd, back = [], []
    for r in range(1, 5):
        angle = 2.0 * np.pi * ((b[:, None] * (9 * b[None, :] + r)) % LON) / LON
        mr, mi = np.cos(angle), -np.sin(angle)
        w = np.block([[mr, mi], [-mi, mr]])
        fwd.append(w)
        back.append(w.T * (2.0 / LON))
    angle = 2.0 * np.pi * ((b[:, None] * b[None, :]) % LANE) / LANE
    w0 = np.concatenate([np.cos(angle[:, :65]), np.sin(angle[:, 1:64])], axis=1)
    weight = np.full((LANE,), 2.0)
    weight[0] = weight[64] = 1.0
    b0 = (w0 * weight[None, :]).T / LON
    wf = np.stack(fwd).astype(np.float32)
    wb = np.stack(back).astype(np.float32)
    wz = np.stack([w0, b0]).astype(np.float32)
    sines = np.zeros((8, LANE))
    freq0 = np.concatenate([np.arange(65), np.arange(1, 64)]) * 9
    sines[0] = np.sin(np.pi * freq0 / LON) ** 2 * CUT
    for r in range(1, 5):
        sines[r] = np.sin(np.pi * (9 * b + r) / LON) ** 2 * CUT
    lat = (np.arange(NLAT * ROWS, dtype=np.float32) + np.float32(0.5)) * np.float32(
        math.pi / (NLAT * ROWS)
    ) - np.float32(0.5 * math.pi)
    csq = np.cos(lat.astype(np.float64)).astype(np.float32) ** 2
    csq = np.broadcast_to(csq.reshape(NLAT, ROWS, 1), (NLAT, ROWS, LANE)).astype(np.float32)
    return wf, wb, wz, sines.astype(np.float32), np.ascontiguousarray(csq)


def east_west(x):
    return pltpu.roll(x, LON - 1, 1) - pltpu.roll(x, 1, 1)


def first_kernel(
    u_hbm, v_hbm, t_hbm, p_hbm, a_hbm, b_hbm, terr_hbm, csq_hbm, sin_hbm, wf_hbm, wb_hbm, wz_hbm,
    height, east, north, t_out, p_out, a_out, b_out, geo_off,
    fields, terr, csq, sines, wf32, wb32, wz32, wf, wb, wz,
    cum, logmid, halo_t, halo_p, damp,
    s_own, s_pair, s_chip, s_recv, pre, pre_pair,
    d_own, d_pair, d_chip, d_recv, geo_pair,
    y4, y1, z4, z1,
    load_sem, halo_s, halo_r, out_s, out_r,
    bp_s, bp_r, bz_s, bz_r, bq_s, bq_r, be_s, be_r,
    cp_s, cp_r, cz_s, cz_r, cq_s, cq_r, ce_s, ce_r,
):
    la, le = lax.axis_index("lat"), lax.axis_index("lev")
    chip, core = le // 2, le % 2
    other = 1 - core
    up, down = (la + 1) % NLAT, (la + NLAT - 1) % NLAT
    pair_dev = (la, chip * 2 + other)
    side_lat = (la + NLAT - 1 + 2 * core) % NLAT
    cross_dev = (side_lat, chip * 2 + other)
    side_dev = (side_lat, le)
    core_f = core.astype(F32)
    other_f = other.astype(F32)

    def remote(src, dst, send, recv, dev):
        return pltpu.make_async_remote_copy(
            src_ref=src, dst_ref=dst, send_sem=send, recv_sem=recv, device_id=dev, device_id_type=MESH
        )

    ins = (u_hbm, v_hbm, t_hbm, p_hbm, a_hbm, b_hbm)
    load = [
        pltpu.make_async_copy(ins[f], fields.at[f, pl.ds(1, ROWS)], load_sem.at[f]) for f in range(6)
    ]
    load += [
        pltpu.make_async_copy(terr_hbm, terr, load_sem.at[6]),
        pltpu.make_async_copy(csq_hbm.at[la], csq, load_sem.at[7]),
        pltpu.make_async_copy(sin_hbm, sines, load_sem.at[8]),
        pltpu.make_async_copy(wf_hbm, wf32, load_sem.at[9]),
        pltpu.make_async_copy(wb_hbm, wb32, load_sem.at[10]),
        pltpu.make_async_copy(wz_hbm, wz32, load_sem.at[11]),
    ]

    barrier = pltpu.get_barrier_semaphore()
    partners = [(up, le), (down, le), pair_dev, cross_dev]
    partners += [(la, ((chip + d) % CHIPS) * 2 + core) for d in range(1, CHIPS)]
    for dev in partners:
        pl.semaphore_signal(barrier, inc=1, device_id=dev, device_id_type=MESH)
    for f in (2, 3, 0, 1):
        load[f].start()
    pl.semaphore_wait(barrier, len(partners))

    halo = {}
    for f in (2, 3, 0, 1, 4, 5):
        halo[f, 0] = remote(
            ins[f].at[ROWS - 1], fields.at[f, 0], halo_s.at[f, 0], halo_r.at[f, 0], (up, le)
        )
        halo[f, 1] = remote(
            ins[f].at[0], fields.at[f, ROWS + 1], halo_s.at[f, 1], halo_r.at[f, 1], (down, le)
        )
        halo[f, 0].start()
        halo[f, 1].start()
    for f in (4, 5, 6, 7, 8, 9, 10, 11):
        load[f].start()

    row = lax.broadcasted_iota(jnp.int32, (LEVS, LON), 0)

    def halves(x):
        hi = x.astype(BF16)
        return hi, (x - hi.astype(F32)).astype(BF16)

    def run_down(x):
        for s in (1, 2, 4):
            x = x + jnp.where(row >= s, pltpu.roll(x, s, 0), 0.0)
        return x

    def run_up(x):
        for s in (1, 2, 4):
            x = x + jnp.where(row < LEVS - s, pltpu.roll(x, LEVS - s, 0), 0.0)
        return x

    def advected(f, j):
        x = fields[f, j + 1]
        merid = fields[f, j + 2] - fields[f, j]
        return x - COURANT * (fields[0, j + 1] * east_west(x) + fields[1, j + 1] * merid)

    def halo_ready(f):
        halo[f, 0].wait_recv()
        halo[f, 1].wait_recv()

        @pl.when(la == 0)
        def _():
            fields[f, 0] = fields[f, 1]

        @pl.when(la == NLAT - 1)
        def _():
            fields[f, ROWS + 1] = fields[f, ROWS]

    def column_row(j):
        t_out[j] = advected(2, j)
        p = advected(3, j)
        p_out[j] = p
        c = run_down(p)
        cum[j + 1] = c
        s_own[j] = c[LEVS - 1 :, :]

    def span(k):
        if k == EDGE:
            return (ROWS - 1) * core, (ROWS - 1) * other, 1
        start, n = INTERIOR[k]
        return start + n * core, start + n * other, n

    def chunk_rows(k, body):
        if k == EDGE:
            body(0)
            body(ROWS - 1)
        else:
            start, n = INTERIOR[k]

            @pl.loop(start, start + 2 * n)
            def _(j):
                body(j)

    def scan(k, own, pair, total, recv, result, result_pair, sign, base, ps, pr, zs, zr, qs, qr, es, er):
        mine, theirs, n = span(k)
        mine_s, theirs_s = pl.ds(mine, n), pl.ds(theirs, n)
        to_pair = remote(own.at[theirs_s], pair.at[theirs_s], ps.at[k], pr.at[k], pair_dev)
        from_pair = remote(own.at[mine_s], pair.at[mine_s], ps.at[k], pr.at[k], pair_dev)
        share = remote(
            result_pair.at[mine_s], result.at[pl.ds(mine + 1, n)], qs.at[k], qr.at[k], pair_dev
        )
        shared = remote(
            result_pair.at[theirs_s], result.at[pl.ds(theirs + 1, n)], qs.at[k], qr.at[k], pair_dev
        )
        hops = {}
        for d in (2, 1, 3):
            hops[d] = remote(
                total.at[mine_s], recv.at[d - 1, mine_s], zs.at[k, d - 1], zr.at[k, d - 1],
                (la, ((chip + CHIPS + sign * d) % CHIPS) * 2 + core),
            )
        if sign > 0:
            sends = {d: chip + d < CHIPS for d in hops}
            gets = {d: chip >= d for d in hops}
        else:
            sends = {d: chip >= d for d in hops}
            gets = {d: chip + d < CHIPS for d in hops}
        edges = []
        if k == EDGE:
            slot = (ROWS + 1) * other
            edges = [
                remote(result.at[mine + 1], result.at[slot], es.at[0], er.at[other], side_dev),
                remote(result_pair.at[mine], result.at[slot], es.at[1], er.at[other], cross_dev),
            ]

        def begin():
            to_pair.start()

        def middle():
            from_pair.wait_recv()
            total[mine_s] = own[mine_s] + pair[mine_s]
            for d in hops:
                pl.when(sends[d])(hops[d].start)

        def end():
            acc = base(mine, n)
            result[pl.ds(mine + 1, n)] = acc
            for d in hops:

                @pl.when(gets[d])
                def _():
                    hops[d].wait_recv()
                    result[pl.ds(mine + 1, n)] = result[pl.ds(mine + 1, n)] + recv[d - 1, mine_s]

            acc = result[pl.ds(mine + 1, n)]
            mine_f, pair_f = (core_f, other_f) if sign > 0 else (other_f, core_f)
            result_pair[mine_s] = acc + pair_f * own[mine_s]
            share.start()
            result[pl.ds(mine + 1, n)] = acc + mine_f * pair[mine_s]
            for e in edges:
                e.start()

        def finish():
            shared.wait_recv()

        def edge_ready():
            for side in range(2):
                remote(
                    result.at[(ROWS + 1) * side], result.at[(ROWS + 1) * side],
                    es.at[0], er.at[side], side_dev,
                ).wait_recv()

        def drain():
            to_pair.wait_send()
            share.wait_send()
            for d in hops:
                pl.when(sends[d])(hops[d].wait_send)
            for e in edges:
                e.wait_send()

        return begin, middle, end, finish, edge_ready, drain

    def base_top(mine, n):
        return jnp.full((n, 1, LON), TOP, F32)

    def base_terrain(mine, n):
        return jnp.stack([terr[pl.ds(mine + i, 1), :] for i in range(n)], 0)

    top = [
        scan(
            k, s_own, s_pair, s_chip, s_recv, pre, pre_pair, 1, base_top,
            bp_s, bp_r, bz_s, bz_r, bq_s, bq_r, be_s, be_r,
        )
        for k in range(NCHUNK)
    ]
    bottom = [
        scan(
            k, d_own, d_pair, d_chip, d_recv, geo_off, geo_pair, -1, base_terrain,
            cp_s, cp_r, cz_s, cz_r, cq_s, cq_r, ce_s, ce_r,
        )
        for k in range(NCHUNK)
    ]

    def thickness(i, temp):
        base = pre[i]
        lp = jnp.log(base + cum[i])
        above = jnp.where(row == 0, jnp.log(base), pltpu.roll(lp, 1, 0))
        depth = GAS * temp * (lp - above)
        below = run_up(depth)
        height[i] = below - 0.5 * depth
        logmid[i] = 0.5 * (lp + above)
        return below[:1, :]

    def thickness_row(j):
        d_own[j] = thickness(j + 1, t_out[j])

    def gradient_row(j):
        pull = GAS * t_out[j]
        east[j] = east[j] - GRAD * (east_west(height[j + 1]) + pull * east_west(logmid[j + 1]))
        north[j] = north[j] - GRAD * (
            (height[j + 2] - height[j]) + pull * (logmid[j + 2] - logmid[j])
        )

    for f in (2, 3, 0, 1):
        load[f].wait()
    for k in range(EDGE):
        chunk_rows(k, column_row)
        top[k][0]()
    for k in range(EDGE):
        top[k][1]()

    load[4].wait()
    load[5].wait()

    def tracers(j):
        a_out[j] = advected(4, j)
        b_out[j] = advected(5, j)

    @pl.loop(1, ROWS // 2)
    def _(j):
        tracers(j)

    halo_ready(2)
    halo_ready(3)
    column_row(0)
    column_row(ROWS - 1)
    top[EDGE][0]()
    out_copies = []
    for n, (src, dst) in enumerate(((t_out, halo_t), (p_out, halo_p))):
        out_copies.append(
            remote(src.at[ROWS - 1], dst.at[0], out_s.at[n, 0], out_r.at[n, 0], (up, le))
        )
        out_copies.append(remote(src.at[0], dst.at[1], out_s.at[n, 1], out_r.at[n, 1], (down, le)))
    for c in out_copies:
        c.start()

    @pl.loop(ROWS // 2, ROWS - 1)
    def _(j):
        tracers(j)

    top[EDGE][1]()

    load[7].wait()
    load[8].wait()

    @pl.loop(0, ROWS)
    def _(j):
        c = csq[pl.ds(j, 1), :]
        at = pl.ds(pl.multiple_of(j * LEVS, LEVS), LEVS)
        for r in range(5):
            d = c / jnp.maximum(c, sines[r : r + 1, :])
            damp[r, at, :] = jnp.broadcast_to(d, (LEVS, LANE))

    cos9 = [math.cos(2.0 * math.pi * i / 9) for i in range(9)]
    sin9 = [math.sin(2.0 * math.pi * i / 9) for i in range(9)]

    def forward_nine(i):
        at = pl.ds(pl.multiple_of(i * 16, 16), 16)
        for f in range(2):
            x = jnp.concatenate([advected(f, 2 * i), advected(f, 2 * i + 1)], axis=0)
            xs = [x[:, LANE * a : LANE * (a + 1)] for a in range(9)]
            even = [xs[a] + xs[9 - a] for a in range(1, 5)]
            odd = [xs[a] - xs[9 - a] for a in range(1, 5)]
            y1[f, 0, at, :], y1[f, 1, at, :] = halves(xs[0] + ((even[0] + even[1]) + (even[2] + even[3])))
            for r in range(1, 5):
                re, im = xs[0], None
                for a in range(1, 5):
                    re = re + cos9[(a * r) % 9] * even[a - 1]
                    term = -sin9[(a * r) % 9] * odd[a - 1]
                    im = term if im is None else im + term
                hi, lo = halves(re)
                y4[f, r - 1, 0, at, :LANE], y4[f, r - 1, 1, at, :LANE] = hi, lo
                hi, lo = halves(im)
                y4[f, r - 1, 0, at, LANE:], y4[f, r - 1, 1, at, LANE:] = hi, lo

    def dot3(xh, xl, wh, wl):
        def mm(x, w):
            return jnp.dot(x, w, preferred_element_type=F32)

        return mm(xh, wh) + (mm(xl, wh) + mm(xh, wl))

    def spectrum(n):
        f, r = n // 4, n % 4
        x = dot3(y4[f, r, 0], y4[f, r, 1], wf[r, 0], wf[r, 1])
        d = damp[r + 1]
        xh, xl = halves(x * jnp.concatenate([d, d], axis=1))
        z4[f, r] = dot3(xh, xl, wb[r, 0], wb[r, 1])

    def spectrum_zero(f):
        x = dot3(y1[f, 0], y1[f, 1], wz[0], wz[1])
        xh, xl = halves(x * damp[0])
        z1[f] = dot3(xh, xl, wz[2], wz[3])

    def backward_nine(i):
        at = pl.ds(pl.multiple_of(i * 16, 16), 16)
        for f, dst in ((0, east), (1, north)):
            z0 = z1[f, at, :]
            re = [z4[f, r, at, :LANE] for r in range(4)]
            im = [z4[f, r, at, LANE:] for r in range(4)]
            outs = [None] * 9
            outs[0] = z0 + ((re[0] + re[1]) + (re[2] + re[3]))
            for a in range(1, 5):
                even, odd = z0, None
                for r in range(1, 5):
                    even = even + cos9[(a * r) % 9] * re[r - 1]
                    term = sin9[(a * r) % 9] * im[r - 1]
                    odd = term if odd is None else odd + term
                outs[a], outs[9 - a] = even - odd, even + odd
            for a in range(9):
                dst[2 * i, :, LANE * a : LANE * (a + 1)] = outs[a][:LEVS]
                dst[2 * i + 1, :, LANE * a : LANE * (a + 1)] = outs[a][LEVS:]

    for n in (9, 10, 11):
        load[n].wait()

    @pl.loop(0, 4)
    def _(r):
        @pl.loop(0, 4)
        def _(i):
            at = pl.ds(pl.multiple_of(i * 64, 64), 64)
            wf[r, 0, at, :], wf[r, 1, at, :] = halves(wf32[r, at, :])
            wb[r, 0, at, :], wb[r, 1, at, :] = halves(wb32[r, at, :])

    wz[0], wz[1] = halves(wz32[0])
    wz[2], wz[3] = halves(wz32[1])

    halo_ready(0)
    halo_ready(1)

    @pl.loop(0, ROWS // 2)
    def _(i):
        forward_nine(i)

    load[6].wait()

    for k in range(EDGE):
        top[k][2]()
        top[k][3]()
        chunk_rows(k, thickness_row)
        bottom[k][0]()
        if k == 0:
            spectrum_zero(0)
            spectrum_zero(1)
        else:
            pl.loop(0, 1)(spectrum)
        bottom[k][1]()
    top[EDGE][2]()
    top[EDGE][3]()
    chunk_rows(EDGE, thickness_row)
    bottom[EDGE][0]()
    halo_ready(4)
    halo_ready(5)
    tracers(0)
    tracers(ROWS - 1)
    bottom[EDGE][1]()

    pl.loop(1, 8)(spectrum)

    @pl.loop(0, ROWS // 2)
    def _(i):
        backward_nine(i)

    for c in out_copies:
        c.wait_recv()
    top[EDGE][4]()
    for side in range(2):
        i = (ROWS + 1) * side
        cum[i] = run_down(halo_p[side])
        thickness(i, halo_t[side])

    @pl.when(la == 0)
    def _():
        height[0] = height[1]
        logmid[0] = logmid[1]

    @pl.when(la == NLAT - 1)
    def _():
        height[ROWS + 1] = height[ROWS]
        logmid[ROWS + 1] = logmid[ROWS]

    @pl.loop(0, ROWS)
    def _(j):
        gradient_row(j)

    for k in range(NCHUNK):
        bottom[k][2]()
    for k in range(NCHUNK):
        bottom[k][3]()
    bottom[EDGE][4]()

    @pl.when(la == 0)
    def _():
        geo_off[0] = geo_off[1]

    @pl.when(la == NLAT - 1)
    def _():
        geo_off[ROWS + 1] = geo_off[ROWS]

    for k in range(NCHUNK):
        top[k][5]()
        bottom[k][5]()
    for key in halo:
        halo[key].wait_send()
    for c in out_copies:
        c.wait_send()


def second_kernel(
    height, east, north, t_out, p_out, a_out, b_out, geo_off,
    east_hbm, north_hbm, t_hbm, p_hbm, a_hbm, b_hbm, geo_hbm,
    east_buf, north_buf, geo_buf, sem,
):
    copies = [
        pltpu.make_async_copy(src, dst, sem.at[n])
        for n, (src, dst) in enumerate(((t_out, t_hbm), (p_out, p_hbm), (a_out, a_hbm), (b_out, b_hbm)))
    ]
    for c in copies:
        c.start()
    part = 8
    for q in range(ROWS // part):

        @pl.loop(part * q, part * (q + 1))
        def _(j):
            off = geo_off[j + 1]
            geo_buf[j] = height[j + 1] + off
            east_buf[j] = east[j] - GRAD * east_west(off)
            north_buf[j] = north[j] - GRAD * (geo_off[j + 2] - geo_off[j])

        for m, (src, dst) in enumerate(((east_buf, east_hbm), (north_buf, north_hbm), (geo_buf, geo_hbm))):
            rows = pl.ds(part * q, part)
            c = pltpu.make_async_copy(src.at[rows], dst.at[rows], sem.at[4 + 3 * q + m])
            c.start()
            copies.append(c)
    for c in copies:
        c.wait()


def shards(u, v, t, p, a, b, terrain):
    wf, wb, wz, sines, csq = (jnp.asarray(x) for x in tables())
    ins = [u, v, t, p, a, b, terrain, csq, sines, wf, wb, wz]
    ins = [pltpu.with_memory_space_constraint(x, pltpu.HBM) for x in ins]
    full = (ROWS, LEVS, LON)
    wide = (ROWS + 2, LEVS, LON)
    line = (ROWS, 1, LON)
    line_wide = (ROWS + 2, 1, LON)
    dma = pltpu.SemaphoreType.DMA
    scan_sems = [
        dma((NCHUNK,)), dma((NCHUNK,)), dma((NCHUNK, 3)), dma((NCHUNK, 3)),
        dma((NCHUNK,)), dma((NCHUNK,)), dma((2,)), dma((2,)),
    ]
    mids = pl.pallas_call(
        first_kernel,
        out_shape=[pltpu.VMEM(wide, F32)] + [pltpu.VMEM(full, F32)] * 6 + [pltpu.VMEM(line_wide, F32)],
        in_specs=[pl.BlockSpec(memory_space=pltpu.HBM)] * len(ins),
        out_specs=[pl.BlockSpec(memory_space=pltpu.VMEM)] * 8,
        scratch_shapes=[
            pltpu.VMEM((6,) + wide, F32),
            pltpu.VMEM((ROWS, LON), F32),
            pltpu.VMEM((ROWS, LANE), F32),
            pltpu.VMEM((8, LANE), F32),
            pltpu.VMEM((4, 256, 256), F32),
            pltpu.VMEM((4, 256, 256), F32),
            pltpu.VMEM((2, LANE, LANE), F32),
            pltpu.VMEM((4, 2, 256, 256), BF16),
            pltpu.VMEM((4, 2, 256, 256), BF16),
            pltpu.VMEM((4, LANE, LANE), BF16),
            pltpu.VMEM(wide, F32),
            pltpu.VMEM(wide, F32),
            pltpu.VMEM((2, LEVS, LON), F32),
            pltpu.VMEM((2, LEVS, LON), F32),
            pltpu.VMEM((5, ROWS * LEVS, LANE), F32),
            pltpu.VMEM(line, F32),
            pltpu.VMEM(line, F32),
            pltpu.VMEM(line, F32),
            pltpu.VMEM((3,) + line, F32),
            pltpu.VMEM(line_wide, F32),
            pltpu.VMEM(line, F32),
            pltpu.VMEM(line, F32),
            pltpu.VMEM(line, F32),
            pltpu.VMEM(line, F32),
            pltpu.VMEM((3,) + line, F32),
            pltpu.VMEM(line, F32),
            pltpu.VMEM((2, 4, 2, ROWS * LEVS, 2 * LANE), BF16),
            pltpu.VMEM((2, 2, ROWS * LEVS, LANE), BF16),
            pltpu.VMEM((2, 4, ROWS * LEVS, 2 * LANE), F32),
            pltpu.VMEM((2, ROWS * LEVS, LANE), F32),
            dma((12,)), dma((6, 2)), dma((6, 2)), dma((2, 2)), dma((2, 2)),
        ]
        + scan_sems
        + scan_sems,
        compiler_params=pltpu.CompilerParams(
            collective_id=0, has_side_effects=True, vmem_limit_bytes=40 << 20
        ),
    )(*ins)
    outs = pl.pallas_call(
        second_kernel,
        out_shape=[jax.ShapeDtypeStruct(full, F32)] * 7,
        in_specs=[pl.BlockSpec(memory_space=pltpu.VMEM)] * 8,
        out_specs=[pl.BlockSpec(memory_space=pltpu.HBM)] * 7,
        scratch_shapes=[pltpu.VMEM(full, F32)] * 3 + [dma((13,))],
        compiler_params=pltpu.CompilerParams(vmem_limit_bytes=20 << 20),
    )(*mids)
    return tuple(outs)


def solution(mesh):
    field = P("lat", "lev", None)
    return jax.shard_map(
        shards,
        mesh=mesh,
        in_specs=(field,) * 6 + (P("lat", None),),
        out_specs=(field,) * 7,
        check_vma=False,
    )
```

```python
import functools
import math

import jax
import jax.numpy as jnp
import numpy as np
from jax import lax
from jax.experimental import pallas as pl
from jax.experimental.pallas import tpu as pltpu
from jax.sharding import PartitionSpec as P

MESH = pl.DeviceIdType.MESH
F32 = jnp.float32
BF16 = jnp.bfloat16

ROWS, LEVS, LON = 24, 8, 1152
NLAT = 32
CHIPS = 4
LANE = 128
COURANT = 0.1
GRAD = 0.1
GAS = 0.3
TOP = 1.0
CUT = 0.5

POLAR = sum(
    math.cos(((ROWS * band + ROWS - 0.5) / (NLAT * ROWS) - 0.5) * math.pi) ** 2 < CUT
    or math.cos(((ROWS * band + 0.5) / (NLAT * ROWS) - 0.5) * math.pi) ** 2 < CUT
    for band in range(NLAT // 2)
)
INTERIOR = ((1, 6), (13, 5))
EDGE = len(INTERIOR)
NCHUNK = EDGE + 1


@functools.cache
def tables():
    b = np.arange(LANE)
    fwd, back = [], []
    for r in range(1, 5):
        angle = 2.0 * np.pi * ((b[:, None] * (9 * b[None, :] + r)) % LON) / LON
        mr, mi = np.cos(angle), -np.sin(angle)
        w = np.block([[mr, mi], [-mi, mr]])
        fwd.append(w)
        back.append(w.T * (2.0 / LON))
    angle = 2.0 * np.pi * ((b[:, None] * b[None, :]) % LANE) / LANE
    w0 = np.concatenate([np.cos(angle[:, :65]), np.sin(angle[:, 1:64])], axis=1)
    weight = np.full((LANE,), 2.0)
    weight[0] = weight[64] = 1.0
    b0 = (w0 * weight[None, :]).T / LON
    wf = np.stack(fwd).astype(np.float32)
    wb = np.stack(back).astype(np.float32)
    wz = np.stack([w0, b0]).astype(np.float32)
    sines = np.zeros((8, LANE))
    freq0 = np.concatenate([np.arange(65), np.arange(1, 64)]) * 9
    sines[0] = np.sin(np.pi * freq0 / LON) ** 2 * CUT
    for r in range(1, 5):
        sines[r] = np.sin(np.pi * (9 * b + r) / LON) ** 2 * CUT
    lat = (np.arange(NLAT * ROWS, dtype=np.float32) + np.float32(0.5)) * np.float32(
        math.pi / (NLAT * ROWS)
    ) - np.float32(0.5 * math.pi)
    csq = np.cos(lat.astype(np.float64)).astype(np.float32) ** 2
    csq = np.broadcast_to(csq.reshape(NLAT, ROWS, 1), (NLAT, ROWS, LANE)).astype(np.float32)
    return wf, wb, wz, sines.astype(np.float32), np.ascontiguousarray(csq)


def east_west(x):
    return pltpu.roll(x, LON - 1, 1) - pltpu.roll(x, 1, 1)


def first_kernel(
    u_hbm, v_hbm, t_hbm, p_hbm, a_hbm, b_hbm, terr_hbm, csq_hbm, sin_hbm, wf_hbm, wb_hbm, wz_hbm,
    height, east, north, t_out, p_out, a_out, b_out, geo_off,
    fields, terr, csq, sines, wf32, wb32, wz32, wf, wb, wz,
    cum, logmid, halo_t, halo_p, damp, pair_t, pair_c,
    s_own, s_pair, s_chip, s_recv, pre, pre_pair,
    d_own, d_pair, d_chip, d_recv, geo_pair,
    y4, y1, z4, z1,
    ready, load_sem, halo_s, halo_r, out_s, out_r, both_s, both_r,
    bp_s, bp_r, bz_s, bz_r, bq_s, bq_r, be_s, be_r,
    cz_s, cz_r, cq_s, cq_r, ce_s, ce_r,
):
    la, le = lax.axis_index("lat"), lax.axis_index("lev")
    chip, core = le // 2, le % 2
    other = 1 - core
    up, down = (la + 1) % NLAT, (la + NLAT - 1) % NLAT
    pair_dev = (la, chip * 2 + other)
    side_lat = (la + NLAT - 1 + 2 * core) % NLAT
    cross_dev = (side_lat, chip * 2 + other)
    side_dev = (side_lat, le)
    has_up, has_down = la < NLAT - 1, la > 0
    has_side = jnp.where(core == 0, la, NLAT - 1 - la) > 0
    core_f = core.astype(F32)
    other_f = other.astype(F32)

    def remote(src, dst, send, recv, dev):
        return pltpu.make_async_remote_copy(
            src_ref=src, dst_ref=dst, send_sem=send, recv_sem=recv, device_id=dev, device_id_type=MESH
        )

    ins = (u_hbm, v_hbm, t_hbm, p_hbm, a_hbm, b_hbm)
    load = [
        pltpu.make_async_copy(ins[f], fields.at[f, pl.ds(1, ROWS)], load_sem.at[f]) for f in range(6)
    ]
    load += [
        pltpu.make_async_copy(terr_hbm, terr, load_sem.at[6]),
        pltpu.make_async_copy(csq_hbm.at[la], csq, load_sem.at[7]),
        pltpu.make_async_copy(sin_hbm, sines, load_sem.at[8]),
        pltpu.make_async_copy(wf_hbm, wf32, load_sem.at[9]),
        pltpu.make_async_copy(wb_hbm, wb32, load_sem.at[10]),
        pltpu.make_async_copy(wz_hbm, wz32, load_sem.at[11]),
    ]

    barrier = pltpu.get_barrier_semaphore()
    upper = chip < CHIPS // 2
    others = [(chip + d) % CHIPS for d in range(1, CHIPS)]
    greet = [(la >= 0, pair_dev), (has_up, (up, le)), (has_down, (down, le)), (has_side, cross_dev)]
    greet += [(upper | (c >= CHIPS // 2), (la, c * 2 + core)) for c in others]
    for there, dev in greet:

        @pl.when(there)
        def _():
            pl.semaphore_signal(barrier, inc=1, device_id=dev, device_id_type=MESH)

    for f in (3, 0, 1, 2):
        load[f].start()

    halo = {}
    for f in (2, 3, 0, 1, 4, 5):
        halo[f, 0] = remote(
            ins[f].at[ROWS - 1], fields.at[f, 0], halo_s.at[f, 0], halo_r.at[f, 0], (up, le)
        )
        halo[f, 1] = remote(
            ins[f].at[0], fields.at[f, ROWS + 1], halo_s.at[f, 1], halo_r.at[f, 1], (down, le)
        )

    seam = la == NLAT // 2 - 1

    def halo_start(f):
        pl.when(has_up & ~seam)(halo[f, 0].start)
        pl.when(has_down)(halo[f, 1].start)

    def enter():
        near = has_up.astype(jnp.int32) + has_down.astype(jnp.int32) + has_side.astype(jnp.int32)
        pl.semaphore_wait(barrier, near + jnp.where(upper, 2, 4))

        @pl.when(~upper)
        def _():
            for c in range(CHIPS // 2):
                pl.semaphore_signal(ready, inc=1, device_id=(la, c * 2 + core), device_id_type=MESH)

        for f in (3, 2):
            pl.when(has_up)(halo[f, 0].start)
            pl.when(has_down)(halo[f, 1].start)

    enter()

    row = lax.broadcasted_iota(jnp.int32, (LEVS, LON), 0)

    def halves(x):
        hi = x.astype(BF16)
        return hi, (x - hi.astype(F32)).astype(BF16)

    def run_down(x):
        for s in (1, 2, 4):
            x = x + jnp.where(row >= s, pltpu.roll(x, s, 0), 0.0)
        return x

    def run_up(x):
        for s in (1, 2, 4):
            x = x + jnp.where(row < LEVS - s, pltpu.roll(x, LEVS - s, 0), 0.0)
        return x

    def advected(f, j):
        x = fields[f, j + 1]
        merid = fields[f, j + 2] - fields[f, j]
        return x - COURANT * (fields[0, j + 1] * east_west(x) + fields[1, j + 1] * merid)

    def halo_ready(f):
        @pl.when(has_down)
        def _():
            halo[f, 0].wait_recv()

        @pl.when(has_up)
        def _():
            halo[f, 1].wait_recv()

        @pl.when(la == 0)
        def _():
            fields[f, 0] = fields[f, 1]

        @pl.when(la == NLAT - 1)
        def _():
            fields[f, ROWS + 1] = fields[f, ROWS]

    def column_t(j):
        t_out[j] = advected(2, j)

    def column_p(j):
        p = advected(3, j)
        p_out[j] = p
        c = run_down(p)
        cum[j + 1] = c
        s_own[j] = c[LEVS - 1 :, :]

    def span(k):
        if k == EDGE:
            return (ROWS - 1) * core, (ROWS - 1) * other, 1
        start, n = INTERIOR[k]
        return start + n * core, start + n * other, n

    def chunk_rows(k, body):
        if k == EDGE:
            body(0)
            body(ROWS - 1)
        else:
            start, n = INTERIOR[k]

            @pl.loop(start, start + 2 * n, unroll=2)
            def _(j):
                body(j)

    def scan(k, own, pair, total, recv, result, result_pair, sign, base, zs, zr, qs, qr, es, er, ps=None, pr=None):
        mine, theirs, n = span(k)
        mine_s, theirs_s = pl.ds(mine, n), pl.ds(theirs, n)
        if ps is not None:
            to_pair = remote(own.at[theirs_s], pair.at[theirs_s], ps.at[k], pr.at[k], pair_dev)
            from_pair = remote(own.at[mine_s], pair.at[mine_s], ps.at[k], pr.at[k], pair_dev)
        share = remote(
            result_pair.at[mine_s], result.at[pl.ds(mine + 1, n)], qs.at[k], qr.at[k], pair_dev
        )
        shared = remote(
            result_pair.at[theirs_s], result.at[pl.ds(theirs + 1, n)], qs.at[k], qr.at[k], pair_dev
        )
        hops = {}
        for d in (2, 1, 3):
            hops[d] = remote(
                total.at[mine_s], recv.at[d - 1, mine_s], zs.at[k, d - 1], zr.at[k, d - 1],
                (la, ((chip + CHIPS + sign * d) % CHIPS) * 2 + core),
            )
        if sign > 0:
            sends = {d: chip + d < CHIPS for d in hops}
            gets = {d: chip >= d for d in hops}
        else:
            sends = {d: chip >= d for d in hops}
            gets = {d: chip + d < CHIPS for d in hops}
        edges = []
        if k == EDGE:
            slot = (ROWS + 1) * other
            edges = [
                remote(result.at[mine + 1], result.at[slot], es.at[0], er.at[other], side_dev),
                remote(result_pair.at[mine], result.at[slot], es.at[1], er.at[other], cross_dev),
            ]

        def begin():
            to_pair.start()

        def middle():
            if ps is not None:
                from_pair.wait_recv()
            total[mine_s] = own[mine_s] + pair[mine_s]
            if sign > 0:
                pl.when(chip % 2 == 0)(hops[1].start)
            else:
                for d in hops:
                    pl.when(sends[d])(hops[d].start)

        def across():
            for d in hops:
                pl.when(upper & sends[d] & ((chip + d) >= CHIPS // 2))(hops[d].start)

        def end():
            acc = base(mine, n)
            result[pl.ds(mine + 1, n)] = acc
            for d in hops:

                @pl.when(gets[d])
                def _():
                    hops[d].wait_recv()
                    result[pl.ds(mine + 1, n)] = result[pl.ds(mine + 1, n)] + recv[d - 1, mine_s]

            acc = result[pl.ds(mine + 1, n)]
            mine_f, pair_f = (core_f, other_f) if sign > 0 else (other_f, core_f)
            result_pair[mine_s] = acc + pair_f * own[mine_s]
            share.start()
            result[pl.ds(mine + 1, n)] = acc + mine_f * pair[mine_s]
            for e in edges:
                pl.when(has_side)(e.start)

        def finish():
            shared.wait_recv()

        def edge_ready():
            for side, there in ((0, has_down), (1, has_up)):
                slot = (ROWS + 1) * side
                c = remote(result.at[slot], result.at[slot], es.at[0], er.at[side], side_dev)
                pl.when(there)(c.wait_recv)

        def drain():
            if ps is not None:
                to_pair.wait_send()
            share.wait_send()
            for d in hops:
                pl.when(sends[d])(hops[d].wait_send)
            for e in edges:
                pl.when(has_side)(e.wait_send)

        return begin, middle, end, finish, edge_ready, drain, across

    def base_top(mine, n):
        return jnp.full((n, 1, LON), TOP, F32)

    def base_terrain(mine, n):
        return jnp.stack([terr[pl.ds(mine + i, 1), :] for i in range(n)], 0)

    top = [
        scan(
            k, s_own, s_pair, s_chip, s_recv, pre, pre_pair, 1, base_top,
            bz_s, bz_r, bq_s, bq_r, be_s, be_r, bp_s, bp_r,
        )
        for k in range(NCHUNK)
    ]
    bottom = [
        scan(
            k, d_own, d_pair, d_chip, d_recv, geo_off, geo_pair, -1, base_terrain,
            cz_s, cz_r, cq_s, cq_r, ce_s, ce_r,
        )
        for k in range(NCHUNK)
    ]

    def thickness(i, temp):
        base = pre[i]
        lp = jnp.log(base + cum[i])
        above = jnp.where(row == 0, jnp.log(base), pltpu.roll(lp, 1, 0))
        depth = GAS * temp * (lp - above)
        below = run_up(depth)
        height[i] = below - 0.5 * depth
        logmid[i] = 0.5 * (lp + above)
        return below[:1, :]

    def thickness_row(j):
        d_own[j] = thickness(j + 1, t_out[j])

    def gradient_row(j):
        pull = GAS * t_out[j]
        east[j] = east[j] - GRAD * (east_west(height[j + 1]) + pull * east_west(logmid[j + 1]))
        north[j] = north[j] - GRAD * (
            (height[j + 2] - height[j]) + pull * (logmid[j + 2] - logmid[j])
        )

    def both(k):
        _, theirs, n = span(k)
        at = pl.ds(theirs, n)
        return (
            remote(cum.at[pl.ds(theirs + 1, n)], pair_c.at[at], both_s.at[k, 0], both_r.at[k, 0], pair_dev),
            remote(t_out.at[at], pair_t.at[at], both_s.at[k, 1], both_r.at[k, 1], pair_dev),
        )

    def pair_row(j):
        base = pre_pair[j]
        lp = jnp.log(base + pair_c[j])
        above = jnp.where(row == 0, jnp.log(base), pltpu.roll(lp, 1, 0))
        depth = GAS * pair_t[j] * (lp - above)
        d_pair[j] = jnp.sum(depth, axis=0, keepdims=True)

    def mine_rows(k):
        mine, _, n = span(k)

        @pl.loop(0, n, unroll=n)
        def _(i):
            thickness_row(mine + i)
            pair_row(mine + i)

    def their_rows(k):
        _, theirs, n = span(k)

        @pl.loop(0, n, unroll=n)
        def _(i):
            thickness_row(theirs + i)

    def tracers(j):
        a_out[j] = advected(4, j)
        b_out[j] = advected(5, j)

    def inner_tracers():
        @pl.loop(1, ROWS - 1, unroll=2)
        def _(j):
            tracers(j)

    for f in (3, 0, 1):
        load[f].wait()
    for f in (4, 5, 6, 7, 8, 9, 10, 11):
        load[f].start()
    for k in range(EDGE):
        chunk_rows(k, column_p)
        top[k][0]()
    load[2].wait()
    pairs = [both(k) for k in range(NCHUNK)]
    for k in range(EDGE):
        chunk_rows(k, column_t)
        for c in pairs[k]:
            c.start()
    for k in range(EDGE):
        top[k][1]()
    halo_start(0)
    halo_start(1)

    @pl.when(upper)
    def _():
        pl.semaphore_wait(ready, CHIPS // 2)

    for k in range(EDGE):
        top[k][6]()

    halo_ready(3)
    column_p(0)
    column_p(ROWS - 1)
    top[EDGE][0]()
    halo_ready(2)
    column_t(0)
    column_t(ROWS - 1)
    for c in pairs[EDGE]:
        c.start()
    out_copies = []
    for n, (src, dst) in enumerate(((t_out, halo_t), (p_out, halo_p))):
        out_copies.append(
            remote(src.at[ROWS - 1], dst.at[0], out_s.at[n, 0], out_r.at[n, 0], (up, le))
        )
        out_copies.append(remote(src.at[0], dst.at[1], out_s.at[n, 1], out_r.at[n, 1], (down, le)))
    ways = (has_up, has_down)
    top[EDGE][1]()
    top[EDGE][6]()
    for n, c in enumerate(out_copies):
        pl.when(ways[n % 2])(c.start)

    @pl.when(seam)
    def _():
        halo[0, 0].start()
        halo[1, 0].start()

    for f in (4, 5):
        pl.when(has_up)(halo[f, 0].start)
        pl.when(has_down)(halo[f, 1].start)

    for n in (4, 5, 6, 7, 8, 9, 10, 11):
        load[n].wait()

    def prepare():
        @pl.loop(0, ROWS, unroll=4)
        def _(j):
            c = csq[pl.ds(j, 1), :]
            at = pl.ds(pl.multiple_of(j * LEVS, LEVS), LEVS)
            for r in range(5):
                d = c / jnp.maximum(c, sines[r : r + 1, :])
                damp[r, at, :] = jnp.broadcast_to(d, (LEVS, LANE))

        for full, parts in ((wf32, wf), (wb32, wb)):

            @pl.loop(0, 4)
            def _(r):
                for i in range(0, 256, 64):
                    hi, lo = halves(full[r, i : i + 64, :])
                    parts[r, i : i + 64, :] = hi
                    parts[r, 256 + i : 320 + i, :] = hi
                    parts[r, 512 + i : 576 + i, :] = lo

        for n in range(2):
            hi, lo = halves(wz32[n])
            wz[n, :LANE, :], wz[n, LANE : 2 * LANE, :], wz[n, 2 * LANE :, :] = hi, hi, lo

    cos9 = [math.cos(2.0 * math.pi * i / 9) for i in range(9)]
    sin9 = [math.sin(2.0 * math.pi * i / 9) for i in range(9)]

    def forward_nine(i):
        for f in range(2):
            at = pl.ds(pl.multiple_of(f * ROWS * LEVS + i * 16, 16), 16)
            x = jnp.concatenate([advected(f, 2 * i), advected(f, 2 * i + 1)], axis=0)
            xs = [x[:, LANE * a : LANE * (a + 1)] for a in range(9)]
            even = [xs[a] + xs[9 - a] for a in range(1, 5)]
            odd = [xs[a] - xs[9 - a] for a in range(1, 5)]
            hi, lo = halves(xs[0] + ((even[0] + even[1]) + (even[2] + even[3])))
            y1[at, :LANE], y1[at, LANE : 2 * LANE], y1[at, 2 * LANE :] = hi, lo, hi
            for r in range(1, 5):
                re, im = xs[0], None
                for a in range(1, 5):
                    re = re + cos9[(a * r) % 9] * even[a - 1]
                    term = -sin9[(a * r) % 9] * odd[a - 1]
                    im = term if im is None else im + term
                for part, y in ((0, re), (1, im)):
                    hi, lo = halves(y)
                    for place, value in ((0, hi), (2, lo), (4, hi)):
                        place = (place + part) * LANE
                        y4[r - 1, at, place : place + LANE] = value

    def triple(x):
        hi, lo = halves(x)
        return jnp.concatenate([hi, lo, hi], axis=1)

    def mm(x, w):
        return jnp.dot(x, w, preferred_element_type=F32)

    def spectrum(r):
        d = damp[r + 1]
        d = jnp.concatenate([d, d], axis=1)
        d = jnp.concatenate([d, d], axis=0)
        z4[r] = mm(triple(mm(y4[r], wf[r]) * d), wb[r])

    def spectrum_zero():
        d = jnp.concatenate([damp[0], damp[0]], axis=0)
        z1[...] = mm(triple(mm(y1[...], wz[0]) * d), wz[1])

    def backward_nine(i):
        for f, dst in ((0, east), (1, north)):
            at = pl.ds(pl.multiple_of(f * ROWS * LEVS + i * 16, 16), 16)
            z0 = z1[at, :]
            re = [z4[r, at, :LANE] for r in range(4)]
            im = [z4[r, at, LANE:] for r in range(4)]
            outs = [None] * 9
            outs[0] = z0 + ((re[0] + re[1]) + (re[2] + re[3]))
            for a in range(1, 5):
                even, odd = z0, None
                for r in range(1, 5):
                    even = even + cos9[(a * r) % 9] * re[r - 1]
                    term = sin9[(a * r) % 9] * im[r - 1]
                    odd = term if odd is None else odd + term
                outs[a], outs[9 - a] = even - odd, even + odd
            for a in range(9):
                dst[2 * i, :, LANE * a : LANE * (a + 1)] = outs[a][:LEVS]
                dst[2 * i + 1, :, LANE * a : LANE * (a + 1)] = outs[a][LEVS:]

    polar = (la < POLAR) | (la >= NLAT - POLAR)

    def forward():
        prepare()
        halo_ready(0)
        halo_ready(1)

        @pl.loop(0, ROWS // 2, unroll=2)
        def _(i):
            forward_nine(i)

    pl.when(upper)(inner_tracers)
    pl.when(polar & upper)(forward)

    for k in range(EDGE):
        top[k][2]()
        for c in pairs[k]:
            c.wait_recv()
        mine_rows(k)
        bottom[k][1]()
    top[EDGE][2]()
    for c in pairs[EDGE]:
        c.wait_recv()
    mine_rows(EDGE)
    bottom[EDGE][1]()
    for k in range(NCHUNK):
        top[k][3]()
        their_rows(k)
    pl.when(~upper)(inner_tracers)
    pl.when(polar & ~upper)(forward)

    @pl.when(polar)
    def _():
        spectrum_zero()
        pl.loop(0, 4)(spectrum)

        @pl.loop(0, ROWS // 2, unroll=2)
        def _(i):
            backward_nine(i)

    @pl.when(~polar)
    def _():
        @pl.loop(1, ROWS - 1, unroll=2)
        def _(j):
            east[j] = advected(0, j)
            north[j] = advected(1, j)

        halo_ready(0)
        halo_ready(1)
        for j in (0, ROWS - 1):
            east[j] = advected(0, j)
            north[j] = advected(1, j)

    @pl.loop(1, ROWS - 1, unroll=2)
    def _(j):
        gradient_row(j)

    halo_ready(4)
    halo_ready(5)
    tracers(0)
    tracers(ROWS - 1)

    for n, c in enumerate(out_copies):
        pl.when(ways[1 - n % 2])(c.wait_recv)
    top[EDGE][4]()
    for side, there in ((0, has_down), (1, has_up)):

        @pl.when(there)
        def _():
            i = (ROWS + 1) * side
            cum[i] = run_down(halo_p[side])
            thickness(i, halo_t[side])

    @pl.when(la == 0)
    def _():
        height[0] = height[1]
        logmid[0] = logmid[1]

    @pl.when(la == NLAT - 1)
    def _():
        height[ROWS + 1] = height[ROWS]
        logmid[ROWS + 1] = logmid[ROWS]

    gradient_row(0)
    gradient_row(ROWS - 1)

    for k in range(NCHUNK):
        bottom[k][2]()
    for k in range(NCHUNK):
        bottom[k][3]()
    bottom[EDGE][4]()

    @pl.when(la == 0)
    def _():
        geo_off[0] = geo_off[1]

    @pl.when(la == NLAT - 1)
    def _():
        geo_off[ROWS + 1] = geo_off[ROWS]

    for k in range(NCHUNK):
        top[k][5]()
        bottom[k][5]()
    for pair in pairs:
        for c in pair:
            c.wait_send()
    for (f, side), c in halo.items():
        pl.when(ways[side])(c.wait_send)
    for n, c in enumerate(out_copies):
        pl.when(ways[n % 2])(c.wait_send)


def second_kernel(
    height, east, north, t_out, p_out, a_out, b_out, geo_off,
    east_hbm, north_hbm, t_hbm, p_hbm, a_hbm, b_hbm, geo_hbm,
    east_buf, north_buf, geo_buf, sem,
):
    copies = [
        pltpu.make_async_copy(src, dst, sem.at[n])
        for n, (src, dst) in enumerate(((t_out, t_hbm), (p_out, p_hbm), (a_out, a_hbm), (b_out, b_hbm)))
    ]
    for c in copies:
        c.start()
    part = 8
    for q in range(ROWS // part):

        @pl.loop(part * q, part * (q + 1), unroll=4)
        def _(j):
            off = geo_off[j + 1]
            geo_buf[j] = height[j + 1] + off
            east_buf[j] = east[j] - GRAD * east_west(off)
            north_buf[j] = north[j] - GRAD * (geo_off[j + 2] - geo_off[j])

        for m, (src, dst) in enumerate(((east_buf, east_hbm), (north_buf, north_hbm), (geo_buf, geo_hbm))):
            rows = pl.ds(part * q, part)
            c = pltpu.make_async_copy(src.at[rows], dst.at[rows], sem.at[4 + 3 * q + m])
            c.start()
            copies.append(c)
    for c in copies:
        c.wait()


def shards(u, v, t, p, a, b, terrain):
    wf, wb, wz, sines, csq = (jnp.asarray(x) for x in tables())
    ins = [u, v, t, p, a, b, terrain, csq, sines, wf, wb, wz]
    ins = [pltpu.with_memory_space_constraint(x, pltpu.HBM) for x in ins]
    full = (ROWS, LEVS, LON)
    wide = (ROWS + 2, LEVS, LON)
    line = (ROWS, 1, LON)
    line_wide = (ROWS + 2, 1, LON)
    dma = pltpu.SemaphoreType.DMA
    scan_sems = [
        dma((NCHUNK,)), dma((NCHUNK,)), dma((NCHUNK, 3)), dma((NCHUNK, 3)),
        dma((NCHUNK,)), dma((NCHUNK,)), dma((2,)), dma((2,)),
    ]
    mids = pl.pallas_call(
        first_kernel,
        out_shape=[pltpu.VMEM(wide, F32)] + [pltpu.VMEM(full, F32)] * 6 + [pltpu.VMEM(line_wide, F32)],
        in_specs=[pl.BlockSpec(memory_space=pltpu.HBM)] * len(ins),
        out_specs=[pl.BlockSpec(memory_space=pltpu.VMEM)] * 8,
        scratch_shapes=[
            pltpu.VMEM((6,) + wide, F32),
            pltpu.VMEM((ROWS, LON), F32),
            pltpu.VMEM((ROWS, LANE), F32),
            pltpu.VMEM((8, LANE), F32),
            pltpu.VMEM((4, 256, 256), F32),
            pltpu.VMEM((4, 256, 256), F32),
            pltpu.VMEM((2, LANE, LANE), F32),
            pltpu.VMEM((4, 3 * 256, 256), BF16),
            pltpu.VMEM((4, 3 * 256, 256), BF16),
            pltpu.VMEM((2, 3 * LANE, LANE), BF16),
            pltpu.VMEM(wide, F32),
            pltpu.VMEM(wide, F32),
            pltpu.VMEM((2, LEVS, LON), F32),
            pltpu.VMEM((2, LEVS, LON), F32),
            pltpu.VMEM((5, ROWS * LEVS, LANE), F32),
            pltpu.VMEM(full, F32),
            pltpu.VMEM(full, F32),
            pltpu.VMEM(line, F32),
            pltpu.VMEM(line, F32),
            pltpu.VMEM(line, F32),
            pltpu.VMEM((3,) + line, F32),
            pltpu.VMEM(line_wide, F32),
            pltpu.VMEM(line, F32),
            pltpu.VMEM(line, F32),
            pltpu.VMEM(line, F32),
            pltpu.VMEM(line, F32),
            pltpu.VMEM((3,) + line, F32),
            pltpu.VMEM(line, F32),
            pltpu.VMEM((4, 2 * ROWS * LEVS, 6 * LANE), BF16),
            pltpu.VMEM((2 * ROWS * LEVS, 3 * LANE), BF16),
            pltpu.VMEM((4, 2 * ROWS * LEVS, 2 * LANE), F32),
            pltpu.VMEM((2 * ROWS * LEVS, LANE), F32),
            pltpu.SemaphoreType.REGULAR, dma((12,)), dma((6, 2)), dma((6, 2)), dma((2, 2)), dma((2, 2)),
            dma((NCHUNK, 2)), dma((NCHUNK, 2)),
        ]
        + scan_sems
        + scan_sems[2:],
        compiler_params=pltpu.CompilerParams(
            collective_id=0, has_side_effects=True, vmem_limit_bytes=40 << 20
        ),
    )(*ins)
    outs = pl.pallas_call(
        second_kernel,
        out_shape=[jax.ShapeDtypeStruct(full, F32)] * 7,
        in_specs=[pl.BlockSpec(memory_space=pltpu.VMEM)] * 8,
        out_specs=[pl.BlockSpec(memory_space=pltpu.HBM)] * 7,
        scratch_shapes=[pltpu.VMEM(full, F32)] * 3 + [dma((13,))],
        compiler_params=pltpu.CompilerParams(vmem_limit_bytes=20 << 20),
    )(*mids)
    return tuple(outs)


def solution(mesh):
    field = P("lat", "lev", None)
    return jax.shard_map(
        shards,
        mesh=mesh,
        in_specs=(field,) * 6 + (P("lat", None),),
        out_specs=(field,) * 7,
        check_vma=False,
    )
```

```python
import functools
import math

import jax
import jax.numpy as jnp
import numpy as np
from jax import lax
from jax.experimental import pallas as pl
from jax.experimental.pallas import tpu as pltpu
from jax.sharding import PartitionSpec as P

MESH = pl.DeviceIdType.MESH
F32 = jnp.float32
BF16 = jnp.bfloat16

ROWS, LEVS, LON = 24, 8, 1152
NLAT = 32
CHIPS = 4
LANE = 128
COURANT = 0.1
GRAD = 0.1
GAS = 0.3
TOP = 1.0
CUT = 0.5

POLAR = sum(
    math.cos(((ROWS * band + ROWS - 0.5) / (NLAT * ROWS) - 0.5) * math.pi) ** 2 < CUT
    or math.cos(((ROWS * band + 0.5) / (NLAT * ROWS) - 0.5) * math.pi) ** 2 < CUT
    for band in range(NLAT // 2)
)
INTERIOR = ((1, 6), (13, 5))
EDGE = len(INTERIOR)
NCHUNK = EDGE + 1


@functools.cache
def tables():
    b = np.arange(LANE)
    fwd, back = [], []
    for r in range(1, 5):
        angle = 2.0 * np.pi * ((b[:, None] * (9 * b[None, :] + r)) % LON) / LON
        mr, mi = np.cos(angle), -np.sin(angle)
        w = np.block([[mr, mi], [-mi, mr]])
        fwd.append(w)
        back.append(w.T * (2.0 / LON))
    angle = 2.0 * np.pi * ((b[:, None] * b[None, :]) % LANE) / LANE
    w0 = np.concatenate([np.cos(angle[:, :65]), np.sin(angle[:, 1:64])], axis=1)
    weight = np.full((LANE,), 2.0)
    weight[0] = weight[64] = 1.0
    b0 = (w0 * weight[None, :]).T / LON
    wf = np.stack(fwd).astype(np.float32)
    wb = np.stack(back).astype(np.float32)
    wz = np.stack([w0, b0]).astype(np.float32)
    sines = np.zeros((8, LANE))
    freq0 = np.concatenate([np.arange(65), np.arange(1, 64)]) * 9
    sines[0] = np.sin(np.pi * freq0 / LON) ** 2 * CUT
    for r in range(1, 5):
        sines[r] = np.sin(np.pi * (9 * b + r) / LON) ** 2 * CUT
    lat = (np.arange(NLAT * ROWS, dtype=np.float32) + np.float32(0.5)) * np.float32(
        math.pi / (NLAT * ROWS)
    ) - np.float32(0.5 * math.pi)
    csq = np.cos(lat.astype(np.float64)).astype(np.float32) ** 2
    csq = np.broadcast_to(csq.reshape(NLAT, ROWS, 1), (NLAT, ROWS, LANE)).astype(np.float32)
    return wf, wb, wz, sines.astype(np.float32), np.ascontiguousarray(csq)


def east_west(x):
    return pltpu.roll(x, LON - 1, 1) - pltpu.roll(x, 1, 1)


def first_kernel(
    u_hbm, v_hbm, t_hbm, p_hbm, a_hbm, b_hbm, terr_hbm, csq_hbm, sin_hbm, wf_hbm, wb_hbm, wz_hbm,
    height, east, north, t_out, p_out, a_out, b_out, geo_off,
    fields, terr, csq, sines, wf32, wb32, wz32, wf, wb, wz,
    cum, logmid, halo_t, halo_p, damp, pair_t, pair_c,
    s_own, s_pair, s_chip, s_recv, pre, pre_pair,
    d_own, d_pair, d_chip, d_recv, geo_pair,
    edge_s, edge_d, edge_h, both_chips,
    y4, y1, z4, z1,
    ready, load_sem, halo_s, halo_r, out_s, out_r, both_s, both_r,
    bp_s, bp_r, bz_s, bz_r, bq_s, bq_r, be_s, be_r,
    cz_s, cz_r, cq_s, cq_r, ce_s, ce_r,
    ez_s, ez_r, dz_s, dz_r, hz_s, hz_r,
):
    la, le = lax.axis_index("lat"), lax.axis_index("lev")
    chip, core = le // 2, le % 2
    other = 1 - core
    up, down = (la + 1) % NLAT, (la + NLAT - 1) % NLAT
    pair_dev = (la, chip * 2 + other)
    side_lat = (la + NLAT - 1 + 2 * core) % NLAT
    cross_dev = (side_lat, chip * 2 + other)
    side_dev = (side_lat, le)
    has_up, has_down = la < NLAT - 1, la > 0
    has_side = jnp.where(core == 0, la, NLAT - 1 - la) > 0
    core_f = core.astype(F32)
    other_f = other.astype(F32)

    def remote(src, dst, send, recv, dev):
        return pltpu.make_async_remote_copy(
            src_ref=src, dst_ref=dst, send_sem=send, recv_sem=recv, device_id=dev, device_id_type=MESH
        )

    ins = (u_hbm, v_hbm, t_hbm, p_hbm, a_hbm, b_hbm)
    load = [
        pltpu.make_async_copy(ins[f], fields.at[f, pl.ds(1, ROWS)], load_sem.at[f]) for f in range(6)
    ]
    load += [
        pltpu.make_async_copy(terr_hbm, terr, load_sem.at[6]),
        pltpu.make_async_copy(csq_hbm.at[la], csq, load_sem.at[7]),
        pltpu.make_async_copy(sin_hbm, sines, load_sem.at[8]),
        pltpu.make_async_copy(wf_hbm, wf32, load_sem.at[9]),
        pltpu.make_async_copy(wb_hbm, wb32, load_sem.at[10]),
        pltpu.make_async_copy(wz_hbm, wz32, load_sem.at[11]),
    ]

    barrier = pltpu.get_barrier_semaphore()
    upper = chip < CHIPS // 2
    others = [(chip + d) % CHIPS for d in range(1, CHIPS)]
    starts, ends = la == NLAT // 2, la == NLAT // 2 - 1
    to_up = [(has_up, (up, le)), (has_up & (core == 1), cross_dev)]
    to_down = [(has_down, (down, le)), (has_down & (core == 0), cross_dev)]
    far_up = [(has_up & (c > chip), (up, c * 2)) for c in others]
    far_down = [(has_down & (c > chip), (down, c * 2 + 1)) for c in others]
    n_up = has_up.astype(jnp.int32) + jnp.where(has_up & (core == 1), 1 + 2 * chip, 0)
    n_down = has_down.astype(jnp.int32) + jnp.where(has_down & (core == 0), 1 + 2 * chip, 0)
    greet = [(la >= 0, pair_dev)] + to_down + far_down + [(there & ~ends, dev) for there, dev in to_up + far_up]
    for c in others:
        inside = upper | (c >= CHIPS // 2)
        greet += [(inside, (la, c * 2 + core)), (inside, (la, c * 2 + other))]
    for there, dev in greet:

        @pl.when(there)
        def _():
            pl.semaphore_signal(barrier, inc=1, device_id=dev, device_id_type=MESH)

    for f in (3, 0, 1, 2):
        load[f].start()

    halo = {}
    for f in (2, 3, 0, 1, 4, 5):
        halo[f, 0] = remote(
            ins[f].at[ROWS - 1], fields.at[f, 0], halo_s.at[f, 0], halo_r.at[f, 0], (up, le)
        )
        halo[f, 1] = remote(
            ins[f].at[0], fields.at[f, ROWS + 1], halo_s.at[f, 1], halo_r.at[f, 1], (down, le)
        )

    seam = starts | ends
    hub = (starts & (core == 0)) | (ends & (core == 1))

    def halo_start(f):
        pl.when(has_up & ~ends)(halo[f, 0].start)
        pl.when(has_down & ~starts)(halo[f, 1].start)

    def enter():
        pl.semaphore_wait(barrier, jnp.where(upper, 3, 7) + n_up + jnp.where(starts, 0, n_down))

        @pl.when(~upper)
        def _():
            for c in range(CHIPS):
                at = ready.at[jnp.where(c // 2 == CHIPS - 1 - chip, 0, 1)]
                pl.semaphore_signal(at, inc=1, device_id=(la, c), device_id_type=MESH)

        for there, dev in to_up:

            @pl.when(there & ends)
            def _():
                pl.semaphore_signal(ready.at[2], inc=1, device_id=dev, device_id_type=MESH)

        for f in (3, 2):
            pl.when(has_up)(halo[f, 0].start)
            pl.when(has_down & ~starts)(halo[f, 1].start)

    def enter_down():
        @pl.when(starts)
        def _():
            pl.semaphore_wait(ready.at[2], 2 - core)
            for f in (3, 2):
                halo[f, 1].start()

    enter()

    row = lax.broadcasted_iota(jnp.int32, (LEVS, LON), 0)

    def halves(x):
        hi = x.astype(BF16)
        return hi, (x - hi.astype(F32)).astype(BF16)

    def run_down(x):
        for s in (1, 2, 4):
            x = x + jnp.where(row >= s, pltpu.roll(x, s, 0), 0.0)
        return x

    def run_up(x):
        for s in (1, 2, 4):
            x = x + jnp.where(row < LEVS - s, pltpu.roll(x, LEVS - s, 0), 0.0)
        return x

    def advected(f, j):
        x = fields[f, j + 1]
        merid = fields[f, j + 2] - fields[f, j]
        return x - COURANT * (fields[0, j + 1] * east_west(x) + fields[1, j + 1] * merid)

    def halo_side(f, side):
        edge, there = (1, has_down) if side == 0 else (ROWS, has_up)
        beyond = (ROWS + 1) * side
        pl.when(there)(halo[f, side].wait_recv)

        @pl.when(~there)
        def _():
            fields[f, beyond] = fields[f, edge]

    def halo_ready(f):
        halo_side(f, 0)
        halo_side(f, 1)

    def column_t(j):
        t_out[j] = advected(2, j)

    def column_p(j):
        p = advected(3, j)
        p_out[j] = p
        c = run_down(p)
        cum[j + 1] = c
        s_own[j] = c[LEVS - 1 :, :]

    def span(k):
        if k == EDGE:
            return (ROWS - 1) * core, (ROWS - 1) * other, 1
        start, n = INTERIOR[k]
        return start + n * core, start + n * other, n

    def chunk_rows(k, body):
        if k == EDGE:
            body(0)
            body(ROWS - 1)
        else:
            start, n = INTERIOR[k]

            @pl.loop(start, start + 2 * n, unroll=2)
            def _(j):
                body(j)

    def scan(k, own, pair, total, recv, result, result_pair, sign, base, zs, zr, qs, qr, es, er, ps=None, pr=None):
        mine, theirs, n = span(k)
        mine_s, theirs_s = pl.ds(mine, n), pl.ds(theirs, n)
        if ps is not None:
            to_pair = remote(own.at[theirs_s], pair.at[theirs_s], ps.at[k], pr.at[k], pair_dev)
            from_pair = remote(own.at[mine_s], pair.at[mine_s], ps.at[k], pr.at[k], pair_dev)
        share = remote(
            result_pair.at[mine_s], result.at[pl.ds(mine + 1, n)], qs.at[k], qr.at[k], pair_dev
        )
        shared = remote(
            result_pair.at[theirs_s], result.at[pl.ds(theirs + 1, n)], qs.at[k], qr.at[k], pair_dev
        )
        hops = {}
        buddy = remote(
            total.at[mine_s], recv.at[0, mine_s], zs.at[k, 0], zr.at[k, 0],
            (la, (chip + 1 - 2 * (chip % 2)) * 2 + core),
        )
        relay = remote(
            both_chips.at[mine_s], recv.at[1, mine_s], zs.at[k, 1], zr.at[k, 1],
            (la, (CHIPS - 1 - chip) * 2 + core),
        )
        for d in (3, 2, 1):
            hops[d] = remote(
                total.at[mine_s], recv.at[d - 1, mine_s], zs.at[k, d - 1], zr.at[k, d - 1],
                (la, ((chip + CHIPS + sign * d) % CHIPS) * 2 + core),
            )
        if sign > 0:
            sends = {d: chip + d < CHIPS for d in hops}
            gets = {d: chip >= d for d in hops}
        else:
            sends = {d: chip >= d for d in hops}
            gets = {d: chip + d < CHIPS for d in hops}
        edges = []
        if k == EDGE:
            direct = {
                (d, w): remote(
                    own.at[(ROWS - 1) * w], edge_s.at[d - 1, core], ez_s.at[d - 1, w], ez_r.at[d - 1, core],
                    (la, ((chip + d) % CHIPS) * 2 + w),
                )
                for d in (1, 2, 3)
                for w in range(2)
            }
            slot = (ROWS + 1) * other
            edges = [
                remote(result.at[mine + 1], result.at[slot], es.at[0], er.at[other], side_dev),
                remote(result_pair.at[mine], result.at[slot], es.at[1], er.at[other], cross_dev),
            ]

        def begin():
            to_pair.start()

        def middle(row=None):
            if k == EDGE:
                for (d, w), c in direct.items():
                    if w == row:
                        pl.when(sends[d])(c.start)
                return
            if ps is not None:
                from_pair.wait_recv()
            total[mine_s] = own[mine_s] + pair[mine_s]
            if sign > 0:
                pl.when(chip < CHIPS - 1)(buddy.start)
            else:
                for d in hops:
                    pl.when(sends[d])(hops[d].start)

        def across():
            buddy.wait_recv()
            both_chips[mine_s] = total[mine_s] + recv[0, mine_s]
            relay.start()

        def end():
            acc = base(mine, n)
            result[pl.ds(mine + 1, n)] = acc
            if k == EDGE:
                from_pair.wait_recv()
            if sign > 0 and k != EDGE:

                @pl.when(chip == CHIPS - 1)
                def _():
                    buddy.wait_recv()

                @pl.when(chip % 2 == 1)
                def _():
                    result[pl.ds(mine + 1, n)] = result[pl.ds(mine + 1, n)] + recv[0, mine_s]

                @pl.when(~upper)
                def _():
                    relay.wait_recv()
                    result[pl.ds(mine + 1, n)] = result[pl.ds(mine + 1, n)] + recv[1, mine_s]

            for d in hops if sign < 0 or k == EDGE else ():

                @pl.when(gets[d])
                def _():
                    if k == EDGE:
                        for w in range(2):
                            remote(
                                edge_s.at[d - 1, w], edge_s.at[d - 1, w], ez_s.at[d - 1, w], ez_r.at[d - 1, w], pair_dev
                            ).wait_recv()
                        result[mine + 1] = result[mine + 1] + (edge_s[d - 1, 0] + edge_s[d - 1, 1])
                        return
                    hops[d].wait_recv()
                    result[pl.ds(mine + 1, n)] = result[pl.ds(mine + 1, n)] + recv[d - 1, mine_s]

            acc = result[pl.ds(mine + 1, n)]
            mine_f, pair_f = (core_f, other_f) if sign > 0 else (other_f, core_f)
            result_pair[mine_s] = acc + pair_f * own[mine_s]
            share.start()
            result[pl.ds(mine + 1, n)] = acc + mine_f * pair[mine_s]
            for e in edges:
                pl.when(has_side)(e.start)

        def finish():
            shared.wait_recv()

        def edge_ready():
            for side, there in ((0, has_down), (1, has_up)):
                slot = (ROWS + 1) * side
                c = remote(result.at[slot], result.at[slot], es.at[0], er.at[side], side_dev)
                pl.when(there)(c.wait_recv)

        def drain():
            if ps is not None:
                to_pair.wait_send()
            share.wait_send()
            if k == EDGE:
                for (d, _), c in direct.items():
                    pl.when(sends[d])(c.wait_send)
            elif sign > 0:
                pl.when(chip < CHIPS - 1)(buddy.wait_send)
                pl.when(upper)(relay.wait_send)
            else:
                for d in hops:
                    pl.when(sends[d])(hops[d].wait_send)
            for e in edges:
                pl.when(has_side)(e.wait_send)

        return begin, middle, end, finish, edge_ready, drain, across

    def base_top(mine, n):
        return jnp.full((n, 1, LON), TOP, F32)

    def base_terrain(mine, n):
        return jnp.stack([terr[pl.ds(mine + i, 1), :] for i in range(n)], 0)

    top = [
        scan(
            k, s_own, s_pair, s_chip, s_recv, pre, pre_pair, 1, base_top,
            bz_s, bz_r, bq_s, bq_r, be_s, be_r, bp_s, bp_r,
        )
        for k in range(NCHUNK)
    ]
    bottom = [
        scan(
            k, d_own, d_pair, d_chip, d_recv, geo_off, geo_pair, -1, base_terrain,
            cz_s, cz_r, cq_s, cq_r, ce_s, ce_r,
        )
        for k in range(EDGE)
    ]

    edge_row = (ROWS - 1) * core
    edge_sends = []
    for d in (3, 2, 1):
        above = chip + CHIPS - d
        for tc in range(2):
            edge_sends.append((
                has_side & (chip >= d),
                remote(
                    d_chip.at[edge_row], edge_h.at[other, d - 1], hz_s.at[d - 1, tc], hz_r.at[other, d - 1],
                    (side_lat, (above % CHIPS) * 2 + tc),
                ),
            ))
            edge_sends.append((
                chip >= d,
                remote(
                    d_chip.at[edge_row], edge_d.at[core, d - 1], dz_s.at[d - 1, tc], dz_r.at[core, d - 1],
                    (la, (above % CHIPS) * 2 + tc),
                ),
            ))
    edge_slot = (ROWS + 1) * other
    edge_sends += [
        (has_side, remote(geo_pair.at[edge_row], geo_off.at[edge_slot], ce_s.at[0], ce_r.at[other], side_dev)),
        (has_side, remote(geo_pair.at[(ROWS - 1) * other], geo_off.at[edge_slot], ce_s.at[1], ce_r.at[other], cross_dev)),
    ]
    last = ROWS - 1
    to_upper = remote(d_own.at[last], d_pair.at[last], cq_s.at[EDGE], cq_r.at[EDGE], pair_dev)

    def edge_depths():
        own, pair = d_own[edge_row], d_pair[edge_row]
        d_chip[edge_row] = own + pair
        ground = terr[pl.ds(edge_row, 1), :]
        geo_pair[0] = ground + jnp.where(core == 0, pair, own)
        geo_pair[ROWS - 1] = ground
        for there, c in edge_sends:
            pl.when(there)(c.start)
        pl.when(core == 1)(to_upper.start)

    def edge_offsets():
        for w in range(2):
            r = last * w
            geo_off[r + 1] = terr[pl.ds(r, 1), :]

        @pl.when(core == 0)
        def _():
            to_upper.wait_recv()
            for w in range(2):
                geo_off[last * w + 1] = geo_off[last * w + 1] + d_pair[last * w]

        for side, there in ((0, has_down), (1, has_up)):
            slot = (ROWS + 1) * side

            @pl.when(there)
            def _():
                remote(geo_off.at[slot], geo_off.at[slot], ce_s.at[0], ce_r.at[side], side_dev).wait_recv()

        for d in (1, 2, 3):
            for w in range(2):

                @pl.when(chip + d < CHIPS)
                def _():
                    slot = edge_d.at[w, d - 1]
                    remote(slot, slot, dz_s.at[0, 0], dz_r.at[w, d - 1], pair_dev).wait_recv()
                    geo_off[last * w + 1] = geo_off[last * w + 1] + edge_d[w, d - 1]

            for side, there in ((0, has_down), (1, has_up)):

                @pl.when(there & (chip + d < CHIPS))
                def _():
                    slot = edge_h.at[side, d - 1]
                    remote(slot, slot, dz_s.at[0, 0], hz_r.at[side, d - 1], pair_dev).wait_recv()
                    i = (ROWS + 1) * side
                    geo_off[i] = geo_off[i] + edge_h[side, d - 1]

    def edge_drain():
        for there, c in edge_sends:
            pl.when(there)(c.wait_send)
        pl.when(core == 1)(to_upper.wait_send)

    def thickness(i, temp):
        base = pre[i]
        lp = jnp.log(base + cum[i])
        above = jnp.where(row == 0, jnp.log(base), pltpu.roll(lp, 1, 0))
        depth = GAS * temp * (lp - above)
        below = run_up(depth)
        height[i] = below - 0.5 * depth
        logmid[i] = 0.5 * (lp + above)
        return below[:1, :]

    def thickness_row(j):
        d_own[j] = thickness(j + 1, t_out[j])

    def gradient_row(j):
        pull = GAS * t_out[j]
        east[j] = east[j] - GRAD * (east_west(height[j + 1]) + pull * east_west(logmid[j + 1]))
        north[j] = north[j] - GRAD * (
            (height[j + 2] - height[j]) + pull * (logmid[j + 2] - logmid[j])
        )

    def both(k):
        _, theirs, n = span(k)
        at = pl.ds(theirs, n)
        return (
            remote(cum.at[pl.ds(theirs + 1, n)], pair_c.at[at], both_s.at[k, 0], both_r.at[k, 0], pair_dev),
            remote(t_out.at[at], pair_t.at[at], both_s.at[k, 1], both_r.at[k, 1], pair_dev),
        )

    def pair_row(j):
        base = pre_pair[j]
        lp = jnp.log(base + pair_c[j])
        above = jnp.where(row == 0, jnp.log(base), pltpu.roll(lp, 1, 0))
        depth = GAS * pair_t[j] * (lp - above)
        d_pair[j] = jnp.sum(depth, axis=0, keepdims=True)

    def mine_rows(k):
        mine, _, n = span(k)

        @pl.loop(0, n, unroll=n)
        def _(i):
            thickness_row(mine + i)
            pair_row(mine + i)

    def their_rows(k):
        _, theirs, n = span(k)

        @pl.loop(0, n, unroll=n)
        def _(i):
            thickness_row(theirs + i)

    def tracers(j):
        a_out[j] = advected(4, j)
        b_out[j] = advected(5, j)

    def inner_tracers():
        @pl.loop(1, ROWS - 1, unroll=2)
        def _(j):
            tracers(j)

    for f in (3, 0, 1):
        load[f].wait()
    for f in (4, 5, 6, 7, 8, 9, 10, 11):
        load[f].start()
    for k in range(EDGE):
        chunk_rows(k, column_p)
        top[k][0]()
    load[2].wait()
    pairs = [both(k) for k in range(NCHUNK)]
    for k in range(EDGE):
        chunk_rows(k, column_t)
        for c in pairs[k]:
            c.start()
    for k in range(EDGE):
        top[k][1]()
    halo_start(0)
    halo_start(1)

    @pl.when(upper)
    def _():
        pl.semaphore_wait(ready.at[0], 2)
        for k in range(EDGE):
            top[k][6]()

    out_copies = []
    for n, (src, dst) in enumerate(((t_out, halo_t), (p_out, halo_p))):
        out_copies.append(
            remote(src.at[ROWS - 1], dst.at[0], out_s.at[n, 0], out_r.at[n, 0], (up, le))
        )
        out_copies.append(remote(src.at[0], dst.at[1], out_s.at[n, 1], out_r.at[n, 1], (down, le)))
    ways = (has_up, has_down)

    def edge_rows(w):
        r = (ROWS - 1) * w
        halo_side(3, w)
        column_p(r)
        pl.when(core != w)(top[EDGE][0])
        top[EDGE][1](w)
        halo_side(2, w)
        column_t(r)
        for c in pairs[EDGE]:
            pl.when(core != w)(c.start)
        for n, c in enumerate(out_copies):
            if n % 2 != w:
                pl.when(ways[n % 2])(c.start)

    def edge_sums():
        top[EDGE][2]()
        for c in pairs[EDGE]:
            c.wait_recv()
        mine_rows(EDGE)
        edge_depths()

    def seam_rows():
        pl.when(starts)(functools.partial(edge_rows, 0))
        pl.when(ends)(functools.partial(edge_rows, 1))

    enter_down()

    @pl.when(upper)
    def _():
        pl.semaphore_wait(ready.at[1], 2)

    pl.when(~starts)(functools.partial(edge_rows, 0))
    pl.when(~ends)(functools.partial(edge_rows, 1))
    for f in (4, 5):
        halo_start(f)

    for n in (4, 5, 6, 7, 8, 9, 10, 11):
        load[n].wait()

    def prepare():
        @pl.loop(0, ROWS, unroll=4)
        def _(j):
            c = csq[pl.ds(j, 1), :]
            at = pl.ds(pl.multiple_of(j * LEVS, LEVS), LEVS)
            for r in range(5):
                d = c / jnp.maximum(c, sines[r : r + 1, :])
                damp[r, at, :] = jnp.broadcast_to(d, (LEVS, LANE))

        for full, parts in ((wf32, wf), (wb32, wb)):

            @pl.loop(0, 4)
            def _(r):
                for i in range(0, 256, 64):
                    hi, lo = halves(full[r, i : i + 64, :])
                    parts[r, i : i + 64, :] = hi
                    parts[r, 256 + i : 320 + i, :] = hi
                    parts[r, 512 + i : 576 + i, :] = lo

        for n in range(2):
            hi, lo = halves(wz32[n])
            wz[n, :LANE, :], wz[n, LANE : 2 * LANE, :], wz[n, 2 * LANE :, :] = hi, hi, lo

    cos9 = [math.cos(2.0 * math.pi * i / 9) for i in range(9)]
    sin9 = [math.sin(2.0 * math.pi * i / 9) for i in range(9)]

    def forward_nine(i):
        for f in range(2):
            at = pl.ds(pl.multiple_of(f * ROWS * LEVS + i * 16, 16), 16)
            x = jnp.concatenate([advected(f, 2 * i), advected(f, 2 * i + 1)], axis=0)
            xs = [x[:, LANE * a : LANE * (a + 1)] for a in range(9)]
            even = [xs[a] + xs[9 - a] for a in range(1, 5)]
            odd = [xs[a] - xs[9 - a] for a in range(1, 5)]
            hi, lo = halves(xs[0] + ((even[0] + even[1]) + (even[2] + even[3])))
            y1[at, :LANE], y1[at, LANE : 2 * LANE], y1[at, 2 * LANE :] = hi, lo, hi
            for r in range(1, 5):
                re, im = xs[0], None
                for a in range(1, 5):
                    re = re + cos9[(a * r) % 9] * even[a - 1]
                    term = -sin9[(a * r) % 9] * odd[a - 1]
                    im = term if im is None else im + term
                for part, y in ((0, re), (1, im)):
                    hi, lo = halves(y)
                    for place, value in ((0, hi), (2, lo), (4, hi)):
                        place = (place + part) * LANE
                        y4[r - 1, at, place : place + LANE] = value

    def triple(x):
        hi, lo = halves(x)
        return jnp.concatenate([hi, lo, hi], axis=1)

    def mm(x, w):
        return jnp.dot(x, w, preferred_element_type=F32)

    def spectrum(r):
        d = damp[r + 1]
        d = jnp.concatenate([d, d], axis=1)
        d = jnp.concatenate([d, d], axis=0)
        z4[r] = mm(triple(mm(y4[r], wf[r]) * d), wb[r])

    def spectrum_zero():
        d = jnp.concatenate([damp[0], damp[0]], axis=0)
        z1[...] = mm(triple(mm(y1[...], wz[0]) * d), wz[1])

    def backward_nine(i):
        for f, dst in ((0, east), (1, north)):
            at = pl.ds(pl.multiple_of(f * ROWS * LEVS + i * 16, 16), 16)
            z0 = z1[at, :]
            re = [z4[r, at, :LANE] for r in range(4)]
            im = [z4[r, at, LANE:] for r in range(4)]
            outs = [None] * 9
            outs[0] = z0 + ((re[0] + re[1]) + (re[2] + re[3]))
            for a in range(1, 5):
                even, odd = z0, None
                for r in range(1, 5):
                    even = even + cos9[(a * r) % 9] * re[r - 1]
                    term = sin9[(a * r) % 9] * im[r - 1]
                    odd = term if odd is None else odd + term
                outs[a], outs[9 - a] = even - odd, even + odd
            for a in range(9):
                dst[2 * i, :, LANE * a : LANE * (a + 1)] = outs[a][:LEVS]
                dst[2 * i + 1, :, LANE * a : LANE * (a + 1)] = outs[a][LEVS:]

    polar = (la < POLAR) | (la >= NLAT - POLAR)

    def forward():
        halo_ready(0)
        halo_ready(1)

        @pl.loop(0, ROWS // 2, unroll=2)
        def _(i):
            forward_nine(i)

    inner_tracers()
    pl.when(polar)(prepare)
    pl.when(polar & upper)(forward)

    for k in range(EDGE):
        top[k][2]()
        for c in pairs[k]:
            c.wait_recv()
        mine_rows(k)
        bottom[k][1]()
    pl.when(hub)(seam_rows)
    edge_sums()
    pl.when(seam & ~hub)(seam_rows)
    for f in (0, 1, 4, 5):
        pl.when(ends)(halo[f, 0].start)
        pl.when(starts)(halo[f, 1].start)
    for k in range(NCHUNK):
        top[k][3]()
        their_rows(k)
    pl.when(polar & ~upper)(forward)

    @pl.when(polar)
    def _():
        spectrum_zero()
        pl.loop(0, 4)(spectrum)

        @pl.loop(0, ROWS // 2, unroll=2)
        def _(i):
            backward_nine(i)

    @pl.when(~polar)
    def _():
        @pl.loop(1, ROWS - 1, unroll=2)
        def _(j):
            east[j] = advected(0, j)
            north[j] = advected(1, j)

        halo_ready(0)
        halo_ready(1)
        for j in (0, ROWS - 1):
            east[j] = advected(0, j)
            north[j] = advected(1, j)

    @pl.loop(1, ROWS - 1, unroll=2)
    def _(j):
        gradient_row(j)

    halo_ready(4)
    halo_ready(5)
    tracers(0)
    tracers(ROWS - 1)

    for n, c in enumerate(out_copies):
        pl.when(ways[1 - n % 2])(c.wait_recv)
    top[EDGE][4]()
    for side, there in ((0, has_down), (1, has_up)):

        @pl.when(there)
        def _():
            i = (ROWS + 1) * side
            cum[i] = run_down(halo_p[side])
            thickness(i, halo_t[side])

    @pl.when(la == 0)
    def _():
        height[0] = height[1]
        logmid[0] = logmid[1]

    @pl.when(la == NLAT - 1)
    def _():
        height[ROWS + 1] = height[ROWS]
        logmid[ROWS + 1] = logmid[ROWS]

    gradient_row(0)
    gradient_row(ROWS - 1)

    for k in range(EDGE):
        bottom[k][2]()
    edge_offsets()
    for k in range(EDGE):
        bottom[k][3]()

    @pl.when(la == 0)
    def _():
        geo_off[0] = geo_off[1]

    @pl.when(la == NLAT - 1)
    def _():
        geo_off[ROWS + 1] = geo_off[ROWS]

    for k in range(NCHUNK):
        top[k][5]()
    for k in range(EDGE):
        bottom[k][5]()
    edge_drain()
    for pair in pairs:
        for c in pair:
            c.wait_send()
    for (f, side), c in halo.items():
        pl.when(ways[side])(c.wait_send)
    for n, c in enumerate(out_copies):
        pl.when(ways[n % 2])(c.wait_send)


def second_kernel(
    height, east, north, t_out, p_out, a_out, b_out, geo_off,
    east_hbm, north_hbm, t_hbm, p_hbm, a_hbm, b_hbm, geo_hbm,
    east_buf, north_buf, geo_buf, sem,
):
    copies = [
        pltpu.make_async_copy(src, dst, sem.at[n])
        for n, (src, dst) in enumerate(((t_out, t_hbm), (p_out, p_hbm), (a_out, a_hbm), (b_out, b_hbm)))
    ]
    for c in copies:
        c.start()
    part = 8
    for q in range(ROWS // part):

        @pl.loop(part * q, part * (q + 1), unroll=4)
        def _(j):
            off = geo_off[j + 1]
            geo_buf[j] = height[j + 1] + off
            east_buf[j] = east[j] - GRAD * east_west(off)
            north_buf[j] = north[j] - GRAD * (geo_off[j + 2] - geo_off[j])

        for m, (src, dst) in enumerate(((east_buf, east_hbm), (north_buf, north_hbm), (geo_buf, geo_hbm))):
            rows = pl.ds(part * q, part)
            c = pltpu.make_async_copy(src.at[rows], dst.at[rows], sem.at[4 + 3 * q + m])
            c.start()
            copies.append(c)
    for c in copies:
        c.wait()


def shards(u, v, t, p, a, b, terrain):
    wf, wb, wz, sines, csq = (jnp.asarray(x) for x in tables())
    ins = [u, v, t, p, a, b, terrain, csq, sines, wf, wb, wz]
    ins = [pltpu.with_memory_space_constraint(x, pltpu.HBM) for x in ins]
    full = (ROWS, LEVS, LON)
    wide = (ROWS + 2, LEVS, LON)
    line = (ROWS, 1, LON)
    line_wide = (ROWS + 2, 1, LON)
    dma = pltpu.SemaphoreType.DMA
    scan_sems = [
        dma((NCHUNK,)), dma((NCHUNK,)), dma((NCHUNK, 3)), dma((NCHUNK, 3)),
        dma((NCHUNK,)), dma((NCHUNK,)), dma((2,)), dma((2,)),
    ]
    mids = pl.pallas_call(
        first_kernel,
        out_shape=[pltpu.VMEM(wide, F32)] + [pltpu.VMEM(full, F32)] * 6 + [pltpu.VMEM(line_wide, F32)],
        in_specs=[pl.BlockSpec(memory_space=pltpu.HBM)] * len(ins),
        out_specs=[pl.BlockSpec(memory_space=pltpu.VMEM)] * 8,
        scratch_shapes=[
            pltpu.VMEM((6,) + wide, F32),
            pltpu.VMEM((ROWS, LON), F32),
            pltpu.VMEM((ROWS, LANE), F32),
            pltpu.VMEM((8, LANE), F32),
            pltpu.VMEM((4, 256, 256), F32),
            pltpu.VMEM((4, 256, 256), F32),
            pltpu.VMEM((2, LANE, LANE), F32),
            pltpu.VMEM((4, 3 * 256, 256), BF16),
            pltpu.VMEM((4, 3 * 256, 256), BF16),
            pltpu.VMEM((2, 3 * LANE, LANE), BF16),
            pltpu.VMEM(wide, F32),
            pltpu.VMEM(wide, F32),
            pltpu.VMEM((2, LEVS, LON), F32),
            pltpu.VMEM((2, LEVS, LON), F32),
            pltpu.VMEM((5, ROWS * LEVS, LANE), F32),
            pltpu.VMEM(full, F32),
            pltpu.VMEM(full, F32),
            pltpu.VMEM(line, F32),
            pltpu.VMEM(line, F32),
            pltpu.VMEM(line, F32),
            pltpu.VMEM((3,) + line, F32),
            pltpu.VMEM(line_wide, F32),
            pltpu.VMEM(line, F32),
            pltpu.VMEM(line, F32),
            pltpu.VMEM(line, F32),
            pltpu.VMEM(line, F32),
            pltpu.VMEM((3,) + line, F32),
            pltpu.VMEM(line, F32),
            pltpu.VMEM((3, 2, 1, LON), F32),
            pltpu.VMEM((2, 3, 1, LON), F32),
            pltpu.VMEM((2, 3, 1, LON), F32),
            pltpu.VMEM(line, F32),
            pltpu.VMEM((4, 2 * ROWS * LEVS, 6 * LANE), BF16),
            pltpu.VMEM((2 * ROWS * LEVS, 3 * LANE), BF16),
            pltpu.VMEM((4, 2 * ROWS * LEVS, 2 * LANE), F32),
            pltpu.VMEM((2 * ROWS * LEVS, LANE), F32),
            pltpu.SemaphoreType.REGULAR((3,)), dma((12,)), dma((6, 2)), dma((6, 2)), dma((2, 2)), dma((2, 2)),
            dma((NCHUNK, 2)), dma((NCHUNK, 2)),
        ]
        + scan_sems
        + scan_sems[2:]
        + [dma((3, 2)), dma((3, 2)), dma((3, 2)), dma((2, 3)), dma((3, 2)), dma((2, 3))],
        compiler_params=pltpu.CompilerParams(
            collective_id=0, has_side_effects=True, vmem_limit_bytes=40 << 20
        ),
    )(*ins)
    outs = pl.pallas_call(
        second_kernel,
        out_shape=[jax.ShapeDtypeStruct(full, F32)] * 7,
        in_specs=[pl.BlockSpec(memory_space=pltpu.VMEM)] * 8,
        out_specs=[pl.BlockSpec(memory_space=pltpu.HBM)] * 7,
        scratch_shapes=[pltpu.VMEM(full, F32)] * 3 + [dma((13,))],
        compiler_params=pltpu.CompilerParams(vmem_limit_bytes=20 << 20),
    )(*mids)
    return tuple(outs)


def solution(mesh):
    field = P("lat", "lev", None)
    return jax.shard_map(
        shards,
        mesh=mesh,
        in_specs=(field,) * 6 + (P("lat", None),),
        out_specs=(field,) * 7,
        check_vma=False,
    )
```

```python
import functools
import math

import jax
import jax.numpy as jnp
import numpy as np
from jax import lax
from jax.experimental import pallas as pl
from jax.experimental.pallas import tpu as pltpu
from jax.sharding import PartitionSpec as P

MESH = pl.DeviceIdType.MESH
F32 = jnp.float32
BF16 = jnp.bfloat16

ROWS, LEVS, LON = 24, 8, 1152
NLAT = 32
CHIPS = 4
LANE = 128
COURANT = 0.1
GRAD = 0.1
GAS = 0.3
TOP = 1.0
CUT = 0.5

POLAR = sum(
    math.cos(((ROWS * band + ROWS - 0.5) / (NLAT * ROWS) - 0.5) * math.pi) ** 2 < CUT
    or math.cos(((ROWS * band + 0.5) / (NLAT * ROWS) - 0.5) * math.pi) ** 2 < CUT
    for band in range(NLAT // 2)
)
INTERIOR = ((1, 6), (13, 5))
EDGE = len(INTERIOR)
NCHUNK = EDGE + 1


@functools.cache
def tables():
    b = np.arange(LANE)
    fwd, back = [], []
    for r in range(1, 5):
        angle = 2.0 * np.pi * ((b[:, None] * (9 * b[None, :] + r)) % LON) / LON
        mr, mi = np.cos(angle), -np.sin(angle)
        w = np.block([[mr, mi], [-mi, mr]])
        fwd.append(w)
        back.append(w.T * (2.0 / LON))
    angle = 2.0 * np.pi * ((b[:, None] * b[None, :]) % LANE) / LANE
    w0 = np.concatenate([np.cos(angle[:, :65]), np.sin(angle[:, 1:64])], axis=1)
    weight = np.full((LANE,), 2.0)
    weight[0] = weight[64] = 1.0
    b0 = (w0 * weight[None, :]).T / LON
    wf = np.stack(fwd).astype(np.float32)
    wb = np.stack(back).astype(np.float32)
    wz = np.stack([w0, b0]).astype(np.float32)
    sines = np.zeros((8, LANE))
    freq0 = np.concatenate([np.arange(65), np.arange(1, 64)]) * 9
    sines[0] = np.sin(np.pi * freq0 / LON) ** 2 * CUT
    for r in range(1, 5):
        sines[r] = np.sin(np.pi * (9 * b + r) / LON) ** 2 * CUT
    lat = (np.arange(NLAT * ROWS, dtype=np.float32) + np.float32(0.5)) * np.float32(
        math.pi / (NLAT * ROWS)
    ) - np.float32(0.5 * math.pi)
    csq = np.cos(lat.astype(np.float64)).astype(np.float32) ** 2
    csq = np.broadcast_to(csq.reshape(NLAT, ROWS, 1), (NLAT, ROWS, LANE)).astype(np.float32)
    return wf, wb, wz, sines.astype(np.float32), np.ascontiguousarray(csq)


def east_west(x):
    return pltpu.roll(x, LON - 1, 1) - pltpu.roll(x, 1, 1)


def first_kernel(
    u_hbm, v_hbm, t_hbm, p_hbm, a_hbm, b_hbm, terr_hbm, csq_hbm, sin_hbm, wf_hbm, wb_hbm, wz_hbm,
    height, east, north, t_out, p_out, a_out, b_out, geo_off,
    fields, terr, csq, sines, wf32, wb32, wz32, wf, wb, wz,
    cum, logmid, halo_t, halo_p, damp, pair_t, pair_c,
    s_own, s_pair, s_chip, s_recv, pre, pre_pair,
    d_own, d_pair, d_chip, d_recv, geo_pair,
    edge_s, edge_d, edge_h, both_chips,
    y4, y1, z4, z1,
    ready, load_sem, halo_s, halo_r, out_s, out_r, both_s, both_r,
    bp_s, bp_r, bz_s, bz_r, bq_s, bq_r, be_s, be_r,
    cz_s, cz_r, cq_s, cq_r, ce_s, ce_r,
    ez_s, ez_r, dz_s, dz_r, hz_s, hz_r,
):
    la, le = lax.axis_index("lat"), lax.axis_index("lev")
    chip, core = le // 2, le % 2
    other = 1 - core
    up, down = (la + 1) % NLAT, (la + NLAT - 1) % NLAT
    pair_dev = (la, chip * 2 + other)
    side_lat = (la + NLAT - 1 + 2 * core) % NLAT
    cross_dev = (side_lat, chip * 2 + other)
    side_dev = (side_lat, le)
    has_up, has_down = la < NLAT - 1, la > 0
    has_side = jnp.where(core == 0, la, NLAT - 1 - la) > 0
    core_f = core.astype(F32)
    other_f = other.astype(F32)

    def remote(src, dst, send, recv, dev):
        return pltpu.make_async_remote_copy(
            src_ref=src, dst_ref=dst, send_sem=send, recv_sem=recv, device_id=dev, device_id_type=MESH
        )

    ins = (u_hbm, v_hbm, t_hbm, p_hbm, a_hbm, b_hbm)
    load = [
        pltpu.make_async_copy(ins[f], fields.at[f, pl.ds(1, ROWS)], load_sem.at[f]) for f in range(6)
    ]
    load += [
        pltpu.make_async_copy(terr_hbm, terr, load_sem.at[6]),
        pltpu.make_async_copy(csq_hbm.at[la], csq, load_sem.at[7]),
        pltpu.make_async_copy(sin_hbm, sines, load_sem.at[8]),
        pltpu.make_async_copy(wf_hbm, wf32, load_sem.at[9]),
        pltpu.make_async_copy(wb_hbm, wb32, load_sem.at[10]),
        pltpu.make_async_copy(wz_hbm, wz32, load_sem.at[11]),
    ]

    barrier = pltpu.get_barrier_semaphore()
    upper = chip < CHIPS // 2
    others = [(chip + d) % CHIPS for d in range(1, CHIPS)]
    starts, ends = la == NLAT // 2, la == NLAT // 2 - 1
    to_up = [(has_up, (up, le)), (has_up & (core == 1), cross_dev)]
    to_down = [(has_down, (down, le)), (has_down & (core == 0), cross_dev)]
    far_up = [(has_up & (c > chip), (up, c * 2)) for c in others]
    far_down = [(has_down & (c > chip), (down, c * 2 + 1)) for c in others]
    n_up = has_up.astype(jnp.int32) + jnp.where(has_up & (core == 1), 1 + 2 * chip, 0)
    n_down = has_down.astype(jnp.int32) + jnp.where(has_down & (core == 0), 1 + 2 * chip, 0)
    greet = [(la >= 0, pair_dev)] + to_down + far_down + to_up + far_up
    for c in others:
        inside = upper | (c >= CHIPS // 2)
        greet += [(inside, (la, c * 2 + core)), (inside, (la, c * 2 + other))]
    for there, dev in greet:

        @pl.when(there)
        def _():
            pl.semaphore_signal(barrier, inc=1, device_id=dev, device_id_type=MESH)

    for f in (3, 0, 1, 2):
        load[f].start()

    halo = {}
    for f in (2, 3, 0, 1, 4, 5):
        halo[f, 0] = remote(
            ins[f].at[ROWS - 1], fields.at[f, 0], halo_s.at[f, 0], halo_r.at[f, 0], (up, le)
        )
        halo[f, 1] = remote(
            ins[f].at[0], fields.at[f, ROWS + 1], halo_s.at[f, 1], halo_r.at[f, 1], (down, le)
        )


    def halo_start(f):
        pl.when(has_up & ~ends)(halo[f, 0].start)
        pl.when(has_down & ~starts)(halo[f, 1].start)

    def enter():
        pl.semaphore_wait(barrier, jnp.where(upper, 3, 7) + n_up + n_down)

        @pl.when(~upper)
        def _():
            for c in range(CHIPS):
                at = ready.at[jnp.where(c // 2 == CHIPS - 1 - chip, 0, 1)]
                pl.semaphore_signal(at, inc=1, device_id=(la, c), device_id_type=MESH)

        for f in (3, 2):
            pl.when(has_up)(halo[f, 0].start)
            pl.when(has_down)(halo[f, 1].start)

    enter()

    row = lax.broadcasted_iota(jnp.int32, (LEVS, LON), 0)

    def halves(x):
        hi = x.astype(BF16)
        return hi, (x - hi.astype(F32)).astype(BF16)

    def run_down(x):
        for s in (1, 2, 4):
            x = x + jnp.where(row >= s, pltpu.roll(x, s, 0), 0.0)
        return x

    def run_up(x):
        for s in (1, 2, 4):
            x = x + jnp.where(row < LEVS - s, pltpu.roll(x, LEVS - s, 0), 0.0)
        return x

    def advected(f, j):
        x = fields[f, j + 1]
        merid = fields[f, j + 2] - fields[f, j]
        return x - COURANT * (fields[0, j + 1] * east_west(x) + fields[1, j + 1] * merid)

    def halo_side(f, side):
        edge, there = (1, has_down) if side == 0 else (ROWS, has_up)
        beyond = (ROWS + 1) * side
        pl.when(there)(halo[f, side].wait_recv)

        @pl.when(~there)
        def _():
            fields[f, beyond] = fields[f, edge]

    def halo_ready(f):
        halo_side(f, 0)
        halo_side(f, 1)

    def column_t(j):
        t_out[j] = advected(2, j)

    def column_p(j):
        p = advected(3, j)
        p_out[j] = p
        c = run_down(p)
        cum[j + 1] = c
        s_own[j] = c[LEVS - 1 :, :]

    def span(k):
        if k == EDGE:
            return (ROWS - 1) * core, (ROWS - 1) * other, 1
        start, n = INTERIOR[k]
        return start + n * core, start + n * other, n

    def chunk_rows(k, body):
        if k == EDGE:
            body(0)
            body(ROWS - 1)
        else:
            start, n = INTERIOR[k]

            @pl.loop(start, start + 2 * n, unroll=n)
            def _(j):
                body(j)

    def scan(k, own, pair, total, recv, result, result_pair, sign, base, zs, zr, qs, qr, es, er, ps=None, pr=None):
        mine, theirs, n = span(k)
        mine_s, theirs_s = pl.ds(mine, n), pl.ds(theirs, n)
        if ps is not None:
            to_pair = remote(own.at[theirs_s], pair.at[theirs_s], ps.at[k], pr.at[k], pair_dev)
            from_pair = remote(own.at[mine_s], pair.at[mine_s], ps.at[k], pr.at[k], pair_dev)
        share = remote(
            result_pair.at[mine_s], result.at[pl.ds(mine + 1, n)], qs.at[k], qr.at[k], pair_dev
        )
        shared = remote(
            result_pair.at[theirs_s], result.at[pl.ds(theirs + 1, n)], qs.at[k], qr.at[k], pair_dev
        )
        hops = {}
        buddy = remote(
            total.at[mine_s], recv.at[0, mine_s], zs.at[k, 0], zr.at[k, 0],
            (la, (chip + 1 - 2 * (chip % 2)) * 2 + core),
        )
        relay = remote(
            both_chips.at[mine_s], recv.at[1, mine_s], zs.at[k, 1], zr.at[k, 1],
            (la, (CHIPS - 1 - chip) * 2 + core),
        )
        for d in (3, 2, 1):
            hops[d] = remote(
                total.at[mine_s], recv.at[d - 1, mine_s], zs.at[k, d - 1], zr.at[k, d - 1],
                (la, ((chip + CHIPS + sign * d) % CHIPS) * 2 + core),
            )
        if sign > 0:
            sends = {d: chip + d < CHIPS for d in hops}
            gets = {d: chip >= d for d in hops}
        else:
            sends = {d: chip >= d for d in hops}
            gets = {d: chip + d < CHIPS for d in hops}
        edges = []
        if k == EDGE:
            direct = {
                (d, w): remote(
                    own.at[(ROWS - 1) * w], edge_s.at[d - 1, core], ez_s.at[d - 1, w], ez_r.at[d - 1, core],
                    (la, ((chip + d) % CHIPS) * 2 + w),
                )
                for d in (1, 2, 3)
                for w in range(2)
            }
            slot = (ROWS + 1) * other
            edges = [
                remote(result.at[mine + 1], result.at[slot], es.at[0], er.at[other], side_dev),
                remote(result_pair.at[mine], result.at[slot], es.at[1], er.at[other], cross_dev),
            ]

        def begin():
            to_pair.start()

        def middle(row=None):
            if k == EDGE:
                for (d, w), c in direct.items():
                    if w == row:
                        pl.when(sends[d])(c.start)
                return
            if ps is not None:
                from_pair.wait_recv()
            total[mine_s] = own[mine_s] + pair[mine_s]
            if sign > 0:
                pl.when(chip < CHIPS - 1)(buddy.start)
            else:
                for d in hops:
                    pl.when(sends[d])(hops[d].start)

        def across():
            buddy.wait_recv()
            both_chips[mine_s] = total[mine_s] + recv[0, mine_s]
            relay.start()

        def end():
            acc = base(mine, n)
            result[pl.ds(mine + 1, n)] = acc
            if k == EDGE:
                from_pair.wait_recv()
            if sign > 0 and k != EDGE:

                @pl.when(chip == CHIPS - 1)
                def _():
                    buddy.wait_recv()

                @pl.when(chip % 2 == 1)
                def _():
                    result[pl.ds(mine + 1, n)] = result[pl.ds(mine + 1, n)] + recv[0, mine_s]

                @pl.when(~upper)
                def _():
                    relay.wait_recv()
                    result[pl.ds(mine + 1, n)] = result[pl.ds(mine + 1, n)] + recv[1, mine_s]

            for d in hops if sign < 0 or k == EDGE else ():

                @pl.when(gets[d])
                def _():
                    if k == EDGE:
                        for w in range(2):
                            remote(
                                edge_s.at[d - 1, w], edge_s.at[d - 1, w], ez_s.at[d - 1, w], ez_r.at[d - 1, w], pair_dev
                            ).wait_recv()
                        result[mine + 1] = result[mine + 1] + (edge_s[d - 1, 0] + edge_s[d - 1, 1])
                        return
                    hops[d].wait_recv()
                    result[pl.ds(mine + 1, n)] = result[pl.ds(mine + 1, n)] + recv[d - 1, mine_s]

            acc = result[pl.ds(mine + 1, n)]
            mine_f, pair_f = (core_f, other_f) if sign > 0 else (other_f, core_f)
            result_pair[mine_s] = acc + pair_f * own[mine_s]
            share.start()
            result[pl.ds(mine + 1, n)] = acc + mine_f * pair[mine_s]
            for e in edges:
                pl.when(has_side)(e.start)

        def finish():
            shared.wait_recv()

        def edge_ready():
            for side, there in ((0, has_down), (1, has_up)):
                slot = (ROWS + 1) * side
                c = remote(result.at[slot], result.at[slot], es.at[0], er.at[side], side_dev)
                pl.when(there)(c.wait_recv)

        def drain():
            if ps is not None:
                to_pair.wait_send()
            share.wait_send()
            if k == EDGE:
                for (d, _), c in direct.items():
                    pl.when(sends[d])(c.wait_send)
            elif sign > 0:
                pl.when(chip < CHIPS - 1)(buddy.wait_send)
                pl.when(upper)(relay.wait_send)
            else:
                for d in hops:
                    pl.when(sends[d])(hops[d].wait_send)
            for e in edges:
                pl.when(has_side)(e.wait_send)

        return begin, middle, end, finish, edge_ready, drain, across

    def base_top(mine, n):
        return jnp.full((n, 1, LON), TOP, F32)

    def base_terrain(mine, n):
        return jnp.stack([terr[pl.ds(mine + i, 1), :] for i in range(n)], 0)

    top = [
        scan(
            k, s_own, s_pair, s_chip, s_recv, pre, pre_pair, 1, base_top,
            bz_s, bz_r, bq_s, bq_r, be_s, be_r, bp_s, bp_r,
        )
        for k in range(NCHUNK)
    ]
    bottom = [
        scan(
            k, d_own, d_pair, d_chip, d_recv, geo_off, geo_pair, -1, base_terrain,
            cz_s, cz_r, cq_s, cq_r, ce_s, ce_r,
        )
        for k in range(EDGE)
    ]

    edge_row = (ROWS - 1) * core
    edge_sends = []
    for d in (3, 2, 1):
        above = chip + CHIPS - d
        for tc in range(2):
            edge_sends.append((
                has_side & (chip >= d),
                remote(
                    d_chip.at[edge_row], edge_h.at[other, d - 1], hz_s.at[d - 1, tc], hz_r.at[other, d - 1],
                    (side_lat, (above % CHIPS) * 2 + tc),
                ),
            ))
            edge_sends.append((
                chip >= d,
                remote(
                    d_chip.at[edge_row], edge_d.at[core, d - 1], dz_s.at[d - 1, tc], dz_r.at[core, d - 1],
                    (la, (above % CHIPS) * 2 + tc),
                ),
            ))
    edge_slot = (ROWS + 1) * other
    edge_sends += [
        (has_side, remote(geo_pair.at[edge_row], geo_off.at[edge_slot], ce_s.at[0], ce_r.at[other], side_dev)),
        (has_side, remote(geo_pair.at[(ROWS - 1) * other], geo_off.at[edge_slot], ce_s.at[1], ce_r.at[other], cross_dev)),
    ]
    last = ROWS - 1
    to_upper = remote(d_own.at[last], d_pair.at[last], cq_s.at[EDGE], cq_r.at[EDGE], pair_dev)

    def edge_depths():
        own, pair = d_own[edge_row], d_pair[edge_row]
        d_chip[edge_row] = own + pair
        ground = terr[pl.ds(edge_row, 1), :]
        geo_pair[0] = ground + jnp.where(core == 0, pair, own)
        geo_pair[ROWS - 1] = ground
        for there, c in edge_sends:
            pl.when(there)(c.start)
        pl.when(core == 1)(to_upper.start)

    def edge_offsets():
        for w in range(2):
            r = last * w
            geo_off[r + 1] = terr[pl.ds(r, 1), :]

        @pl.when(core == 0)
        def _():
            to_upper.wait_recv()
            for w in range(2):
                geo_off[last * w + 1] = geo_off[last * w + 1] + d_pair[last * w]

        for side, there in ((0, has_down), (1, has_up)):
            slot = (ROWS + 1) * side

            @pl.when(there)
            def _():
                remote(geo_off.at[slot], geo_off.at[slot], ce_s.at[0], ce_r.at[side], side_dev).wait_recv()

        for d in (1, 2, 3):
            for w in range(2):

                @pl.when(chip + d < CHIPS)
                def _():
                    slot = edge_d.at[w, d - 1]
                    remote(slot, slot, dz_s.at[0, 0], dz_r.at[w, d - 1], pair_dev).wait_recv()
                    geo_off[last * w + 1] = geo_off[last * w + 1] + edge_d[w, d - 1]

            for side, there in ((0, has_down), (1, has_up)):

                @pl.when(there & (chip + d < CHIPS))
                def _():
                    slot = edge_h.at[side, d - 1]
                    remote(slot, slot, dz_s.at[0, 0], hz_r.at[side, d - 1], pair_dev).wait_recv()
                    i = (ROWS + 1) * side
                    geo_off[i] = geo_off[i] + edge_h[side, d - 1]

    def edge_drain():
        for there, c in edge_sends:
            pl.when(there)(c.wait_send)
        pl.when(core == 1)(to_upper.wait_send)

    def thickness(i, temp):
        base = pre[i]
        lp = jnp.log(base + cum[i])
        above = jnp.where(row == 0, jnp.log(base), pltpu.roll(lp, 1, 0))
        depth = GAS * temp * (lp - above)
        below = run_up(depth)
        height[i] = below - 0.5 * depth
        logmid[i] = 0.5 * (lp + above)
        return below[:1, :]

    def thickness_row(j):
        d_own[j] = thickness(j + 1, t_out[j])

    def gradient_row(j):
        pull = GAS * t_out[j]
        east[j] = east[j] - GRAD * (east_west(height[j + 1]) + pull * east_west(logmid[j + 1]))
        north[j] = north[j] - GRAD * (
            (height[j + 2] - height[j]) + pull * (logmid[j + 2] - logmid[j])
        )

    def both(k):
        _, theirs, n = span(k)
        at = pl.ds(theirs, n)
        return (
            remote(cum.at[pl.ds(theirs + 1, n)], pair_c.at[at], both_s.at[k, 0], both_r.at[k, 0], pair_dev),
            remote(t_out.at[at], pair_t.at[at], both_s.at[k, 1], both_r.at[k, 1], pair_dev),
        )

    def pair_row(j):
        base = pre_pair[j]
        lp = jnp.log(base + pair_c[j])
        above = jnp.where(row == 0, jnp.log(base), pltpu.roll(lp, 1, 0))
        depth = GAS * pair_t[j] * (lp - above)
        d_pair[j] = jnp.sum(depth, axis=0, keepdims=True)

    def mine_rows(k):
        mine, _, n = span(k)

        @pl.loop(0, n, unroll=n)
        def _(i):
            thickness_row(mine + i)
            pair_row(mine + i)

    def their_rows(k):
        _, theirs, n = span(k)

        @pl.loop(0, n, unroll=n)
        def _(i):
            thickness_row(theirs + i)

    def tracers(j):
        a_out[j] = advected(4, j)
        b_out[j] = advected(5, j)

    def inner_tracers():
        @pl.loop(1, ROWS - 1, unroll=11)
        def _(j):
            tracers(j)

    for f in (3, 0, 1):
        load[f].wait()
    for f in (4, 5, 6, 7, 8, 9, 10, 11):
        load[f].start()
    for k in range(EDGE):
        chunk_rows(k, column_p)
        top[k][0]()
    load[2].wait()
    pairs = [both(k) for k in range(NCHUNK)]
    for k in range(EDGE):
        chunk_rows(k, column_t)
        for c in pairs[k]:
            c.start()
    for k in range(EDGE):
        top[k][1]()
    halo_start(0)
    halo_start(1)

    @pl.when(upper)
    def _():
        pl.semaphore_wait(ready.at[0], 2)
        for k in range(EDGE):
            top[k][6]()

    out_copies = []
    for n, (src, dst) in enumerate(((t_out, halo_t), (p_out, halo_p))):
        out_copies.append(
            remote(src.at[ROWS - 1], dst.at[0], out_s.at[n, 0], out_r.at[n, 0], (up, le))
        )
        out_copies.append(remote(src.at[0], dst.at[1], out_s.at[n, 1], out_r.at[n, 1], (down, le)))
    ways = (has_up, has_down)

    def edge_rows(w):
        r = (ROWS - 1) * w
        halo_side(3, w)
        column_p(r)
        pl.when(core != w)(top[EDGE][0])
        top[EDGE][1](w)
        halo_side(2, w)
        column_t(r)
        for c in pairs[EDGE]:
            pl.when(core != w)(c.start)
        for n, c in enumerate(out_copies):
            if n % 2 != w:
                pl.when(ways[n % 2])(c.start)

    def edge_sums():
        top[EDGE][2]()
        for c in pairs[EDGE]:
            c.wait_recv()
        mine_rows(EDGE)
        edge_depths()

    @pl.when(upper)
    def _():
        pl.semaphore_wait(ready.at[1], 2)

    pl.when(~starts)(functools.partial(edge_rows, 0))
    edge_rows(1)
    pl.when(starts)(functools.partial(edge_rows, 0))
    for f in (4, 5):
        halo_start(f)
    for f in (0, 1):
        pl.when(ends)(halo[f, 0].start)
        pl.when(starts)(halo[f, 1].start)

    for n in (4, 5, 6, 7, 8, 9, 10, 11):
        load[n].wait()

    def prepare():
        @pl.loop(0, ROWS, unroll=4)
        def _(j):
            c = csq[pl.ds(j, 1), :]
            at = pl.ds(pl.multiple_of(j * LEVS, LEVS), LEVS)
            for r in range(5):
                d = c / jnp.maximum(c, sines[r : r + 1, :])
                damp[r, at, :] = jnp.broadcast_to(d, (LEVS, LANE))

        for full, parts in ((wf32, wf), (wb32, wb)):

            @pl.loop(0, 4)
            def _(r):
                for i in range(0, 256, 64):
                    hi, lo = halves(full[r, i : i + 64, :])
                    parts[r, i : i + 64, :] = hi
                    parts[r, 256 + i : 320 + i, :] = hi
                    parts[r, 512 + i : 576 + i, :] = lo

        for n in range(2):
            hi, lo = halves(wz32[n])
            wz[n, :LANE, :], wz[n, LANE : 2 * LANE, :], wz[n, 2 * LANE :, :] = hi, hi, lo

    cos9 = [math.cos(2.0 * math.pi * i / 9) for i in range(9)]
    sin9 = [math.sin(2.0 * math.pi * i / 9) for i in range(9)]

    def forward_nine(i):
        for f in range(2):
            at = pl.ds(pl.multiple_of(f * ROWS * LEVS + i * 16, 16), 16)
            x = jnp.concatenate([advected(f, 2 * i), advected(f, 2 * i + 1)], axis=0)
            xs = [x[:, LANE * a : LANE * (a + 1)] for a in range(9)]
            even = [xs[a] + xs[9 - a] for a in range(1, 5)]
            odd = [xs[a] - xs[9 - a] for a in range(1, 5)]
            hi, lo = halves(xs[0] + ((even[0] + even[1]) + (even[2] + even[3])))
            y1[at, :LANE], y1[at, LANE : 2 * LANE], y1[at, 2 * LANE :] = hi, lo, hi
            for r in range(1, 5):
                re, im = xs[0], None
                for a in range(1, 5):
                    re = re + cos9[(a * r) % 9] * even[a - 1]
                    term = -sin9[(a * r) % 9] * odd[a - 1]
                    im = term if im is None else im + term
                for part, y in ((0, re), (1, im)):
                    hi, lo = halves(y)
                    for place, value in ((0, hi), (2, lo), (4, hi)):
                        place = (place + part) * LANE
                        y4[r - 1, at, place : place + LANE] = value

    def triple(x):
        hi, lo = halves(x)
        return jnp.concatenate([hi, lo, hi], axis=1)

    def mm(x, w):
        return jnp.dot(x, w, preferred_element_type=F32)

    def spectrum(r):
        d = damp[r + 1]
        d = jnp.concatenate([d, d], axis=1)
        d = jnp.concatenate([d, d], axis=0)
        z4[r] = mm(triple(mm(y4[r], wf[r]) * d), wb[r])

    def spectrum_zero():
        d = jnp.concatenate([damp[0], damp[0]], axis=0)
        z1[...] = mm(triple(mm(y1[...], wz[0]) * d), wz[1])

    def backward_nine(i):
        for f, dst in ((0, east), (1, north)):
            at = pl.ds(pl.multiple_of(f * ROWS * LEVS + i * 16, 16), 16)
            z0 = z1[at, :]
            re = [z4[r, at, :LANE] for r in range(4)]
            im = [z4[r, at, LANE:] for r in range(4)]
            outs = [None] * 9
            outs[0] = z0 + ((re[0] + re[1]) + (re[2] + re[3]))
            for a in range(1, 5):
                even, odd = z0, None
                for r in range(1, 5):
                    even = even + cos9[(a * r) % 9] * re[r - 1]
                    term = sin9[(a * r) % 9] * im[r - 1]
                    odd = term if odd is None else odd + term
                outs[a], outs[9 - a] = even - odd, even + odd
            for a in range(9):
                dst[2 * i, :, LANE * a : LANE * (a + 1)] = outs[a][:LEVS]
                dst[2 * i + 1, :, LANE * a : LANE * (a + 1)] = outs[a][LEVS:]

    polar = (la < POLAR) | (la >= NLAT - POLAR)

    def forward():
        halo_ready(0)
        halo_ready(1)

        @pl.loop(0, ROWS // 2, unroll=2)
        def _(i):
            forward_nine(i)

    def early_fill():
        inner_tracers()

        @pl.when(polar)
        def _():
            prepare()
            forward()

    pl.when(upper)(early_fill)

    for k in range(EDGE):
        top[k][2]()
        for c in pairs[k]:
            c.wait_recv()
        mine_rows(k)
        bottom[k][1]()
    edge_sums()
    for f in (4, 5):
        pl.when(ends)(halo[f, 0].start)
        pl.when(starts)(halo[f, 1].start)
    for k in range(NCHUNK):
        top[k][3]()
        their_rows(k)
    pl.when(~upper)(early_fill)

    @pl.when(polar)
    def _():
        spectrum_zero()
        pl.loop(0, 4)(spectrum)

        @pl.loop(0, ROWS // 2, unroll=2)
        def _(i):
            backward_nine(i)

    @pl.when(~polar)
    def _():
        @pl.loop(1, ROWS - 1, unroll=11)
        def _(j):
            east[j] = advected(0, j)
            north[j] = advected(1, j)

        halo_ready(0)
        halo_ready(1)
        for j in (0, ROWS - 1):
            east[j] = advected(0, j)
            north[j] = advected(1, j)

    @pl.loop(1, ROWS - 1, unroll=11)
    def _(j):
        gradient_row(j)

    halo_ready(4)
    halo_ready(5)
    tracers(0)
    tracers(ROWS - 1)

    for n, c in enumerate(out_copies):
        pl.when(ways[1 - n % 2])(c.wait_recv)
    top[EDGE][4]()
    for side, there in ((0, has_down), (1, has_up)):

        @pl.when(there)
        def _():
            i = (ROWS + 1) * side
            cum[i] = run_down(halo_p[side])
            thickness(i, halo_t[side])

    @pl.when(la == 0)
    def _():
        height[0] = height[1]
        logmid[0] = logmid[1]

    @pl.when(la == NLAT - 1)
    def _():
        height[ROWS + 1] = height[ROWS]
        logmid[ROWS + 1] = logmid[ROWS]

    gradient_row(0)
    gradient_row(ROWS - 1)

    for k in range(EDGE):
        bottom[k][2]()
    edge_offsets()
    for k in range(EDGE):
        bottom[k][3]()

    @pl.when(la == 0)
    def _():
        geo_off[0] = geo_off[1]

    @pl.when(la == NLAT - 1)
    def _():
        geo_off[ROWS + 1] = geo_off[ROWS]

    for k in range(NCHUNK):
        top[k][5]()
    for k in range(EDGE):
        bottom[k][5]()
    edge_drain()
    for pair in pairs:
        for c in pair:
            c.wait_send()
    for (f, side), c in halo.items():
        pl.when(ways[side])(c.wait_send)
    for n, c in enumerate(out_copies):
        pl.when(ways[n % 2])(c.wait_send)


def second_kernel(
    height, east, north, t_out, p_out, a_out, b_out, geo_off,
    east_hbm, north_hbm, t_hbm, p_hbm, a_hbm, b_hbm, geo_hbm,
    east_buf, north_buf, geo_buf, sem,
):
    copies = [
        pltpu.make_async_copy(src, dst, sem.at[n])
        for n, (src, dst) in enumerate(((t_out, t_hbm), (p_out, p_hbm), (a_out, a_hbm), (b_out, b_hbm)))
    ]
    for c in copies:
        c.start()
    part = 8
    for q in range(ROWS // part):

        @pl.loop(part * q, part * (q + 1), unroll=4)
        def _(j):
            off = geo_off[j + 1]
            geo_buf[j] = height[j + 1] + off
            east_buf[j] = east[j] - GRAD * east_west(off)
            north_buf[j] = north[j] - GRAD * (geo_off[j + 2] - geo_off[j])

        for m, (src, dst) in enumerate(((east_buf, east_hbm), (north_buf, north_hbm), (geo_buf, geo_hbm))):
            rows = pl.ds(part * q, part)
            c = pltpu.make_async_copy(src.at[rows], dst.at[rows], sem.at[4 + 3 * q + m])
            c.start()
            copies.append(c)
    for c in copies:
        c.wait()


def shards(u, v, t, p, a, b, terrain):
    wf, wb, wz, sines, csq = (jnp.asarray(x) for x in tables())
    ins = [u, v, t, p, a, b, terrain, csq, sines, wf, wb, wz]
    ins = [pltpu.with_memory_space_constraint(x, pltpu.HBM) for x in ins]
    full = (ROWS, LEVS, LON)
    wide = (ROWS + 2, LEVS, LON)
    line = (ROWS, 1, LON)
    line_wide = (ROWS + 2, 1, LON)
    dma = pltpu.SemaphoreType.DMA
    scan_sems = [
        dma((NCHUNK,)), dma((NCHUNK,)), dma((NCHUNK, 3)), dma((NCHUNK, 3)),
        dma((NCHUNK,)), dma((NCHUNK,)), dma((2,)), dma((2,)),
    ]
    mids = pl.pallas_call(
        first_kernel,
        out_shape=[pltpu.VMEM(wide, F32)] + [pltpu.VMEM(full, F32)] * 6 + [pltpu.VMEM(line_wide, F32)],
        in_specs=[pl.BlockSpec(memory_space=pltpu.HBM)] * len(ins),
        out_specs=[pl.BlockSpec(memory_space=pltpu.VMEM)] * 8,
        scratch_shapes=[
            pltpu.VMEM((6,) + wide, F32),
            pltpu.VMEM((ROWS, LON), F32),
            pltpu.VMEM((ROWS, LANE), F32),
            pltpu.VMEM((8, LANE), F32),
            pltpu.VMEM((4, 256, 256), F32),
            pltpu.VMEM((4, 256, 256), F32),
            pltpu.VMEM((2, LANE, LANE), F32),
            pltpu.VMEM((4, 3 * 256, 256), BF16),
            pltpu.VMEM((4, 3 * 256, 256), BF16),
            pltpu.VMEM((2, 3 * LANE, LANE), BF16),
            pltpu.VMEM(wide, F32),
            pltpu.VMEM(wide, F32),
            pltpu.VMEM((2, LEVS, LON), F32),
            pltpu.VMEM((2, LEVS, LON), F32),
            pltpu.VMEM((5, ROWS * LEVS, LANE), F32),
            pltpu.VMEM(full, F32),
            pltpu.VMEM(full, F32),
            pltpu.VMEM(line, F32),
            pltpu.VMEM(line, F32),
            pltpu.VMEM(line, F32),
            pltpu.VMEM((3,) + line, F32),
            pltpu.VMEM(line_wide, F32),
            pltpu.VMEM(line, F32),
            pltpu.VMEM(line, F32),
            pltpu.VMEM(line, F32),
            pltpu.VMEM(line, F32),
            pltpu.VMEM((3,) + line, F32),
            pltpu.VMEM(line, F32),
            pltpu.VMEM((3, 2, 1, LON), F32),
            pltpu.VMEM((2, 3, 1, LON), F32),
            pltpu.VMEM((2, 3, 1, LON), F32),
            pltpu.VMEM(line, F32),
            pltpu.VMEM((4, 2 * ROWS * LEVS, 6 * LANE), BF16),
            pltpu.VMEM((2 * ROWS * LEVS, 3 * LANE), BF16),
            pltpu.VMEM((4, 2 * ROWS * LEVS, 2 * LANE), F32),
            pltpu.VMEM((2 * ROWS * LEVS, LANE), F32),
            pltpu.SemaphoreType.REGULAR((2,)), dma((12,)), dma((6, 2)), dma((6, 2)), dma((2, 2)), dma((2, 2)),
            dma((NCHUNK, 2)), dma((NCHUNK, 2)),
        ]
        + scan_sems
        + scan_sems[2:]
        + [dma((3, 2)), dma((3, 2)), dma((3, 2)), dma((2, 3)), dma((3, 2)), dma((2, 3))],
        compiler_params=pltpu.CompilerParams(
            collective_id=0, has_side_effects=True, vmem_limit_bytes=40 << 20
        ),
    )(*ins)
    outs = pl.pallas_call(
        second_kernel,
        out_shape=[jax.ShapeDtypeStruct(full, F32)] * 7,
        in_specs=[pl.BlockSpec(memory_space=pltpu.VMEM)] * 8,
        out_specs=[pl.BlockSpec(memory_space=pltpu.HBM)] * 7,
        scratch_shapes=[pltpu.VMEM(full, F32)] * 3 + [dma((13,))],
        compiler_params=pltpu.CompilerParams(vmem_limit_bytes=20 << 20),
    )(*mids)
    return tuple(outs)


def solution(mesh):
    field = P("lat", "lev", None)
    return jax.shard_map(
        shards,
        mesh=mesh,
        in_specs=(field,) * 6 + (P("lat", None),),
        out_specs=(field,) * 7,
        check_vma=False,
    )
```

```python
import functools
import math

import jax
import jax.numpy as jnp
import numpy as np
from jax import lax
from jax.experimental import pallas as pl
from jax.experimental.pallas import tpu as pltpu
from jax.sharding import PartitionSpec as P

MESH = pl.DeviceIdType.MESH
F32 = jnp.float32
BF16 = jnp.bfloat16

ROWS, LEVS, LON = 24, 8, 1152
NLAT = 32
CHIPS = 4
LANE = 128
COURANT = 0.1
GRAD = 0.1
GAS = 0.3
TOP = 1.0
CUT = 0.5

POLAR = sum(
    math.cos(((ROWS * band + ROWS - 0.5) / (NLAT * ROWS) - 0.5) * math.pi) ** 2 < CUT
    or math.cos(((ROWS * band + 0.5) / (NLAT * ROWS) - 0.5) * math.pi) ** 2 < CUT
    for band in range(NLAT // 2)
)
INTERIOR = ((1, 6), (13, 5))
EDGE = len(INTERIOR)
NCHUNK = EDGE + 1


@functools.cache
def tables():
    b = np.arange(LANE)
    fwd, back = [], []
    for r in range(1, 5):
        angle = 2.0 * np.pi * ((b[:, None] * (9 * b[None, :] + r)) % LON) / LON
        mr, mi = np.cos(angle), -np.sin(angle)
        w = np.block([[mr, mi], [-mi, mr]])
        fwd.append(w)
        back.append(w.T * (2.0 / LON))
    angle = 2.0 * np.pi * ((b[:, None] * b[None, :]) % LANE) / LANE
    w0 = np.concatenate([np.cos(angle[:, :65]), np.sin(angle[:, 1:64])], axis=1)
    weight = np.full((LANE,), 2.0)
    weight[0] = weight[64] = 1.0
    b0 = (w0 * weight[None, :]).T / LON
    wf = np.stack(fwd).astype(np.float32)
    wb = np.stack(back).astype(np.float32)
    wz = np.stack([w0, b0]).astype(np.float32)
    sines = np.zeros((8, LANE))
    freq0 = np.concatenate([np.arange(65), np.arange(1, 64)]) * 9
    sines[0] = np.sin(np.pi * freq0 / LON) ** 2 * CUT
    for r in range(1, 5):
        sines[r] = np.sin(np.pi * (9 * b + r) / LON) ** 2 * CUT
    lat = (np.arange(NLAT * ROWS, dtype=np.float32) + np.float32(0.5)) * np.float32(
        math.pi / (NLAT * ROWS)
    ) - np.float32(0.5 * math.pi)
    csq = np.cos(lat.astype(np.float64)).astype(np.float32) ** 2
    csq = np.broadcast_to(csq.reshape(NLAT, ROWS, 1), (NLAT, ROWS, LANE)).astype(np.float32)
    return wf, wb, wz, sines.astype(np.float32), np.ascontiguousarray(csq)


def east_west(x):
    return pltpu.roll(x, LON - 1, 1) - pltpu.roll(x, 1, 1)


def first_kernel(
    u_hbm, v_hbm, t_hbm, p_hbm, a_hbm, b_hbm, terr_hbm, csq_hbm, sin_hbm, wf_hbm, wb_hbm, wz_hbm,
    height, east, north, t_out, p_out, a_out, b_out, geo_off,
    fields, terr, csq, sines, wf32, wb32, wz32, wf, wb, wz,
    cum, logmid, halo_t, halo_p, damp, pair_t, pair_c,
    s_own, s_pair, s_chip, s_recv, pre, pre_pair,
    d_own, d_pair, d_chip, d_recv, geo_pair,
    edge_s, edge_d, edge_h, both_chips,
    y4, y1, z4, z1,
    ready, load_sem, halo_s, halo_r, out_s, out_r, both_s, both_r,
    bp_s, bp_r, bz_s, bz_r, bq_s, bq_r, be_s, be_r,
    cz_s, cz_r, cq_s, cq_r, ce_s, ce_r,
    ez_s, ez_r, dz_s, dz_r, hz_s, hz_r,
):
    la, le = lax.axis_index("lat"), lax.axis_index("lev")
    chip, core = le // 2, le % 2
    other = 1 - core
    up, down = (la + 1) % NLAT, (la + NLAT - 1) % NLAT
    pair_dev = (la, chip * 2 + other)
    side_lat = (la + NLAT - 1 + 2 * core) % NLAT
    cross_dev = (side_lat, chip * 2 + other)
    side_dev = (side_lat, le)
    has_up, has_down = la < NLAT - 1, la > 0
    has_side = jnp.where(core == 0, la, NLAT - 1 - la) > 0
    core_f = core.astype(F32)
    other_f = other.astype(F32)

    def remote(src, dst, send, recv, dev):
        return pltpu.make_async_remote_copy(
            src_ref=src, dst_ref=dst, send_sem=send, recv_sem=recv, device_id=dev, device_id_type=MESH
        )

    ins = (u_hbm, v_hbm, t_hbm, p_hbm, a_hbm, b_hbm)
    load = [
        pltpu.make_async_copy(ins[f], fields.at[f, pl.ds(1, ROWS)], load_sem.at[f]) for f in range(6)
    ]
    load += [
        pltpu.make_async_copy(terr_hbm, terr, load_sem.at[6]),
        pltpu.make_async_copy(csq_hbm.at[la], csq, load_sem.at[7]),
        pltpu.make_async_copy(sin_hbm, sines, load_sem.at[8]),
        pltpu.make_async_copy(wf_hbm, wf32, load_sem.at[9]),
        pltpu.make_async_copy(wb_hbm, wb32, load_sem.at[10]),
        pltpu.make_async_copy(wz_hbm, wz32, load_sem.at[11]),
    ]

    barrier = pltpu.get_barrier_semaphore()
    upper = chip < CHIPS // 2
    others = [(chip + d) % CHIPS for d in range(1, CHIPS)]
    starts, ends = la == NLAT // 2, la == NLAT // 2 - 1
    to_up = [(has_up, (up, le)), (has_up & (core == 1), cross_dev)]
    to_down = [(has_down, (down, le)), (has_down & (core == 0), cross_dev)]
    far_up = [(has_up & (c > chip), (up, c * 2)) for c in others]
    far_down = [(has_down & (c > chip), (down, c * 2 + 1)) for c in others]
    n_up = has_up.astype(jnp.int32) + jnp.where(has_up & (core == 1), 1 + 2 * chip, 0)
    n_down = has_down.astype(jnp.int32) + jnp.where(has_down & (core == 0), 1 + 2 * chip, 0)
    greet = [(la >= 0, pair_dev)] + to_down + far_down + to_up + far_up
    for c in others:
        inside = upper | (c >= CHIPS // 2)
        greet += [(inside, (la, c * 2 + core)), (inside, (la, c * 2 + other))]
    for there, dev in greet:

        @pl.when(there)
        def _():
            pl.semaphore_signal(barrier, inc=1, device_id=dev, device_id_type=MESH)

    for f in (3, 0, 1, 2):
        load[f].start()

    halo = {}
    for f in (2, 3, 0, 1, 4, 5):
        halo[f, 0] = remote(
            ins[f].at[ROWS - 1], fields.at[f, 0], halo_s.at[f, 0], halo_r.at[f, 0], (up, le)
        )
        halo[f, 1] = remote(
            ins[f].at[0], fields.at[f, ROWS + 1], halo_s.at[f, 1], halo_r.at[f, 1], (down, le)
        )


    def halo_start(f):
        pl.when(has_up & ~ends)(halo[f, 0].start)
        pl.when(has_down & ~starts)(halo[f, 1].start)

    def enter():
        pl.semaphore_wait(barrier, jnp.where(upper, 3, 7) + n_up + n_down)

        @pl.when(~upper)
        def _():
            for c in range(CHIPS):
                at = ready.at[jnp.where(c // 2 == CHIPS - 1 - chip, 0, 1)]
                pl.semaphore_signal(at, inc=1, device_id=(la, c), device_id_type=MESH)

        for f in (3, 2):
            pl.when(has_up)(halo[f, 0].start)
            pl.when(has_down)(halo[f, 1].start)

    pl.when(~starts)(enter)

    row = lax.broadcasted_iota(jnp.int32, (LEVS, LON), 0)

    def halves(x):
        hi = x.astype(BF16)
        return hi, (x - hi.astype(F32)).astype(BF16)

    def run_down(x):
        for s in (1, 2, 4):
            x = x + jnp.where(row >= s, pltpu.roll(x, s, 0), 0.0)
        return x

    def run_up(x):
        for s in (1, 2, 4):
            x = x + jnp.where(row < LEVS - s, pltpu.roll(x, LEVS - s, 0), 0.0)
        return x

    def advected(f, j):
        x = fields[f, j + 1]
        merid = fields[f, j + 2] - fields[f, j]
        return x - COURANT * (fields[0, j + 1] * east_west(x) + fields[1, j + 1] * merid)

    def halo_side(f, side):
        edge, there = (1, has_down) if side == 0 else (ROWS, has_up)
        beyond = (ROWS + 1) * side
        pl.when(there)(halo[f, side].wait_recv)

        @pl.when(~there)
        def _():
            fields[f, beyond] = fields[f, edge]

    def halo_ready(f):
        halo_side(f, 0)
        halo_side(f, 1)

    def column_t(j):
        t_out[j] = advected(2, j)

    def column_p(j):
        p = advected(3, j)
        p_out[j] = p
        c = run_down(p)
        cum[j + 1] = c
        s_own[j] = c[LEVS - 1 :, :]

    def span(k):
        if k == EDGE:
            return (ROWS - 1) * core, (ROWS - 1) * other, 1
        start, n = INTERIOR[k]
        return start + n * core, start + n * other, n

    def chunk_rows(k, body):
        if k == EDGE:
            body(0)
            body(ROWS - 1)
        else:
            start, n = INTERIOR[k]

            @pl.loop(start, start + 2 * n, unroll=n)
            def _(j):
                body(j)

    def scan(k, own, pair, total, recv, result, result_pair, sign, base, zs, zr, qs, qr, es, er, ps=None, pr=None):
        mine, theirs, n = span(k)
        mine_s, theirs_s = pl.ds(mine, n), pl.ds(theirs, n)
        if ps is not None:
            to_pair = remote(own.at[theirs_s], pair.at[theirs_s], ps.at[k], pr.at[k], pair_dev)
            from_pair = remote(own.at[mine_s], pair.at[mine_s], ps.at[k], pr.at[k], pair_dev)
        share = remote(
            result_pair.at[mine_s], result.at[pl.ds(mine + 1, n)], qs.at[k], qr.at[k], pair_dev
        )
        shared = remote(
            result_pair.at[theirs_s], result.at[pl.ds(theirs + 1, n)], qs.at[k], qr.at[k], pair_dev
        )
        hops = {}
        buddy = remote(
            total.at[mine_s], recv.at[0, mine_s], zs.at[k, 0], zr.at[k, 0],
            (la, (chip + 1 - 2 * (chip % 2)) * 2 + core),
        )
        relay = remote(
            both_chips.at[mine_s], recv.at[1, mine_s], zs.at[k, 1], zr.at[k, 1],
            (la, (CHIPS - 1 - chip) * 2 + core),
        )
        for d in (3, 2, 1):
            hops[d] = remote(
                total.at[mine_s], recv.at[d - 1, mine_s], zs.at[k, d - 1], zr.at[k, d - 1],
                (la, ((chip + CHIPS + sign * d) % CHIPS) * 2 + core),
            )
        if sign > 0:
            sends = {d: chip + d < CHIPS for d in hops}
            gets = {d: chip >= d for d in hops}
        else:
            sends = {d: chip >= d for d in hops}
            gets = {d: chip + d < CHIPS for d in hops}
        edges = []
        if k == EDGE:
            direct = {
                (d, w): remote(
                    own.at[(ROWS - 1) * w], edge_s.at[d - 1, core], ez_s.at[d - 1, w], ez_r.at[d - 1, core],
                    (la, ((chip + d) % CHIPS) * 2 + w),
                )
                for d in (1, 2, 3)
                for w in range(2)
            }
            slot = (ROWS + 1) * other
            edges = [
                remote(result.at[mine + 1], result.at[slot], es.at[0], er.at[other], side_dev),
                remote(result_pair.at[mine], result.at[slot], es.at[1], er.at[other], cross_dev),
            ]

        def begin():
            to_pair.start()

        def middle(row=None):
            if k == EDGE:
                for (d, w), c in direct.items():
                    if w == row:
                        pl.when(sends[d])(c.start)
                return
            if ps is not None:
                from_pair.wait_recv()
            total[mine_s] = own[mine_s] + pair[mine_s]
            if sign > 0:
                pl.when(chip < CHIPS - 1)(buddy.start)
            else:
                for d in hops:
                    pl.when(sends[d])(hops[d].start)

        def across():
            buddy.wait_recv()
            both_chips[mine_s] = total[mine_s] + recv[0, mine_s]
            relay.start()

        def end():
            acc = base(mine, n)
            result[pl.ds(mine + 1, n)] = acc
            if k == EDGE:
                from_pair.wait_recv()
            if sign > 0 and k != EDGE:

                @pl.when(chip == CHIPS - 1)
                def _():
                    buddy.wait_recv()

                @pl.when(chip % 2 == 1)
                def _():
                    result[pl.ds(mine + 1, n)] = result[pl.ds(mine + 1, n)] + recv[0, mine_s]

                @pl.when(~upper)
                def _():
                    relay.wait_recv()
                    result[pl.ds(mine + 1, n)] = result[pl.ds(mine + 1, n)] + recv[1, mine_s]

            for d in hops if sign < 0 or k == EDGE else ():

                @pl.when(gets[d])
                def _():
                    if k == EDGE:
                        for w in range(2):
                            remote(
                                edge_s.at[d - 1, w], edge_s.at[d - 1, w], ez_s.at[d - 1, w], ez_r.at[d - 1, w], pair_dev
                            ).wait_recv()
                        result[mine + 1] = result[mine + 1] + (edge_s[d - 1, 0] + edge_s[d - 1, 1])
                        return
                    hops[d].wait_recv()
                    result[pl.ds(mine + 1, n)] = result[pl.ds(mine + 1, n)] + recv[d - 1, mine_s]

            acc = result[pl.ds(mine + 1, n)]
            mine_f, pair_f = (core_f, other_f) if sign > 0 else (other_f, core_f)
            result_pair[mine_s] = acc + pair_f * own[mine_s]
            share.start()
            result[pl.ds(mine + 1, n)] = acc + mine_f * pair[mine_s]
            for e in edges:
                pl.when(has_side)(e.start)

        def finish():
            shared.wait_recv()

        def edge_ready():
            for side, there in ((0, has_down), (1, has_up)):
                slot = (ROWS + 1) * side
                c = remote(result.at[slot], result.at[slot], es.at[0], er.at[side], side_dev)
                pl.when(there)(c.wait_recv)

        def drain():
            if ps is not None:
                to_pair.wait_send()
            if k == EDGE:
                for (d, _), c in direct.items():
                    pl.when(sends[d])(c.wait_send)
            elif sign > 0:
                pl.when(chip < CHIPS - 1)(buddy.wait_send)
                pl.when(upper)(relay.wait_send)
            else:
                for d in hops:
                    pl.when(sends[d])(hops[d].wait_send)
            for e in edges:
                pl.when(has_side)(e.wait_send)

        def drain_share():
            share.wait_send()

        return begin, middle, end, finish, edge_ready, drain, across, drain_share

    def base_top(mine, n):
        return jnp.full((n, 1, LON), TOP, F32)

    def base_terrain(mine, n):
        return jnp.stack([terr[pl.ds(mine + i, 1), :] for i in range(n)], 0)

    top = [
        scan(
            k, s_own, s_pair, s_chip, s_recv, pre, pre_pair, 1, base_top,
            bz_s, bz_r, bq_s, bq_r, be_s, be_r, bp_s, bp_r,
        )
        for k in range(NCHUNK)
    ]
    bottom = [
        scan(
            k, d_own, d_pair, d_chip, d_recv, geo_off, geo_pair, -1, base_terrain,
            cz_s, cz_r, cq_s, cq_r, ce_s, ce_r,
        )
        for k in range(EDGE)
    ]

    edge_row = (ROWS - 1) * core
    edge_sends = []
    for d in (3, 2, 1):
        above = chip + CHIPS - d
        for tc in range(2):
            edge_sends.append((
                has_side & (chip >= d),
                remote(
                    d_chip.at[edge_row], edge_h.at[other, d - 1], hz_s.at[d - 1, tc], hz_r.at[other, d - 1],
                    (side_lat, (above % CHIPS) * 2 + tc),
                ),
            ))
            edge_sends.append((
                chip >= d,
                remote(
                    d_chip.at[edge_row], edge_d.at[core, d - 1], dz_s.at[d - 1, tc], dz_r.at[core, d - 1],
                    (la, (above % CHIPS) * 2 + tc),
                ),
            ))
    edge_slot = (ROWS + 1) * other
    edge_sends += [
        (has_side, remote(geo_pair.at[edge_row], geo_off.at[edge_slot], ce_s.at[0], ce_r.at[other], side_dev)),
        (has_side, remote(geo_pair.at[(ROWS - 1) * other], geo_off.at[edge_slot], ce_s.at[1], ce_r.at[other], cross_dev)),
    ]
    last = ROWS - 1
    to_upper = remote(d_own.at[last], d_pair.at[last], cq_s.at[EDGE], cq_r.at[EDGE], pair_dev)

    def edge_depths():
        own, pair = d_own[edge_row], d_pair[edge_row]
        d_chip[edge_row] = own + pair
        ground = terr[pl.ds(edge_row, 1), :]
        geo_pair[0] = ground + jnp.where(core == 0, pair, own)
        geo_pair[ROWS - 1] = ground
        for there, c in edge_sends:
            pl.when(there)(c.start)
        pl.when(core == 1)(to_upper.start)

    def edge_offsets():
        for w in range(2):
            r = last * w
            geo_off[r + 1] = terr[pl.ds(r, 1), :]

        @pl.when(core == 0)
        def _():
            to_upper.wait_recv()
            for w in range(2):
                geo_off[last * w + 1] = geo_off[last * w + 1] + d_pair[last * w]

        for side, there in ((0, has_down), (1, has_up)):
            slot = (ROWS + 1) * side

            @pl.when(there)
            def _():
                remote(geo_off.at[slot], geo_off.at[slot], ce_s.at[0], ce_r.at[side], side_dev).wait_recv()

        for d in (1, 2, 3):
            for w in range(2):

                @pl.when(chip + d < CHIPS)
                def _():
                    slot = edge_d.at[w, d - 1]
                    remote(slot, slot, dz_s.at[0, 0], dz_r.at[w, d - 1], pair_dev).wait_recv()
                    geo_off[last * w + 1] = geo_off[last * w + 1] + edge_d[w, d - 1]

            for side, there in ((0, has_down), (1, has_up)):

                @pl.when(there & (chip + d < CHIPS))
                def _():
                    slot = edge_h.at[side, d - 1]
                    remote(slot, slot, dz_s.at[0, 0], hz_r.at[side, d - 1], pair_dev).wait_recv()
                    i = (ROWS + 1) * side
                    geo_off[i] = geo_off[i] + edge_h[side, d - 1]

    def edge_drain():
        for there, c in edge_sends:
            pl.when(there)(c.wait_send)
        pl.when(core == 1)(to_upper.wait_send)

    def thickness(i, temp):
        base = pre[i]
        lp = jnp.log(base + cum[i])
        above = jnp.where(row == 0, jnp.log(base), pltpu.roll(lp, 1, 0))
        depth = GAS * temp * (lp - above)
        below = run_up(depth)
        height[i] = below - 0.5 * depth
        logmid[i] = 0.5 * (lp + above)
        return below[:1, :]

    def thickness_row(j):
        d_own[j] = thickness(j + 1, t_out[j])

    def gradient_row(j):
        pull = GAS * t_out[j]
        east[j] = east[j] - GRAD * (east_west(height[j + 1]) + pull * east_west(logmid[j + 1]))
        north[j] = north[j] - GRAD * (
            (height[j + 2] - height[j]) + pull * (logmid[j + 2] - logmid[j])
        )

    def both(k):
        _, theirs, n = span(k)
        at = pl.ds(theirs, n)
        return (
            remote(cum.at[pl.ds(theirs + 1, n)], pair_c.at[at], both_s.at[k, 0], both_r.at[k, 0], pair_dev),
            remote(t_out.at[at], pair_t.at[at], both_s.at[k, 1], both_r.at[k, 1], pair_dev),
        )

    def pair_row(j):
        base = pre_pair[j]
        lp = jnp.log(base + pair_c[j])
        above = jnp.where(row == 0, jnp.log(base), pltpu.roll(lp, 1, 0))
        depth = GAS * pair_t[j] * (lp - above)
        d_pair[j] = jnp.sum(depth, axis=0, keepdims=True)

    def mine_rows(k):
        mine, _, n = span(k)

        @pl.loop(0, n, unroll=n)
        def _(i):
            thickness_row(mine + i)
            pair_row(mine + i)

    def their_rows(k):
        _, theirs, n = span(k)

        @pl.loop(0, n, unroll=n)
        def _(i):
            thickness_row(theirs + i)

    def tracers(j):
        a_out[j] = advected(4, j)
        b_out[j] = advected(5, j)

    def inner_tracers():
        @pl.loop(1, ROWS - 1, unroll=11)
        def _(j):
            tracers(j)

    for f in (3, 0, 1):
        load[f].wait()
    for f in (4, 5, 6, 7, 8, 9, 10, 11):
        load[f].start()
    for k in range(EDGE):
        chunk_rows(k, column_p)
        pl.when(~starts)(top[k][0])

    @pl.when(starts)
    def _():
        enter()
        for k in range(EDGE):
            top[k][0]()

    load[2].wait()
    pairs = [both(k) for k in range(NCHUNK)]
    for k in range(EDGE):
        chunk_rows(k, column_t)
        for c in pairs[k]:
            c.start()
    for k in range(EDGE):
        top[k][1]()
    halo_start(0)
    halo_start(1)

    @pl.when(upper)
    def _():
        pl.semaphore_wait(ready.at[0], 2)
        for k in range(EDGE):
            top[k][6]()

    out_copies = []
    for n, (src, dst) in enumerate(((t_out, halo_t), (p_out, halo_p))):
        out_copies.append(
            remote(src.at[ROWS - 1], dst.at[0], out_s.at[n, 0], out_r.at[n, 0], (up, le))
        )
        out_copies.append(remote(src.at[0], dst.at[1], out_s.at[n, 1], out_r.at[n, 1], (down, le)))
    ways = (has_up, has_down)

    def edge_rows(w):
        r = (ROWS - 1) * w
        halo_side(3, w)
        column_p(r)
        pl.when(core != w)(top[EDGE][0])
        top[EDGE][1](w)
        halo_side(2, w)
        column_t(r)
        for c in pairs[EDGE]:
            pl.when(core != w)(c.start)
        for n, c in enumerate(out_copies):
            if n % 2 != w:
                pl.when(ways[n % 2])(c.start)

    def edge_sums():
        top[EDGE][2]()
        for c in pairs[EDGE]:
            c.wait_recv()
        mine_rows(EDGE)
        edge_depths()

    @pl.when(upper)
    def _():
        pl.semaphore_wait(ready.at[1], 2)

    pl.when(~starts)(functools.partial(edge_rows, 0))
    pl.when(~(ends & ~upper))(functools.partial(edge_rows, 1))
    pl.when(starts)(functools.partial(edge_rows, 0))
    for f in (4, 5):
        halo_start(f)
    for f in (0, 1):
        pl.when(ends)(halo[f, 0].start)
        pl.when(starts)(halo[f, 1].start)

    for n in (4, 5, 6, 7, 8, 9, 10, 11):
        load[n].wait()

    def prepare():
        @pl.loop(0, ROWS, unroll=4)
        def _(j):
            c = csq[pl.ds(j, 1), :]
            at = pl.ds(pl.multiple_of(j * LEVS, LEVS), LEVS)
            for r in range(5):
                d = c / jnp.maximum(c, sines[r : r + 1, :])
                damp[r, at, :] = jnp.broadcast_to(d, (LEVS, LANE))

        for full, parts in ((wf32, wf), (wb32, wb)):

            @pl.loop(0, 4)
            def _(r):
                for i in range(0, 256, 64):
                    hi, lo = halves(full[r, i : i + 64, :])
                    parts[r, i : i + 64, :] = hi
                    parts[r, 256 + i : 320 + i, :] = hi
                    parts[r, 512 + i : 576 + i, :] = lo

        for n in range(2):
            hi, lo = halves(wz32[n])
            wz[n, :LANE, :], wz[n, LANE : 2 * LANE, :], wz[n, 2 * LANE :, :] = hi, hi, lo

    cos9 = [math.cos(2.0 * math.pi * i / 9) for i in range(9)]
    sin9 = [math.sin(2.0 * math.pi * i / 9) for i in range(9)]

    def forward_nine(i):
        for f in range(2):
            at = pl.ds(pl.multiple_of(f * ROWS * LEVS + i * 16, 16), 16)
            x = jnp.concatenate([advected(f, 2 * i), advected(f, 2 * i + 1)], axis=0)
            xs = [x[:, LANE * a : LANE * (a + 1)] for a in range(9)]
            even = [xs[a] + xs[9 - a] for a in range(1, 5)]
            odd = [xs[a] - xs[9 - a] for a in range(1, 5)]
            hi, lo = halves(xs[0] + ((even[0] + even[1]) + (even[2] + even[3])))
            y1[at, :LANE], y1[at, LANE : 2 * LANE], y1[at, 2 * LANE :] = hi, lo, hi
            for r in range(1, 5):
                re, im = xs[0], None
                for a in range(1, 5):
                    re = re + cos9[(a * r) % 9] * even[a - 1]
                    term = -sin9[(a * r) % 9] * odd[a - 1]
                    im = term if im is None else im + term
                for part, y in ((0, re), (1, im)):
                    hi, lo = halves(y)
                    for place, value in ((0, hi), (2, lo), (4, hi)):
                        place = (place + part) * LANE
                        y4[r - 1, at, place : place + LANE] = value

    def triple(x):
        hi, lo = halves(x)
        return jnp.concatenate([hi, lo, hi], axis=1)

    def mm(x, w):
        return jnp.dot(x, w, preferred_element_type=F32)

    def spectrum(r):
        d = damp[r + 1]
        d = jnp.concatenate([d, d], axis=1)
        d = jnp.concatenate([d, d], axis=0)
        z4[r] = mm(triple(mm(y4[r], wf[r]) * d), wb[r])

    def spectrum_zero():
        d = jnp.concatenate([damp[0], damp[0]], axis=0)
        z1[...] = mm(triple(mm(y1[...], wz[0]) * d), wz[1])

    def backward_nine(i):
        for f, dst in ((0, east), (1, north)):
            at = pl.ds(pl.multiple_of(f * ROWS * LEVS + i * 16, 16), 16)
            z0 = z1[at, :]
            re = [z4[r, at, :LANE] for r in range(4)]
            im = [z4[r, at, LANE:] for r in range(4)]
            outs = [None] * 9
            outs[0] = z0 + ((re[0] + re[1]) + (re[2] + re[3]))
            for a in range(1, 5):
                even, odd = z0, None
                for r in range(1, 5):
                    even = even + cos9[(a * r) % 9] * re[r - 1]
                    term = sin9[(a * r) % 9] * im[r - 1]
                    odd = term if odd is None else odd + term
                outs[a], outs[9 - a] = even - odd, even + odd
            for a in range(9):
                dst[2 * i, :, LANE * a : LANE * (a + 1)] = outs[a][:LEVS]
                dst[2 * i + 1, :, LANE * a : LANE * (a + 1)] = outs[a][LEVS:]

    polar = (la < POLAR) | (la >= NLAT - POLAR)

    def forward():
        halo_ready(0)
        halo_ready(1)

        @pl.loop(0, ROWS // 2, unroll=2)
        def _(i):
            forward_nine(i)

    def early_fill():
        inner_tracers()

        @pl.when(polar)
        def _():
            prepare()
            forward()

    pl.when(upper)(early_fill)

    for k in range(EDGE):
        top[k][2]()
        for c in pairs[k]:
            c.wait_recv()
        mine_rows(k)
        bottom[k][1]()
    pl.when(ends & ~upper)(functools.partial(edge_rows, 1))
    edge_sums()
    for f in (4, 5):
        pl.when(ends)(halo[f, 0].start)
        pl.when(starts)(halo[f, 1].start)
    for k in range(NCHUNK):
        top[k][3]()
        their_rows(k)
    pl.when(~upper)(early_fill)

    @pl.when(polar)
    def _():
        spectrum_zero()
        pl.loop(0, 4)(spectrum)

        @pl.loop(0, ROWS // 2, unroll=2)
        def _(i):
            backward_nine(i)

    @pl.when(~polar)
    def _():
        @pl.loop(1, ROWS - 1, unroll=11)
        def _(j):
            east[j] = advected(0, j)
            north[j] = advected(1, j)

        halo_ready(0)
        halo_ready(1)
        for j in (0, ROWS - 1):
            east[j] = advected(0, j)
            north[j] = advected(1, j)

    @pl.loop(1, ROWS - 1, unroll=11)
    def _(j):
        gradient_row(j)

    halo_ready(4)
    halo_ready(5)
    tracers(0)
    tracers(ROWS - 1)

    for n, c in enumerate(out_copies):
        pl.when(ways[1 - n % 2])(c.wait_recv)
    top[EDGE][4]()
    for side, there in ((0, has_down), (1, has_up)):

        @pl.when(there)
        def _():
            i = (ROWS + 1) * side
            cum[i] = run_down(halo_p[side])
            thickness(i, halo_t[side])

    @pl.when(la == 0)
    def _():
        height[0] = height[1]
        logmid[0] = logmid[1]

    @pl.when(la == NLAT - 1)
    def _():
        height[ROWS + 1] = height[ROWS]
        logmid[ROWS + 1] = logmid[ROWS]

    gradient_row(0)
    gradient_row(ROWS - 1)

    for k in range(NCHUNK):
        top[k][5]()
        top[k][7]()
    for k in range(EDGE):
        bottom[k][5]()
    edge_drain()
    for pair in pairs:
        for c in pair:
            c.wait_send()
    for (f, side), c in halo.items():
        pl.when(ways[side])(c.wait_send)
    for n, c in enumerate(out_copies):
        pl.when(ways[n % 2])(c.wait_send)
    for k in range(EDGE):
        bottom[k][2]()
    edge_offsets()
    for k in range(EDGE):
        bottom[k][3]()

    @pl.when(la == 0)
    def _():
        geo_off[0] = geo_off[1]

    @pl.when(la == NLAT - 1)
    def _():
        geo_off[ROWS + 1] = geo_off[ROWS]
    for k in range(EDGE):
        bottom[k][7]()


def second_kernel(
    height, east, north, t_out, p_out, a_out, b_out, geo_off,
    east_hbm, north_hbm, t_hbm, p_hbm, a_hbm, b_hbm, geo_hbm,
    east_buf, north_buf, geo_buf, sem,
):
    copies = [
        pltpu.make_async_copy(src, dst, sem.at[n])
        for n, (src, dst) in enumerate(((t_out, t_hbm), (p_out, p_hbm), (a_out, a_hbm), (b_out, b_hbm)))
    ]
    for c in copies:
        c.start()
    part = 8
    for q in range(ROWS // part):

        @pl.loop(part * q, part * (q + 1), unroll=4)
        def _(j):
            off = geo_off[j + 1]
            geo_buf[j] = height[j + 1] + off
            east_buf[j] = east[j] - GRAD * east_west(off)
            north_buf[j] = north[j] - GRAD * (geo_off[j + 2] - geo_off[j])

        for m, (src, dst) in enumerate(((east_buf, east_hbm), (north_buf, north_hbm), (geo_buf, geo_hbm))):
            rows = pl.ds(part * q, part)
            c = pltpu.make_async_copy(src.at[rows], dst.at[rows], sem.at[4 + 3 * q + m])
            c.start()
            copies.append(c)
    for c in copies:
        c.wait()


def shards(u, v, t, p, a, b, terrain):
    wf, wb, wz, sines, csq = (jnp.asarray(x) for x in tables())
    ins = [u, v, t, p, a, b, terrain, csq, sines, wf, wb, wz]
    ins = [pltpu.with_memory_space_constraint(x, pltpu.HBM) for x in ins]
    full = (ROWS, LEVS, LON)
    wide = (ROWS + 2, LEVS, LON)
    line = (ROWS, 1, LON)
    line_wide = (ROWS + 2, 1, LON)
    dma = pltpu.SemaphoreType.DMA
    scan_sems = [
        dma((NCHUNK,)), dma((NCHUNK,)), dma((NCHUNK, 3)), dma((NCHUNK, 3)),
        dma((NCHUNK,)), dma((NCHUNK,)), dma((2,)), dma((2,)),
    ]
    mids = pl.pallas_call(
        first_kernel,
        out_shape=[pltpu.VMEM(wide, F32)] + [pltpu.VMEM(full, F32)] * 6 + [pltpu.VMEM(line_wide, F32)],
        in_specs=[pl.BlockSpec(memory_space=pltpu.HBM)] * len(ins),
        out_specs=[pl.BlockSpec(memory_space=pltpu.VMEM)] * 8,
        scratch_shapes=[
            pltpu.VMEM((6,) + wide, F32),
            pltpu.VMEM((ROWS, LON), F32),
            pltpu.VMEM((ROWS, LANE), F32),
            pltpu.VMEM((8, LANE), F32),
            pltpu.VMEM((4, 256, 256), F32),
            pltpu.VMEM((4, 256, 256), F32),
            pltpu.VMEM((2, LANE, LANE), F32),
            pltpu.VMEM((4, 3 * 256, 256), BF16),
            pltpu.VMEM((4, 3 * 256, 256), BF16),
            pltpu.VMEM((2, 3 * LANE, LANE), BF16),
            pltpu.VMEM(wide, F32),
            pltpu.VMEM(wide, F32),
            pltpu.VMEM((2, LEVS, LON), F32),
            pltpu.VMEM((2, LEVS, LON), F32),
            pltpu.VMEM((5, ROWS * LEVS, LANE), F32),
            pltpu.VMEM(full, F32),
            pltpu.VMEM(full, F32),
            pltpu.VMEM(line, F32),
            pltpu.VMEM(line, F32),
            pltpu.VMEM(line, F32),
            pltpu.VMEM((3,) + line, F32),
            pltpu.VMEM(line_wide, F32),
            pltpu.VMEM(line, F32),
            pltpu.VMEM(line, F32),
            pltpu.VMEM(line, F32),
            pltpu.VMEM(line, F32),
            pltpu.VMEM((3,) + line, F32),
            pltpu.VMEM(line, F32),
            pltpu.VMEM((3, 2, 1, LON), F32),
            pltpu.VMEM((2, 3, 1, LON), F32),
            pltpu.VMEM((2, 3, 1, LON), F32),
            pltpu.VMEM(line, F32),
            pltpu.VMEM((4, 2 * ROWS * LEVS, 6 * LANE), BF16),
            pltpu.VMEM((2 * ROWS * LEVS, 3 * LANE), BF16),
            pltpu.VMEM((4, 2 * ROWS * LEVS, 2 * LANE), F32),
            pltpu.VMEM((2 * ROWS * LEVS, LANE), F32),
            pltpu.SemaphoreType.REGULAR((2,)), dma((12,)), dma((6, 2)), dma((6, 2)), dma((2, 2)), dma((2, 2)),
            dma((NCHUNK, 2)), dma((NCHUNK, 2)),
        ]
        + scan_sems
        + scan_sems[2:]
        + [dma((3, 2)), dma((3, 2)), dma((3, 2)), dma((2, 3)), dma((3, 2)), dma((2, 3))],
        compiler_params=pltpu.CompilerParams(
            collective_id=0, has_side_effects=True, vmem_limit_bytes=40 << 20
        ),
    )(*ins)
    outs = pl.pallas_call(
        second_kernel,
        out_shape=[jax.ShapeDtypeStruct(full, F32)] * 7,
        in_specs=[pl.BlockSpec(memory_space=pltpu.VMEM)] * 8,
        out_specs=[pl.BlockSpec(memory_space=pltpu.HBM)] * 7,
        scratch_shapes=[pltpu.VMEM(full, F32)] * 3 + [dma((13,))],
        compiler_params=pltpu.CompilerParams(vmem_limit_bytes=20 << 20),
    )(*mids)
    return tuple(outs)


def solution(mesh):
    field = P("lat", "lev", None)
    return jax.shard_map(
        shards,
        mesh=mesh,
        in_specs=(field,) * 6 + (P("lat", None),),
        out_specs=(field,) * 7,
        check_vma=False,
    )
```

```python
import functools
import math

import jax
import jax.numpy as jnp
import numpy as np
from jax import lax
from jax.experimental import pallas as pl
from jax.experimental.pallas import tpu as pltpu
from jax.sharding import PartitionSpec as P

MESH = pl.DeviceIdType.MESH
F32 = jnp.float32
BF16 = jnp.bfloat16

ROWS, LEVS, LON = 24, 8, 1152
NLAT = 32
CHIPS = 4
LANE = 128
COURANT = 0.1
GRAD = 0.1
GAS = 0.3
TOP = 1.0
CUT = 0.5

POLAR = sum(
    math.cos(((ROWS * band + ROWS - 0.5) / (NLAT * ROWS) - 0.5) * math.pi) ** 2 < CUT
    or math.cos(((ROWS * band + 0.5) / (NLAT * ROWS) - 0.5) * math.pi) ** 2 < CUT
    for band in range(NLAT // 2)
)
INTERIOR = ((1, 6), (13, 5))
EDGE = len(INTERIOR)
NCHUNK = EDGE + 1


@functools.cache
def tables():
    b = np.arange(LANE)
    fwd, back = [], []
    for r in range(1, 5):
        angle = 2.0 * np.pi * ((b[:, None] * (9 * b[None, :] + r)) % LON) / LON
        mr, mi = np.cos(angle), -np.sin(angle)
        w = np.block([[mr, mi], [-mi, mr]])
        fwd.append(w)
        back.append(w.T * (2.0 / LON))
    angle = 2.0 * np.pi * ((b[:, None] * b[None, :]) % LANE) / LANE
    w0 = np.concatenate([np.cos(angle[:, :65]), np.sin(angle[:, 1:64])], axis=1)
    weight = np.full((LANE,), 2.0)
    weight[0] = weight[64] = 1.0
    b0 = (w0 * weight[None, :]).T / LON
    wf = np.stack(fwd).astype(np.float32)
    wb = np.stack(back).astype(np.float32)
    wz = np.stack([w0, b0]).astype(np.float32)
    sines = np.zeros((8, LANE))
    freq0 = np.concatenate([np.arange(65), np.arange(1, 64)]) * 9
    sines[0] = np.sin(np.pi * freq0 / LON) ** 2 * CUT
    for r in range(1, 5):
        sines[r] = np.sin(np.pi * (9 * b + r) / LON) ** 2 * CUT
    lat = (np.arange(NLAT * ROWS, dtype=np.float32) + np.float32(0.5)) * np.float32(
        math.pi / (NLAT * ROWS)
    ) - np.float32(0.5 * math.pi)
    csq = np.cos(lat.astype(np.float64)).astype(np.float32) ** 2
    csq = np.broadcast_to(csq.reshape(NLAT, ROWS, 1), (NLAT, ROWS, LANE)).astype(np.float32)
    return wf, wb, wz, sines.astype(np.float32), np.ascontiguousarray(csq)


def east_west(x):
    return pltpu.roll(x, LON - 1, 1) - pltpu.roll(x, 1, 1)


def first_kernel(
    u_hbm, v_hbm, t_hbm, p_hbm, a_hbm, b_hbm, terr_hbm, csq_hbm, sin_hbm, wf_hbm, wb_hbm, wz_hbm,
    height, east, north, t_out, p_out, a_out, b_out, geo_off,
    fields, terr, csq, sines, wf32, wb32, wz32, wf, wb, wz,
    cum, logmid, halo_t, halo_p, damp, pair_t, pair_c,
    s_own, s_pair, s_chip, s_recv, pre, pre_pair,
    d_own, d_pair, d_chip, d_recv, geo_pair,
    edge_s, edge_d, edge_h, both_chips,
    y4, y1, z4, z1,
    ready, load_sem, halo_s, halo_r, out_s, out_r, both_s, both_r,
    bp_s, bp_r, bz_s, bz_r, bq_s, bq_r, be_s, be_r,
    cz_s, cz_r, cq_s, cq_r, ce_s, ce_r,
    ez_s, ez_r, dz_s, dz_r, hz_s, hz_r,
):
    la, le = lax.axis_index("lat"), lax.axis_index("lev")
    chip, core = le // 2, le % 2
    other = 1 - core
    up, down = (la + 1) % NLAT, (la + NLAT - 1) % NLAT
    pair_dev = (la, chip * 2 + other)
    side_lat = (la + NLAT - 1 + 2 * core) % NLAT
    cross_dev = (side_lat, chip * 2 + other)
    side_dev = (side_lat, le)
    has_up, has_down = la < NLAT - 1, la > 0
    has_side = jnp.where(core == 0, la, NLAT - 1 - la) > 0
    core_f = core.astype(F32)
    other_f = other.astype(F32)

    def remote(src, dst, send, recv, dev):
        return pltpu.make_async_remote_copy(
            src_ref=src, dst_ref=dst, send_sem=send, recv_sem=recv, device_id=dev, device_id_type=MESH
        )

    ins = (u_hbm, v_hbm, t_hbm, p_hbm, a_hbm, b_hbm)
    load = [
        pltpu.make_async_copy(ins[f], fields.at[f, pl.ds(1, ROWS)], load_sem.at[f]) for f in range(6)
    ]
    load += [
        pltpu.make_async_copy(terr_hbm, terr, load_sem.at[6]),
        pltpu.make_async_copy(csq_hbm.at[la], csq, load_sem.at[7]),
        pltpu.make_async_copy(sin_hbm, sines, load_sem.at[8]),
        pltpu.make_async_copy(wf_hbm, wf32, load_sem.at[9]),
        pltpu.make_async_copy(wb_hbm, wb32, load_sem.at[10]),
        pltpu.make_async_copy(wz_hbm, wz32, load_sem.at[11]),
    ]

    barrier = pltpu.get_barrier_semaphore()
    upper = chip < CHIPS // 2
    others = [(chip + d) % CHIPS for d in range(1, CHIPS)]
    starts, ends = la == NLAT // 2, la == NLAT // 2 - 1
    to_up = [(has_up, (up, le)), (has_up & (core == 1), cross_dev)]
    to_down = [(has_down, (down, le)), (has_down & (core == 0), cross_dev)]
    far_up = [(has_up & (c > chip), (up, c * 2)) for c in others]
    far_down = [(has_down & (c > chip), (down, c * 2 + 1)) for c in others]
    n_up = has_up.astype(jnp.int32) + jnp.where(has_up & (core == 1), 1 + 2 * chip, 0)
    n_down = has_down.astype(jnp.int32) + jnp.where(has_down & (core == 0), 1 + 2 * chip, 0)
    greet = [(la >= 0, pair_dev)] + to_down + far_down + to_up + far_up
    for c in others:
        inside = upper | (c >= CHIPS // 2)
        greet += [(inside, (la, c * 2 + core)), (inside, (la, c * 2 + other))]
    for there, dev in greet:

        @pl.when(there)
        def _():
            pl.semaphore_signal(barrier, inc=1, device_id=dev, device_id_type=MESH)

    for f in (3, 0, 1, 2):
        load[f].start()

    halo = {}
    for f in (2, 3, 0, 1, 4, 5):
        halo[f, 0] = remote(
            ins[f].at[ROWS - 1], fields.at[f, 0], halo_s.at[f, 0], halo_r.at[f, 0], (up, le)
        )
        halo[f, 1] = remote(
            ins[f].at[0], fields.at[f, ROWS + 1], halo_s.at[f, 1], halo_r.at[f, 1], (down, le)
        )


    def halo_start(f):
        pl.when(has_up & ~ends)(halo[f, 0].start)
        pl.when(has_down & ~starts)(halo[f, 1].start)

    def enter():
        pl.semaphore_wait(barrier, jnp.where(upper, 3, 7) + n_up + n_down)

        @pl.when(~upper)
        def _():
            for c in range(CHIPS):
                at = ready.at[jnp.where(c // 2 == CHIPS - 1 - chip, 0, 1)]
                pl.semaphore_signal(at, inc=1, device_id=(la, c), device_id_type=MESH)

        for f in (3, 2):
            pl.when(has_up)(halo[f, 0].start)
            pl.when(has_down)(halo[f, 1].start)

    pl.when(~starts)(enter)

    row = lax.broadcasted_iota(jnp.int32, (LEVS, LON), 0)

    def halves(x):
        hi = x.astype(BF16)
        return hi, (x - hi.astype(F32)).astype(BF16)

    def run_down(x):
        for s in (1, 2, 4):
            x = x + jnp.where(row >= s, pltpu.roll(x, s, 0), 0.0)
        return x

    def run_up(x):
        for s in (1, 2, 4):
            x = x + jnp.where(row < LEVS - s, pltpu.roll(x, LEVS - s, 0), 0.0)
        return x

    def advected(f, j):
        x = fields[f, j + 1]
        merid = fields[f, j + 2] - fields[f, j]
        return x - COURANT * (fields[0, j + 1] * east_west(x) + fields[1, j + 1] * merid)

    def halo_side(f, side):
        edge, there = (1, has_down) if side == 0 else (ROWS, has_up)
        beyond = (ROWS + 1) * side
        pl.when(there)(halo[f, side].wait_recv)

        @pl.when(~there)
        def _():
            fields[f, beyond] = fields[f, edge]

    def halo_ready(f):
        halo_side(f, 0)
        halo_side(f, 1)

    def column_t(j):
        t_out[j] = advected(2, j)

    def column_p(j):
        p = advected(3, j)
        p_out[j] = p
        c = run_down(p)
        cum[j + 1] = c
        s_own[j] = c[LEVS - 1 :, :]

    def span(k):
        if k == EDGE:
            return (ROWS - 1) * core, (ROWS - 1) * other, 1
        start, n = INTERIOR[k]
        return start + n * core, start + n * other, n

    def chunk_rows(k, body):
        if k == EDGE:
            body(0)
            body(ROWS - 1)
        else:
            start, n = INTERIOR[k]

            @pl.loop(start, start + 2 * n, unroll=n)
            def _(j):
                body(j)

    def scan(k, own, pair, total, recv, result, result_pair, sign, base, zs, zr, qs, qr, es, er, ps=None, pr=None):
        mine, theirs, n = span(k)
        mine_s, theirs_s = pl.ds(mine, n), pl.ds(theirs, n)
        if ps is not None:
            to_pair = remote(own.at[theirs_s], pair.at[theirs_s], ps.at[k], pr.at[k], pair_dev)
            from_pair = remote(own.at[mine_s], pair.at[mine_s], ps.at[k], pr.at[k], pair_dev)
        share = remote(
            result_pair.at[mine_s], result.at[pl.ds(mine + 1, n)], qs.at[k], qr.at[k], pair_dev
        )
        shared = remote(
            result_pair.at[theirs_s], result.at[pl.ds(theirs + 1, n)], qs.at[k], qr.at[k], pair_dev
        )
        hops = {}
        buddy = remote(
            total.at[mine_s], recv.at[0, mine_s], zs.at[k, 0], zr.at[k, 0],
            (la, (chip + 1 - 2 * (chip % 2)) * 2 + core),
        )
        relay = remote(
            both_chips.at[mine_s], recv.at[1, mine_s], zs.at[k, 1], zr.at[k, 1],
            (la, (CHIPS - 1 - chip) * 2 + core),
        )
        for d in (3, 2, 1):
            hops[d] = remote(
                total.at[mine_s], recv.at[d - 1, mine_s], zs.at[k, d - 1], zr.at[k, d - 1],
                (la, ((chip + CHIPS + sign * d) % CHIPS) * 2 + core),
            )
        if sign > 0:
            sends = {d: chip + d < CHIPS for d in hops}
            gets = {d: chip >= d for d in hops}
        else:
            sends = {d: chip >= d for d in hops}
            gets = {d: chip + d < CHIPS for d in hops}
        edges = []
        if k == EDGE:
            direct = {
                (d, w): remote(
                    own.at[(ROWS - 1) * w], edge_s.at[d - 1, core], ez_s.at[d - 1, w], ez_r.at[d - 1, core],
                    (la, ((chip + d) % CHIPS) * 2 + w),
                )
                for d in (1, 2, 3)
                for w in range(2)
            }
            slot = (ROWS + 1) * other
            edges = [
                remote(result.at[mine + 1], result.at[slot], es.at[0], er.at[other], side_dev),
                remote(result_pair.at[mine], result.at[slot], es.at[1], er.at[other], cross_dev),
            ]

        def begin():
            to_pair.start()

        def middle(row=None):
            if k == EDGE:
                for (d, w), c in direct.items():
                    if w == row:
                        pl.when(sends[d])(c.start)
                return
            if ps is not None:
                from_pair.wait_recv()
            total[mine_s] = own[mine_s] + pair[mine_s]
            if sign > 0:
                pl.when(chip < CHIPS - 1)(buddy.start)
            else:
                for d in hops:
                    pl.when(sends[d])(hops[d].start)

        def across():
            buddy.wait_recv()
            both_chips[mine_s] = total[mine_s] + recv[0, mine_s]
            relay.start()

        def end():
            acc = base(mine, n)
            result[pl.ds(mine + 1, n)] = acc
            if k == EDGE:
                from_pair.wait_recv()
            if sign > 0 and k != EDGE:

                @pl.when(chip == CHIPS - 1)
                def _():
                    buddy.wait_recv()

                @pl.when(chip % 2 == 1)
                def _():
                    result[pl.ds(mine + 1, n)] = result[pl.ds(mine + 1, n)] + recv[0, mine_s]

                @pl.when(~upper)
                def _():
                    relay.wait_recv()
                    result[pl.ds(mine + 1, n)] = result[pl.ds(mine + 1, n)] + recv[1, mine_s]

            for d in hops if sign < 0 or k == EDGE else ():

                @pl.when(gets[d])
                def _():
                    if k == EDGE:
                        for w in range(2):
                            remote(
                                edge_s.at[d - 1, w], edge_s.at[d - 1, w], ez_s.at[d - 1, w], ez_r.at[d - 1, w], pair_dev
                            ).wait_recv()
                        result[mine + 1] = result[mine + 1] + (edge_s[d - 1, 0] + edge_s[d - 1, 1])
                        return
                    hops[d].wait_recv()
                    result[pl.ds(mine + 1, n)] = result[pl.ds(mine + 1, n)] + recv[d - 1, mine_s]

            acc = result[pl.ds(mine + 1, n)]
            mine_f, pair_f = (core_f, other_f) if sign > 0 else (other_f, core_f)
            result_pair[mine_s] = acc + pair_f * own[mine_s]
            share.start()
            result[pl.ds(mine + 1, n)] = acc + mine_f * pair[mine_s]
            for e in edges:
                pl.when(has_side)(e.start)

        def finish():
            shared.wait_recv()

        def edge_ready():
            for side, there in ((0, has_down), (1, has_up)):
                slot = (ROWS + 1) * side
                c = remote(result.at[slot], result.at[slot], es.at[0], er.at[side], side_dev)
                pl.when(there)(c.wait_recv)

        def drain():
            if ps is not None:
                to_pair.wait_send()
            if k == EDGE:
                for (d, _), c in direct.items():
                    pl.when(sends[d])(c.wait_send)
            elif sign > 0:
                pl.when(chip < CHIPS - 1)(buddy.wait_send)
                pl.when(upper)(relay.wait_send)
            else:
                for d in hops:
                    pl.when(sends[d])(hops[d].wait_send)
            for e in edges:
                pl.when(has_side)(e.wait_send)

        def drain_share():
            share.wait_send()

        return begin, middle, end, finish, edge_ready, drain, across, drain_share

    def base_top(mine, n):
        return jnp.full((n, 1, LON), TOP, F32)

    def base_terrain(mine, n):
        return jnp.stack([terr[pl.ds(mine + i, 1), :] for i in range(n)], 0)

    top = [
        scan(
            k, s_own, s_pair, s_chip, s_recv, pre, pre_pair, 1, base_top,
            bz_s, bz_r, bq_s, bq_r, be_s, be_r, bp_s, bp_r,
        )
        for k in range(NCHUNK)
    ]
    bottom = [
        scan(
            k, d_own, d_pair, d_chip, d_recv, geo_off, geo_pair, -1, base_terrain,
            cz_s, cz_r, cq_s, cq_r, ce_s, ce_r,
        )
        for k in range(EDGE)
    ]

    edge_row = (ROWS - 1) * core
    edge_sends = []
    for d in (3, 2, 1):
        above = chip + CHIPS - d
        for tc in range(2):
            edge_sends.append((
                has_side & (chip >= d),
                remote(
                    d_chip.at[edge_row], edge_h.at[other, d - 1], hz_s.at[d - 1, tc], hz_r.at[other, d - 1],
                    (side_lat, (above % CHIPS) * 2 + tc),
                ),
            ))
            edge_sends.append((
                chip >= d,
                remote(
                    d_chip.at[edge_row], edge_d.at[core, d - 1], dz_s.at[d - 1, tc], dz_r.at[core, d - 1],
                    (la, (above % CHIPS) * 2 + tc),
                ),
            ))
    edge_slot = (ROWS + 1) * other
    edge_sends += [
        (has_side, remote(geo_pair.at[edge_row], geo_off.at[edge_slot], ce_s.at[0], ce_r.at[other], side_dev)),
        (has_side, remote(geo_pair.at[(ROWS - 1) * other], geo_off.at[edge_slot], ce_s.at[1], ce_r.at[other], cross_dev)),
    ]
    last = ROWS - 1
    to_upper = remote(d_own.at[last], d_pair.at[last], cq_s.at[EDGE], cq_r.at[EDGE], pair_dev)

    def edge_depths():
        own, pair = d_own[edge_row], d_pair[edge_row]
        d_chip[edge_row] = own + pair
        ground = terr[pl.ds(edge_row, 1), :]
        geo_pair[0] = ground + jnp.where(core == 0, pair, own)
        geo_pair[ROWS - 1] = ground
        for there, c in edge_sends:
            pl.when(there)(c.start)
        pl.when(core == 1)(to_upper.start)

    def edge_offsets():
        for w in range(2):
            r = last * w
            geo_off[r + 1] = terr[pl.ds(r, 1), :]

        @pl.when(core == 0)
        def _():
            to_upper.wait_recv()
            for w in range(2):
                geo_off[last * w + 1] = geo_off[last * w + 1] + d_pair[last * w]

        for side, there in ((0, has_down), (1, has_up)):
            slot = (ROWS + 1) * side

            @pl.when(there)
            def _():
                remote(geo_off.at[slot], geo_off.at[slot], ce_s.at[0], ce_r.at[side], side_dev).wait_recv()

        for d in (1, 2, 3):
            for w in range(2):

                @pl.when(chip + d < CHIPS)
                def _():
                    slot = edge_d.at[w, d - 1]
                    remote(slot, slot, dz_s.at[0, 0], dz_r.at[w, d - 1], pair_dev).wait_recv()
                    geo_off[last * w + 1] = geo_off[last * w + 1] + edge_d[w, d - 1]

            for side, there in ((0, has_down), (1, has_up)):

                @pl.when(there & (chip + d < CHIPS))
                def _():
                    slot = edge_h.at[side, d - 1]
                    remote(slot, slot, dz_s.at[0, 0], hz_r.at[side, d - 1], pair_dev).wait_recv()
                    i = (ROWS + 1) * side
                    geo_off[i] = geo_off[i] + edge_h[side, d - 1]

    def edge_drain():
        for there, c in edge_sends:
            pl.when(there)(c.wait_send)
        pl.when(core == 1)(to_upper.wait_send)

    def thickness(i, temp):
        base = pre[i]
        lp = jnp.log(base + cum[i])
        above = jnp.where(row == 0, jnp.log(base), pltpu.roll(lp, 1, 0))
        depth = GAS * temp * (lp - above)
        below = run_up(depth)
        height[i] = below - 0.5 * depth
        logmid[i] = 0.5 * (lp + above)
        return below[:1, :]

    def thickness_row(j):
        d_own[j] = thickness(j + 1, t_out[j])

    def gradient_row(j):
        pull = GAS * t_out[j]
        east[j] = east[j] - GRAD * (east_west(height[j + 1]) + pull * east_west(logmid[j + 1]))
        north[j] = north[j] - GRAD * (
            (height[j + 2] - height[j]) + pull * (logmid[j + 2] - logmid[j])
        )

    def both(k):
        _, theirs, n = span(k)
        at = pl.ds(theirs, n)
        return (
            remote(cum.at[pl.ds(theirs + 1, n)], pair_c.at[at], both_s.at[k, 0], both_r.at[k, 0], pair_dev),
            remote(t_out.at[at], pair_t.at[at], both_s.at[k, 1], both_r.at[k, 1], pair_dev),
        )

    def pair_row(j):
        base = pre_pair[j]
        lp = jnp.log(base + pair_c[j])
        above = jnp.where(row == 0, jnp.log(base), pltpu.roll(lp, 1, 0))
        depth = GAS * pair_t[j] * (lp - above)
        d_pair[j] = jnp.sum(depth, axis=0, keepdims=True)

    def mine_rows(k):
        mine, _, n = span(k)

        @pl.loop(0, n, unroll=n)
        def _(i):
            thickness_row(mine + i)
            pair_row(mine + i)

    def their_rows(k):
        _, theirs, n = span(k)

        @pl.loop(0, n, unroll=n)
        def _(i):
            thickness_row(theirs + i)

    def tracers(j):
        a_out[j] = advected(4, j)
        b_out[j] = advected(5, j)

    def inner_tracers():
        @pl.loop(1, ROWS - 1, unroll=11)
        def _(j):
            tracers(j)

    for f in (3, 0, 1):
        load[f].wait()
    for f in (4, 5, 6, 7, 8, 9, 10, 11):
        load[f].start()
    for k in range(EDGE):
        chunk_rows(k, column_p)
        pl.when(~starts)(top[k][0])

    @pl.when(starts)
    def _():
        enter()
        for k in range(EDGE):
            top[k][0]()

    load[2].wait()
    pairs = [both(k) for k in range(NCHUNK)]
    for k in range(EDGE):
        chunk_rows(k, column_t)
        for c in pairs[k]:
            c.start()
    for k in range(EDGE):
        top[k][1]()
    halo_start(0)
    halo_start(1)

    @pl.when(upper)
    def _():
        pl.semaphore_wait(ready.at[0], 2)
        for k in range(EDGE):
            top[k][6]()

    out_copies = []
    for n, (src, dst) in enumerate(((t_out, halo_t), (p_out, halo_p))):
        out_copies.append(
            remote(src.at[ROWS - 1], dst.at[0], out_s.at[n, 0], out_r.at[n, 0], (up, le))
        )
        out_copies.append(remote(src.at[0], dst.at[1], out_s.at[n, 1], out_r.at[n, 1], (down, le)))
    ways = (has_up, has_down)

    def edge_rows(w):
        r = (ROWS - 1) * w
        halo_side(3, w)
        column_p(r)
        pl.when(core != w)(top[EDGE][0])
        top[EDGE][1](w)
        halo_side(2, w)
        column_t(r)
        for c in pairs[EDGE]:
            pl.when(core != w)(c.start)
        for n, c in enumerate(out_copies):
            if n % 2 != w:
                pl.when(ways[n % 2])(c.start)

    def edge_sums():
        top[EDGE][2]()
        for c in pairs[EDGE]:
            c.wait_recv()
        mine_rows(EDGE)
        edge_depths()

    @pl.when(upper)
    def _():
        pl.semaphore_wait(ready.at[1], 2)

    pl.when(~starts)(functools.partial(edge_rows, 0))
    pl.when(~(ends & ~upper))(functools.partial(edge_rows, 1))
    pl.when(starts & upper)(functools.partial(edge_rows, 0))
    for f in (4, 5):
        halo_start(f)
    for f in (0, 1, 4, 5):
        now = upper | (f < 2)
        pl.when(ends & now)(halo[f, 0].start)
        pl.when(starts & now)(halo[f, 1].start)

    for n in (4, 5, 6, 7, 8, 9, 10, 11):
        load[n].wait()

    def prepare():
        @pl.loop(0, ROWS, unroll=4)
        def _(j):
            c = csq[pl.ds(j, 1), :]
            at = pl.ds(pl.multiple_of(j * LEVS, LEVS), LEVS)
            for r in range(5):
                d = c / jnp.maximum(c, sines[r : r + 1, :])
                damp[r, at, :] = jnp.broadcast_to(d, (LEVS, LANE))

        for full, parts in ((wf32, wf), (wb32, wb)):

            @pl.loop(0, 4)
            def _(r):
                for i in range(0, 256, 64):
                    hi, lo = halves(full[r, i : i + 64, :])
                    parts[r, i : i + 64, :] = hi
                    parts[r, 256 + i : 320 + i, :] = hi
                    parts[r, 512 + i : 576 + i, :] = lo

        for n in range(2):
            hi, lo = halves(wz32[n])
            wz[n, :LANE, :], wz[n, LANE : 2 * LANE, :], wz[n, 2 * LANE :, :] = hi, hi, lo

    cos9 = [math.cos(2.0 * math.pi * i / 9) for i in range(9)]
    sin9 = [math.sin(2.0 * math.pi * i / 9) for i in range(9)]

    def forward_nine(i):
        for f in range(2):
            at = pl.ds(pl.multiple_of(f * ROWS * LEVS + i * 16, 16), 16)
            x = jnp.concatenate([advected(f, 2 * i), advected(f, 2 * i + 1)], axis=0)
            xs = [x[:, LANE * a : LANE * (a + 1)] for a in range(9)]
            even = [xs[a] + xs[9 - a] for a in range(1, 5)]
            odd = [xs[a] - xs[9 - a] for a in range(1, 5)]
            hi, lo = halves(xs[0] + ((even[0] + even[1]) + (even[2] + even[3])))
            y1[at, :LANE], y1[at, LANE : 2 * LANE], y1[at, 2 * LANE :] = hi, lo, hi
            for r in range(1, 5):
                re, im = xs[0], None
                for a in range(1, 5):
                    re = re + cos9[(a * r) % 9] * even[a - 1]
                    term = -sin9[(a * r) % 9] * odd[a - 1]
                    im = term if im is None else im + term
                for part, y in ((0, re), (1, im)):
                    hi, lo = halves(y)
                    for place, value in ((0, hi), (2, lo), (4, hi)):
                        place = (place + part) * LANE
                        y4[r - 1, at, place : place + LANE] = value

    def triple(x):
        hi, lo = halves(x)
        return jnp.concatenate([hi, lo, hi], axis=1)

    def mm(x, w):
        return jnp.dot(x, w, preferred_element_type=F32)

    def spectrum(r):
        d = damp[r + 1]
        d = jnp.concatenate([d, d], axis=1)
        d = jnp.concatenate([d, d], axis=0)
        z4[r] = mm(triple(mm(y4[r], wf[r]) * d), wb[r])

    def spectrum_zero():
        d = jnp.concatenate([damp[0], damp[0]], axis=0)
        z1[...] = mm(triple(mm(y1[...], wz[0]) * d), wz[1])

    def backward_nine(i):
        for f, dst in ((0, east), (1, north)):
            at = pl.ds(pl.multiple_of(f * ROWS * LEVS + i * 16, 16), 16)
            z0 = z1[at, :]
            re = [z4[r, at, :LANE] for r in range(4)]
            im = [z4[r, at, LANE:] for r in range(4)]
            outs = [None] * 9
            outs[0] = z0 + ((re[0] + re[1]) + (re[2] + re[3]))
            for a in range(1, 5):
                even, odd = z0, None
                for r in range(1, 5):
                    even = even + cos9[(a * r) % 9] * re[r - 1]
                    term = sin9[(a * r) % 9] * im[r - 1]
                    odd = term if odd is None else odd + term
                outs[a], outs[9 - a] = even - odd, even + odd
            for a in range(9):
                dst[2 * i, :, LANE * a : LANE * (a + 1)] = outs[a][:LEVS]
                dst[2 * i + 1, :, LANE * a : LANE * (a + 1)] = outs[a][LEVS:]

    polar = (la < POLAR) | (la >= NLAT - POLAR)

    def forward():
        halo_ready(0)
        halo_ready(1)

        @pl.loop(0, ROWS // 2, unroll=2)
        def _(i):
            forward_nine(i)

    def early_fill():
        inner_tracers()

        @pl.when(polar)
        def _():
            prepare()
            forward()

    pl.when(upper)(early_fill)

    for k in range(EDGE):
        top[k][2]()
        for c in pairs[k]:
            c.wait_recv()
        mine_rows(k)
        bottom[k][1]()
    pl.when(starts & ~upper)(functools.partial(edge_rows, 0))
    pl.when(ends & ~upper)(functools.partial(edge_rows, 1))
    edge_sums()
    for f in (4, 5):
        pl.when(ends & ~upper)(halo[f, 0].start)
        pl.when(starts & ~upper)(halo[f, 1].start)
    for k in range(NCHUNK):
        top[k][3]()
        their_rows(k)
    pl.when(~upper)(early_fill)

    @pl.when(polar)
    def _():
        spectrum_zero()
        pl.loop(0, 4)(spectrum)

        @pl.loop(0, ROWS // 2, unroll=2)
        def _(i):
            backward_nine(i)

    @pl.when(~polar)
    def _():
        @pl.loop(1, ROWS - 1, unroll=11)
        def _(j):
            east[j] = advected(0, j)
            north[j] = advected(1, j)

        halo_ready(0)
        halo_ready(1)
        for j in (0, ROWS - 1):
            east[j] = advected(0, j)
            north[j] = advected(1, j)

    @pl.loop(1, ROWS - 1, unroll=11)
    def _(j):
        gradient_row(j)

    halo_ready(4)
    halo_ready(5)
    tracers(0)
    tracers(ROWS - 1)

    for n, c in enumerate(out_copies):
        pl.when(ways[1 - n % 2])(c.wait_recv)
    top[EDGE][4]()
    for side, there in ((0, has_down), (1, has_up)):

        @pl.when(there)
        def _():
            i = (ROWS + 1) * side
            cum[i] = run_down(halo_p[side])
            thickness(i, halo_t[side])

    @pl.when(la == 0)
    def _():
        height[0] = height[1]
        logmid[0] = logmid[1]

    @pl.when(la == NLAT - 1)
    def _():
        height[ROWS + 1] = height[ROWS]
        logmid[ROWS + 1] = logmid[ROWS]

    gradient_row(0)
    gradient_row(ROWS - 1)

    for k in range(NCHUNK):
        top[k][5]()
        top[k][7]()
    for k in range(EDGE):
        bottom[k][5]()
    edge_drain()
    for pair in pairs:
        for c in pair:
            c.wait_send()
    for (f, side), c in halo.items():
        pl.when(ways[side])(c.wait_send)
    for n, c in enumerate(out_copies):
        pl.when(ways[n % 2])(c.wait_send)
    for k in range(EDGE):
        bottom[k][2]()
    edge_offsets()
    for k in range(EDGE):
        bottom[k][3]()

    @pl.when(la == 0)
    def _():
        geo_off[0] = geo_off[1]

    @pl.when(la == NLAT - 1)
    def _():
        geo_off[ROWS + 1] = geo_off[ROWS]
    for k in range(EDGE):
        bottom[k][7]()


def second_kernel(
    height, east, north, t_out, p_out, a_out, b_out, geo_off,
    east_hbm, north_hbm, t_hbm, p_hbm, a_hbm, b_hbm, geo_hbm,
    east_buf, north_buf, geo_buf, sem,
):
    copies = [
        pltpu.make_async_copy(src, dst, sem.at[n])
        for n, (src, dst) in enumerate(((t_out, t_hbm), (p_out, p_hbm), (a_out, a_hbm), (b_out, b_hbm)))
    ]
    for c in copies:
        c.start()
    part = 8
    for q in range(ROWS // part):

        @pl.loop(part * q, part * (q + 1), unroll=4)
        def _(j):
            off = geo_off[j + 1]
            geo_buf[j] = height[j + 1] + off
            east_buf[j] = east[j] - GRAD * east_west(off)
            north_buf[j] = north[j] - GRAD * (geo_off[j + 2] - geo_off[j])

        for m, (src, dst) in enumerate(((east_buf, east_hbm), (north_buf, north_hbm), (geo_buf, geo_hbm))):
            rows = pl.ds(part * q, part)
            c = pltpu.make_async_copy(src.at[rows], dst.at[rows], sem.at[4 + 3 * q + m])
            c.start()
            copies.append(c)
    for c in copies:
        c.wait()


def shards(u, v, t, p, a, b, terrain):
    wf, wb, wz, sines, csq = (jnp.asarray(x) for x in tables())
    ins = [u, v, t, p, a, b, terrain, csq, sines, wf, wb, wz]
    ins = [pltpu.with_memory_space_constraint(x, pltpu.HBM) for x in ins]
    full = (ROWS, LEVS, LON)
    wide = (ROWS + 2, LEVS, LON)
    line = (ROWS, 1, LON)
    line_wide = (ROWS + 2, 1, LON)
    dma = pltpu.SemaphoreType.DMA
    scan_sems = [
        dma((NCHUNK,)), dma((NCHUNK,)), dma((NCHUNK, 3)), dma((NCHUNK, 3)),
        dma((NCHUNK,)), dma((NCHUNK,)), dma((2,)), dma((2,)),
    ]
    mids = pl.pallas_call(
        first_kernel,
        out_shape=[pltpu.VMEM(wide, F32)] + [pltpu.VMEM(full, F32)] * 6 + [pltpu.VMEM(line_wide, F32)],
        in_specs=[pl.BlockSpec(memory_space=pltpu.HBM)] * len(ins),
        out_specs=[pl.BlockSpec(memory_space=pltpu.VMEM)] * 8,
        scratch_shapes=[
            pltpu.VMEM((6,) + wide, F32),
            pltpu.VMEM((ROWS, LON), F32),
            pltpu.VMEM((ROWS, LANE), F32),
            pltpu.VMEM((8, LANE), F32),
            pltpu.VMEM((4, 256, 256), F32),
            pltpu.VMEM((4, 256, 256), F32),
            pltpu.VMEM((2, LANE, LANE), F32),
            pltpu.VMEM((4, 3 * 256, 256), BF16),
            pltpu.VMEM((4, 3 * 256, 256), BF16),
            pltpu.VMEM((2, 3 * LANE, LANE), BF16),
            pltpu.VMEM(wide, F32),
            pltpu.VMEM(wide, F32),
            pltpu.VMEM((2, LEVS, LON), F32),
            pltpu.VMEM((2, LEVS, LON), F32),
            pltpu.VMEM((5, ROWS * LEVS, LANE), F32),
            pltpu.VMEM(full, F32),
            pltpu.VMEM(full, F32),
            pltpu.VMEM(line, F32),
            pltpu.VMEM(line, F32),
            pltpu.VMEM(line, F32),
            pltpu.VMEM((3,) + line, F32),
            pltpu.VMEM(line_wide, F32),
            pltpu.VMEM(line, F32),
            pltpu.VMEM(line, F32),
            pltpu.VMEM(line, F32),
            pltpu.VMEM(line, F32),
            pltpu.VMEM((3,) + line, F32),
            pltpu.VMEM(line, F32),
            pltpu.VMEM((3, 2, 1, LON), F32),
            pltpu.VMEM((2, 3, 1, LON), F32),
            pltpu.VMEM((2, 3, 1, LON), F32),
            pltpu.VMEM(line, F32),
            pltpu.VMEM((4, 2 * ROWS * LEVS, 6 * LANE), BF16),
            pltpu.VMEM((2 * ROWS * LEVS, 3 * LANE), BF16),
            pltpu.VMEM((4, 2 * ROWS * LEVS, 2 * LANE), F32),
            pltpu.VMEM((2 * ROWS * LEVS, LANE), F32),
            pltpu.SemaphoreType.REGULAR((2,)), dma((12,)), dma((6, 2)), dma((6, 2)), dma((2, 2)), dma((2, 2)),
            dma((NCHUNK, 2)), dma((NCHUNK, 2)),
        ]
        + scan_sems
        + scan_sems[2:]
        + [dma((3, 2)), dma((3, 2)), dma((3, 2)), dma((2, 3)), dma((3, 2)), dma((2, 3))],
        compiler_params=pltpu.CompilerParams(
            collective_id=0, has_side_effects=True, vmem_limit_bytes=40 << 20
        ),
    )(*ins)
    outs = pl.pallas_call(
        second_kernel,
        out_shape=[jax.ShapeDtypeStruct(full, F32)] * 7,
        in_specs=[pl.BlockSpec(memory_space=pltpu.VMEM)] * 8,
        out_specs=[pl.BlockSpec(memory_space=pltpu.HBM)] * 7,
        scratch_shapes=[pltpu.VMEM(full, F32)] * 3 + [dma((13,))],
        compiler_params=pltpu.CompilerParams(vmem_limit_bytes=20 << 20),
    )(*mids)
    return tuple(outs)


def solution(mesh):
    field = P("lat", "lev", None)
    return jax.shard_map(
        shards,
        mesh=mesh,
        in_specs=(field,) * 6 + (P("lat", None),),
        out_specs=(field,) * 7,
        check_vma=False,
    )
```
